512 devices in a mesh: dom: 64 (over x, z, core), rep: 8 (over y).
Axes of the slice: x: 4, y: 8, z: 8, core: 2. Of those that a mesh axis runs over, the one named last changes fastest.
Arguments:
- node_feats: bfloat16 [196608, 256], P(('dom', 'rep')), may hold values from -6 to 6
- node_ids: int32 [196608], replicated, may hold values from 0 to 4194303
- tile_row: int32 [64, 8, 64], replicated, may hold values from -1 to 1535, as said below
- tile_col: int32 [64, 8, 64], replicated, may hold values from -1 to 1535, as said below
- tile_count: int32 [64, 8, 64], replicated, may hold values from 1 to 128, as said below
- self_weight: bfloat16 [256, 512], replicated, may hold values from -0.375 to 0.375
- neigh_weight: bfloat16 [256, 512], replicated, may hold values from -3 to 3
- out_grad: bfloat16 [196608, 512], P(('dom', 'rep')), may hold values from -6 to 6
Outputs:
- hidden_out: bfloat16 [196608, 512], P(('dom', 'rep'))
- feat_grad: bfloat16 [196608, 256], P(('dom', 'rep'))
- self_grad: float32 [256, 512], replicated
- neigh_grad: float32 [256, 512], replicated
The draws below stay inside these ranges and needn't reach their ends.
Inputs may be any that keep to these rules, and one draw needn't show every extreme that they name: `tile_row`: entry [d, r, s] is -1 where the slot holds no tile, else a block row of dom group d: d * 24 plus 0 to 23. In every draw some pair (d, r) has all 64 of its slots filled. `tile_col`: -1 exactly where tile_row is -1; else one of the blocks of device (s, r): s * 24 + r * 3 plus 0 to 2. `tile_count`: read only where a tile is present.
All inputs are finite; a program needn't handle non-finite values.
Results may differ from the reference program's by a relative error of at most 0.01.
Values may be sent and summed in bfloat16 or wider, within the bound.
No kernel may reach another device: no remote copies, remote signals or barrier semaphores. Data moves between devices by JAX's collectives and lax.ppermute only.
A program may use at most 64 MiB of HBM per device.

```python
import math
import jax
import jax.numpy as jnp
from jax import lax

TILE = 128
F_IN = 256
F_OUT = 512
BPD = 3
NODES = 196608
N_DOM = 64
N_REP = 8


def tile_pattern(key):
    folded = jax.random.fold_in(key, 4242)
    subkeys = jax.random.split(folded, 9)
    slot_shape = (N_DOM, N_REP, N_DOM)
    group_blocks = BPD * N_REP
    fill_rates = jax.random.randint(subkeys[0], (N_DOM, 1, 1), 2, 9)
    filled = jax.random.randint(subkeys[1], slot_shape, 0, 8) < fill_rates
    full_dom = jax.random.randint(subkeys[2], (), 0, N_DOM)
    full_rep = jax.random.randint(subkeys[3], (), 0, N_REP)
    forced = (jnp.arange(N_DOM)[:, None, None] == full_dom) & (jnp.arange(N_REP)[None, :, None] == full_rep)
    filled = filled | forced
    first_draw = jax.random.randint(subkeys[4], slot_shape, 0, group_blocks)
    second = jax.random.randint(subkeys[5], slot_shape, 0, group_blocks)
    row_order = jax.random.permutation(subkeys[6], group_blocks)
    local_row = row_order[jnp.minimum(first_draw, second)]
    row_block = jnp.arange(N_DOM)[:, None, None] * group_blocks + local_row
    col_block = jnp.arange(N_DOM)[None, None, :] * group_blocks + jnp.arange(N_REP)[None, :, None] * BPD + jax.random.randint(subkeys[7], slot_shape, 0, BPD)
    count_draws = jax.random.randint(subkeys[8], (2,) + slot_shape, 1, TILE + 1)
    counts = (count_draws[0] * count_draws[1] + TILE - 1) // TILE
    return (jnp.where(filled, row_block, -1).astype(jnp.int32), jnp.where(filled, col_block, -1).astype(jnp.int32), counts.astype(jnp.int32))


def draw_tile_row(key, part):
    return tile_pattern(key)[0]


def draw_tile_col(key, part):
    return tile_pattern(key)[1]


def draw_tile_count(key, part):
    return tile_pattern(key)[2]


def set_ends(result, key, low, top_value):
    extent = result.shape
    place = [jax.random.randint(jax.random.fold_in(key, axis), (), 0, extent[axis]) for axis in range(len(extent))]
    result = result.at[tuple(place)].set(low)
    longest = extent.index(max(extent))
    place[longest] = (place[longest] + 1) % extent[longest]
    return result.at[tuple(place)].set(top_value)


def levels(rng, extent, shards, least, top_value):
    factor_of, own = 1.0, jax.random.fold_in(rng, 6)
    for axis_at, blocks in shards:
        draws = jnp.exp(jax.random.uniform(jax.random.fold_in(own, axis_at), (blocks,), jnp.float32, least / len(shards), top_value / len(shards)))
        factor_of = factor_of * jnp.repeat(draws, extent[axis_at] // blocks).reshape([-1 if axis == axis_at else 1 for axis in range(len(extent))])
    return factor_of


def centred(own_key, extent, deviation, limit, cuts=(), kind=jnp.bfloat16):
    result = jax.random.normal(own_key, extent, jnp.float32) * deviation
    if len(cuts) > 0:
        result = levels(own_key, extent, cuts, -0.22, 0.18) * result
    return jnp.clip(result, min=-limit, max=limit).astype(kind)


def setup_inputs(seed: int = 0) -> dict:
    keys = jax.random.split(jax.random.key(seed), 9)
    return {
        "node_feats": centred(keys[0], (NODES, F_IN), 1.0, 6.0, ((0, 512),)),
        "node_ids": set_ends(jax.random.randint(keys[1], (NODES,), 0, 16777216 // ((NODES + 65520) // 65521)), jax.random.fold_in(keys[1], 1), 0, (16777216 // ((NODES + 65520) // 65521)) - 1).astype(jnp.int32),
        "tile_row": draw_tile_row(jax.random.fold_in(keys[8], 71), 0),
        "tile_col": draw_tile_col(jax.random.fold_in(keys[8], 71), 0),
        "tile_count": draw_tile_count(jax.random.fold_in(keys[8], 71), 0),
        "self_weight": centred(keys[5], (F_IN, F_OUT), F_IN ** -0.5, 0.375),
        "neigh_weight": centred(keys[6], (F_IN, F_OUT), (max(F_IN // 64, 1)) ** -0.5, 3.0),
        "out_grad": centred(keys[7], (NODES, F_OUT), 1.0, 6.0, ((0, 512),)),
    }


def edge_masks(row_ids, col_ids, limits):
    left_ids = (row_ids % 4093)[:, :, None]
    right_ids = (col_ids % 4091)[:, None, :]
    hashed = (left_ids * right_ids + left_ids + 3 * right_ids) % 4099 % TILE
    return (hashed < limits[:, None, None]).astype(jnp.float32)

def slot_masks(id_blocks, rows_in, cols_in, limits_in):
    present = rows_in >= 0
    row_block = jnp.where(present, rows_in, 0)
    col_block = jnp.where(present, cols_in, 0)
    limits = jnp.where(present, limits_in, 0)
    tile_masks = edge_masks(id_blocks[row_block], id_blocks[col_block], limits)
    return (tile_masks, row_block, col_block, present)

def reference(node_feats, node_ids, tile_row, tile_col, tile_count, self_weight, neigh_weight, out_grad):
    node_count, width_in = node_feats.shape
    block_count = node_count // TILE
    group_blocks = block_count // N_DOM
    id_blocks = node_ids.reshape(block_count, TILE)
    feat_blocks = node_feats.astype(jnp.float32).reshape(block_count, TILE, width_in)

    def forward_group(group_index):
        tile_masks, row_block, col_block, present = slot_masks(id_blocks, tile_row[group_index].reshape(-1), tile_col[group_index].reshape(-1), tile_count[group_index].reshape(-1))
        products = jnp.einsum('sij,sjf->sif', tile_masks, feat_blocks[col_block])
        offset = row_block - group_index * group_blocks
        select = ((offset[:, None] == jnp.arange(group_blocks)[None, :]) & present[:, None]).astype(jnp.float32)
        partial_value = jnp.einsum('rsb,rsif->rbif', select.reshape(N_REP, N_DOM, group_blocks), products.reshape(N_REP, N_DOM, TILE, width_in))
        rounded = lax.optimization_barrier(partial_value.astype(jnp.bfloat16))
        return lax.optimization_barrier(jnp.sum(rounded.astype(jnp.float32), axis=0))
    summed = lax.map(forward_group, jnp.arange(N_DOM)).reshape(node_count, width_in)
    flat_rows = tile_row.reshape(-1)
    flat_limits = tile_count.reshape(-1)
    present_all = flat_rows >= 0
    degree = jnp.zeros((block_count,), jnp.float32).at[jnp.where(present_all, flat_rows, 0)].add(jnp.where(present_all, flat_limits, 0).astype(jnp.float32))
    divisor = jnp.repeat(jnp.maximum(degree, 1.0), TILE)[:, None]
    mean_feats = (summed / divisor).astype(jnp.bfloat16)
    preact = jnp.dot(node_feats, self_weight, preferred_element_type=jnp.float32) + jnp.dot(mean_feats, neigh_weight, preferred_element_type=jnp.float32)
    hidden_out = jax.nn.silu(preact).astype(jnp.bfloat16)
    logistic = jax.nn.sigmoid(preact)
    pre_grad = (out_grad.astype(jnp.float32) * logistic * (1.0 + preact * (1.0 - logistic))).astype(jnp.bfloat16)
    grad_scale = 1.0 / math.sqrt(node_count)
    self_grad = jnp.dot(node_feats.T, pre_grad, preferred_element_type=jnp.float32) * grad_scale
    neigh_grad = jnp.dot(mean_feats.T, pre_grad, preferred_element_type=jnp.float32) * grad_scale
    mean_grad = jnp.dot(pre_grad, neigh_weight.T, preferred_element_type=jnp.float32)
    spread = (mean_grad / divisor).astype(jnp.bfloat16)
    spread_blocks = spread.astype(jnp.float32).reshape(block_count, TILE, width_in)

    def backward_group(running, group_index):
        tile_masks, row_block, col_block, present = slot_masks(id_blocks, tile_row[group_index].reshape(-1), tile_col[group_index].reshape(-1), tile_count[group_index].reshape(-1))
        products = jnp.einsum('sij,sif->sjf', tile_masks, spread_blocks[row_block])
        return (running.at[col_block].add(products), None)
    transposed, _ = lax.scan(backward_group, jnp.zeros((block_count, TILE, width_in), jnp.float32), jnp.arange(N_DOM))
    feat_grad = (jnp.dot(pre_grad, self_weight.T, preferred_element_type=jnp.float32) + transposed.reshape(node_count, width_in)).astype(jnp.bfloat16)
    return (hidden_out, feat_grad, self_grad, neigh_grad)
```

```python
import math

import jax
import jax.numpy as jnp
from jax import lax
from jax.experimental import pallas as pl
from jax.experimental.pallas import tpu as pltpu
from jax.sharding import Mesh
from jax.sharding import PartitionSpec as P

TILE = 128
DOM = ("x", "z", "core")
ALL = ("x", "z", "core", "rep")
STEP = 8


def edge_masks(row_ids, col_ids, limits, swapped):
    u = row_ids % 4093
    v = col_ids % 4091
    if swapped:
        u, v = u[:, None, :], v[:, :, None]
    else:
        u, v = u[:, :, None], v[:, None, :]
    hashed = (u * v + u + 3 * v) % 4099 % TILE
    return (hashed < limits[:, None, None]).astype(jnp.bfloat16)


def pair_swap(x, axis, bit):
    n = lax.axis_size(axis)
    return lax.ppermute(x, axis, [(i, i ^ bit) for i in range(n)])


def forward_kernel(offset_ref, mask_ref, feat_ref, out_ref, total_ref):
    step = pl.program_id(0)

    @pl.when(step == 0)
    def _():
        total_ref[...] = jnp.zeros_like(total_ref)

    for t in range(STEP):
        at = offset_ref[step * STEP + t]
        total_ref[at] += jnp.dot(mask_ref[t], feat_ref[t], preferred_element_type=jnp.float32)

    @pl.when(step == pl.num_programs(0) - 1)
    def _():
        out_ref[...] = total_ref[...].astype(out_ref.dtype)


def tile_sums(offsets, masks, feats, blocks):
    slots, tile, width = feats.shape
    return pl.pallas_call(
        forward_kernel,
        grid_spec=pltpu.PrefetchScalarGridSpec(
            num_scalar_prefetch=1,
            grid=(slots // STEP,),
            in_specs=[
                pl.BlockSpec((STEP, tile, tile), lambda i, o: (i, 0, 0)),
                pl.BlockSpec((STEP, tile, width), lambda i, o: (i, 0, 0)),
            ],
            out_specs=pl.BlockSpec((blocks, tile, width), lambda i, o: (0, 0, 0)),
            scratch_shapes=[pltpu.VMEM((blocks, tile, width), jnp.float32)],
        ),
        out_shape=jax.ShapeDtypeStruct((blocks, tile, width), jnp.bfloat16),
        cost_estimate=pl.CostEstimate(
            flops=2 * slots * tile * tile * width,
            bytes_accessed=slots * tile * (tile + width) * 2,
            transcendentals=0,
        ),
        name="tile_sums",
    )(offsets, masks, feats)


def backward_kernel(offset_ref, mask_ref, feat_ref, base_ref, out_ref, total_ref):
    step = pl.program_id(0)

    @pl.when(step == 0)
    def _():
        total_ref[...] = base_ref[...]

    for t in range(STEP):
        at = offset_ref[step * STEP + t]
        total_ref[at] += jnp.dot(mask_ref[t], feat_ref[t], preferred_element_type=jnp.float32)

    @pl.when(step == pl.num_programs(0) - 1)
    def _():
        out_ref[...] = total_ref[...].astype(out_ref.dtype)


def tile_sums_onto(offsets, masks, feats, base):
    slots, tile, width = feats.shape
    blocks = base.shape[0]
    whole = pl.BlockSpec((blocks, tile, width), lambda i, o: (0, 0, 0))
    return pl.pallas_call(
        backward_kernel,
        grid_spec=pltpu.PrefetchScalarGridSpec(
            num_scalar_prefetch=1,
            grid=(slots // STEP,),
            in_specs=[
                pl.BlockSpec((STEP, tile, tile), lambda i, o: (i, 0, 0)),
                pl.BlockSpec((STEP, tile, width), lambda i, o: (i, 0, 0)),
                whole,
            ],
            out_specs=whole,
            scratch_shapes=[pltpu.VMEM((blocks, tile, width), jnp.float32)],
        ),
        out_shape=jax.ShapeDtypeStruct((blocks, tile, width), jnp.bfloat16),
        cost_estimate=pl.CostEstimate(
            flops=2 * slots * tile * tile * width,
            bytes_accessed=slots * tile * (tile + width) * 2,
            transcendentals=0,
        ),
        name="tile_sums_onto",
    )(offsets, masks, feats, base)


def pick_kernel(offset_ref, block_ref, out_ref):
    step = pl.program_id(0)
    for t in range(STEP):
        out_ref[t] = block_ref[offset_ref[step * STEP + t]]


def picked(offsets, blocks):
    slots = offsets.shape[0]
    n, tile, width = blocks.shape
    return pl.pallas_call(
        pick_kernel,
        grid_spec=pltpu.PrefetchScalarGridSpec(
            num_scalar_prefetch=1,
            grid=(slots // STEP,),
            in_specs=[pl.BlockSpec((n, tile, width), lambda i, o: (0, 0, 0))],
            out_specs=pl.BlockSpec((STEP, tile, width), lambda i, o: (i, 0, 0)),
        ),
        out_shape=jax.ShapeDtypeStruct((slots, tile, width), blocks.dtype),
        cost_estimate=pl.CostEstimate(
            flops=0, bytes_accessed=(n + slots) * tile * width * 2, transcendentals=0
        ),
        name="picked",
    )(offsets, blocks)


def shards(
    node_feats, node_ids, tile_row, tile_col, tile_count, self_weight, neigh_weight, out_grad
):
    dom_total = lax.axis_size(DOM)
    rep_total = lax.axis_size("rep")
    dom_here = lax.axis_index(DOM)
    rep_here = lax.axis_index("rep")
    core = lax.axis_index("core")
    rows_here, width_in = node_feats.shape
    width_out = self_weight.shape[1]
    blocks_here = rows_here // TILE
    group_blocks = blocks_here * rep_total
    id_blocks = node_ids.reshape(-1, TILE)
    group_first = dom_here * group_blocks
    own_first = group_first + rep_here * blocks_here

    def sent_tiles(table):
        return lax.dynamic_slice(table, (0, rep_here, dom_here), (dom_total, 1, 1)).reshape(-1)

    def held_tiles(table):
        return lax.dynamic_slice(table, (dom_here, rep_here, 0), (1, 1, dom_total)).reshape(-1)

    sent_cols = sent_tiles(tile_col)
    sent_there = sent_cols >= 0
    sent_offset = jnp.where(sent_there, sent_cols - own_first, 0)
    feat_blocks = node_feats.reshape(blocks_here, 1, TILE, width_in)
    choice = sent_offset[:, None, None]
    outgoing = jnp.broadcast_to(feat_blocks[0], (dom_total, TILE, width_in))
    for b in range(1, blocks_here):
        outgoing = jnp.where(choice == b, feat_blocks[b], outgoing)
    arrived = lax.all_to_all(outgoing, DOM, split_axis=0, concat_axis=0, tiled=True)

    held_rows = held_tiles(tile_row)
    held_there = held_rows >= 0
    held_block = jnp.where(held_there, held_rows, 0)
    held_cols = jnp.where(held_there, held_tiles(tile_col), 0)
    held_limits = jnp.where(held_there, held_tiles(tile_count), 0)
    held_offset = jnp.where(held_there, held_block - group_first, 0)
    held_masks = edge_masks(id_blocks[held_block], id_blocks[held_cols], held_limits, False)

    sent_rows = jnp.where(sent_there, sent_tiles(tile_row), 0)
    sent_limits = jnp.where(sent_there, sent_tiles(tile_count), 0)
    sent_masks = edge_masks(
        id_blocks[sent_rows], id_blocks[jnp.where(sent_there, sent_cols, 0)], sent_limits, True
    )

    partial_sums = tile_sums(held_offset, held_masks, arrived, group_blocks)
    pieces = lax.all_to_all(
        partial_sums.reshape(rep_total, rows_here, width_in), "rep", 0, 0, tiled=True
    )
    summed = pieces.astype(jnp.float32).sum(axis=0)

    group_rows = lax.dynamic_slice_in_dim(tile_row, dom_here, 1, 0).reshape(-1)
    group_limits = lax.dynamic_slice_in_dim(tile_count, dom_here, 1, 0).reshape(-1)
    owned_rows = group_rows[:, None] == own_first + jnp.arange(blocks_here)[None, :]
    degree = jnp.sum(jnp.where(owned_rows, group_limits[:, None], 0), axis=0).astype(jnp.float32)
    divisor = jnp.repeat(jnp.maximum(degree, 1.0), TILE)[:, None]
    mean_feats = (summed / divisor).astype(jnp.bfloat16)
    preact = jnp.dot(node_feats, self_weight, preferred_element_type=jnp.float32) + jnp.dot(
        mean_feats, neigh_weight, preferred_element_type=jnp.float32
    )
    hidden_out = jax.nn.silu(preact).astype(jnp.bfloat16)
    logistic = jax.nn.sigmoid(preact)
    pre_grad = (out_grad.astype(jnp.float32) * logistic * (1.0 + preact * (1.0 - logistic))).astype(
        jnp.bfloat16
    )
    over_rows = (((0,), (0,)), ((), ()))
    over_cols = (((1,), (1,)), ((), ()))
    mean_grad = lax.dot_general(
        pre_grad, neigh_weight, over_cols, preferred_element_type=jnp.float32
    )
    spread = (mean_grad / divisor).astype(jnp.bfloat16)
    self_term = lax.dot_general(node_feats, pre_grad, over_rows, preferred_element_type=jnp.float32)
    neigh_term = lax.dot_general(
        mean_feats, pre_grad, over_rows, preferred_element_type=jnp.float32
    )
    first = core == 0
    kept = jnp.where(first, self_term, neigh_term) + lax.ppermute(
        jnp.where(first, neigh_term, self_term), "core", [(0, 1), (1, 0)]
    )
    grad_rows = width_in * width_out // rep_total // width_in
    kept = kept.reshape(rep_total, -1, width_out).astype(jnp.bfloat16)
    kept = jnp.concatenate([kept[:, :, :width_in], kept[:, :, width_in:]], axis=1)
    both = jnp.concatenate(
        [jnp.broadcast_to(spread[None], (rep_total, rows_here, width_in)), kept], axis=1
    )
    both = lax.all_to_all(both, "rep", 0, 0, tiled=True)
    group_spread = both[:, :rows_here].reshape(group_blocks, TILE, width_in)
    share = both[:, rows_here:].astype(jnp.float32).sum(axis=0)

    returning = picked(held_offset, group_spread)
    returning, share = lax.optimization_barrier((returning, share))
    returned = lax.all_to_all(returning, DOM, split_axis=0, concat_axis=0, tiled=True)

    for axis in ("x", "z"):
        bit = 1
        while bit < lax.axis_size(axis):
            share = share + pair_swap(share, axis, bit)
            bit *= 2
    share = share[None] * (1.0 / math.sqrt(rows_here * dom_total * rep_total))
    bit = 1
    while bit < rep_total:
        other = pair_swap(share, "rep", bit)
        low = (rep_here & bit) == 0
        share = jnp.where(
            low, jnp.concatenate([share, other]), jnp.concatenate([other, share])
        )
        bit *= 2
    half = grad_rows // 2
    share = jnp.concatenate([share[:, :half], share[:, half:]], axis=2).reshape(width_in, width_out)
    other = lax.ppermute(share, "core", [(0, 1), (1, 0)])
    self_grad = jnp.where(first, share, other)
    neigh_grad = jnp.where(first, other, share)

    self_back = lax.dot_general(
        pre_grad, self_weight, over_cols, preferred_element_type=jnp.float32
    )
    feat_grad = tile_sums_onto(
        sent_offset, sent_masks, returned, self_back.reshape(blocks_here, TILE, width_in)
    ).reshape(rows_here, width_in)
    return (hidden_out, feat_grad, self_grad, neigh_grad)


def solution(mesh):
    torus = Mesh(mesh.devices.reshape(4, 8, 2, mesh.shape["rep"]), ALL)
    in_specs = (P(ALL, None), P(), P(), P(), P(), P(), P(), P(ALL, None))
    out_specs = (P(ALL, None), P(ALL, None), P(), P())
    return jax.shard_map(
        shards, mesh=torus, in_specs=in_specs, out_specs=out_specs, check_vma=False
    )
```

```python
import math

import jax
import jax.numpy as jnp
from jax import lax
from jax.experimental import pallas as pl
from jax.experimental.pallas import tpu as pltpu
from jax.sharding import Mesh
from jax.sharding import PartitionSpec as P

TILE = 128
DOM = ("x", "z", "core")
ALL = ("x", "z", "core", "rep")
STEP = 8


def edge_masks(row_ids, col_ids, limits, swapped):
    u = row_ids % 4093
    v = col_ids % 4091
    if swapped:
        u, v = u[:, None, :], v[:, :, None]
    else:
        u, v = u[:, :, None], v[:, None, :]
    hashed = (u * v + u + 3 * v) % 4099 % TILE
    return (hashed < limits[:, None, None]).astype(jnp.bfloat16)


def pair_swap(x, axis, bit):
    n = lax.axis_size(axis)
    return lax.ppermute(x, axis, [(i, i ^ bit) for i in range(n)])


def forward_kernel(offset_ref, mask_ref, feat_ref, out_ref, total_ref):
    step = pl.program_id(0)

    @pl.when(step == 0)
    def _():
        total_ref[...] = jnp.zeros_like(total_ref)

    products = [
        jnp.dot(mask_ref[t], feat_ref[t], preferred_element_type=jnp.float32) for t in range(STEP)
    ]
    for t in range(STEP):
        total_ref[offset_ref[step * STEP + t]] += products[t]

    @pl.when(step == pl.num_programs(0) - 1)
    def _():
        out_ref[...] = total_ref[...].astype(out_ref.dtype)


def tile_sums(offsets, masks, feats, blocks):
    slots, tile, width = feats.shape
    return pl.pallas_call(
        forward_kernel,
        grid_spec=pltpu.PrefetchScalarGridSpec(
            num_scalar_prefetch=1,
            grid=(slots // STEP,),
            in_specs=[
                pl.BlockSpec((STEP, tile, tile), lambda i, o: (i, 0, 0)),
                pl.BlockSpec((STEP, tile, width), lambda i, o: (i, 0, 0)),
            ],
            out_specs=pl.BlockSpec((blocks, tile, width), lambda i, o: (0, 0, 0)),
            scratch_shapes=[pltpu.VMEM((blocks, tile, width), jnp.float32)],
        ),
        out_shape=jax.ShapeDtypeStruct((blocks, tile, width), jnp.bfloat16),
        cost_estimate=pl.CostEstimate(
            flops=2 * slots * tile * tile * width,
            bytes_accessed=slots * tile * (tile + width) * 2,
            transcendentals=0,
        ),
        name="tile_sums",
    )(offsets, masks, feats)


def products_kernel(offset_ref, mask_ref, block_ref, out_ref):
    step = pl.program_id(0)
    for t in range(STEP):
        out_ref[t] = jnp.dot(
            mask_ref[t],
            block_ref[offset_ref[step * STEP + t]],
            preferred_element_type=jnp.float32,
        ).astype(out_ref.dtype)


def tile_products(offsets, masks, blocks):
    slots, tile, _ = masks.shape
    n, _, width = blocks.shape
    return pl.pallas_call(
        products_kernel,
        grid_spec=pltpu.PrefetchScalarGridSpec(
            num_scalar_prefetch=1,
            grid=(slots // STEP,),
            in_specs=[
                pl.BlockSpec((STEP, tile, tile), lambda i, o: (i, 0, 0)),
                pl.BlockSpec((n, tile, width), lambda i, o: (0, 0, 0)),
            ],
            out_specs=pl.BlockSpec((STEP, tile, width), lambda i, o: (i, 0, 0)),
        ),
        out_shape=jax.ShapeDtypeStruct((slots, tile, width), jnp.bfloat16),
        cost_estimate=pl.CostEstimate(
            flops=2 * slots * tile * tile * width,
            bytes_accessed=slots * tile * (tile + width) * 2,
            transcendentals=0,
        ),
        name="tile_products",
    )(offsets, masks, blocks)


def gathered_kernel(offset_ref, part_ref, out_ref, total_ref):
    step = pl.program_id(0)

    @pl.when(step == 0)
    def _():
        total_ref[...] = jnp.zeros_like(total_ref)

    for t in range(STEP):
        total_ref[offset_ref[step * STEP + t]] += part_ref[t].astype(jnp.float32)

    @pl.when(step == pl.num_programs(0) - 1)
    def _():
        out_ref[...] = total_ref[...].astype(out_ref.dtype)


def summed_into(offsets, parts, blocks):
    slots, tile, width = parts.shape
    return pl.pallas_call(
        gathered_kernel,
        grid_spec=pltpu.PrefetchScalarGridSpec(
            num_scalar_prefetch=1,
            grid=(slots // STEP,),
            in_specs=[pl.BlockSpec((STEP, tile, width), lambda i, o: (i, 0, 0))],
            out_specs=pl.BlockSpec((blocks, tile, width), lambda i, o: (0, 0, 0)),
            scratch_shapes=[pltpu.VMEM((blocks, tile, width), jnp.float32)],
        ),
        out_shape=jax.ShapeDtypeStruct((blocks, tile, width), jnp.bfloat16),
        cost_estimate=pl.CostEstimate(
            flops=slots * tile * width, bytes_accessed=slots * tile * width * 2, transcendentals=0
        ),
        name="summed_into",
    )(offsets, parts)


def pick_kernel(offset_ref, block_ref, out_ref, sems):
    slots = out_ref.shape[0]
    copies = [
        pltpu.make_async_copy(block_ref.at[offset_ref[t]], out_ref.at[t], sems.at[t])
        for t in range(slots)
    ]
    for copy in copies:
        copy.start()
    for copy in copies:
        copy.wait()


def picked(offsets, blocks):
    slots = offsets.shape[0]
    n, tile, width = blocks.shape
    return pl.pallas_call(
        pick_kernel,
        in_specs=[
            pl.BlockSpec(memory_space=pltpu.SMEM),
            pl.BlockSpec(memory_space=pltpu.VMEM),
        ],
        out_specs=pl.BlockSpec(memory_space=pl.ANY),
        scratch_shapes=[pltpu.SemaphoreType.DMA((slots,))],
        out_shape=jax.ShapeDtypeStruct((slots, tile, width), blocks.dtype),
        cost_estimate=pl.CostEstimate(
            flops=0, bytes_accessed=(n + slots) * tile * width * 2, transcendentals=0
        ),
        name="picked",
    )(offsets, blocks)


def halved(x, axis, bit):
    half = x.shape[0] // 2
    low = (lax.axis_index(axis) & bit) == 0
    other = pair_swap(jnp.where(low, x[half:], x[:half]), axis, bit)
    return jnp.where(low, x[:half], x[half:]) + other


def doubled(x, axis, bit):
    low = (lax.axis_index(axis) & bit) == 0
    other = pair_swap(x, axis, bit)
    return jnp.where(low, jnp.concatenate([x, other]), jnp.concatenate([other, x]))


def shards(
    node_feats, node_ids, tile_row, tile_col, tile_count, self_weight, neigh_weight, out_grad
):
    dom_total = lax.axis_size(DOM)
    rep_total = lax.axis_size("rep")
    x_total, z_total, core_total = (lax.axis_size(a) for a in DOM)
    dom_here = lax.axis_index(DOM)
    rep_here = lax.axis_index("rep")
    x_here, z_here, core = (lax.axis_index(a) for a in DOM)
    rows_here, width_in = node_feats.shape
    blocks_here = rows_here // TILE
    group_blocks = blocks_here * rep_total
    id_blocks = node_ids.reshape(-1, TILE)
    group_first = dom_here * group_blocks
    bits_of = {
        a: [1 << i for i in range(lax.axis_size(a).bit_length() - 1)] for a in ("x", "z", "rep")
    }

    column = lax.all_to_all(
        jnp.broadcast_to(node_feats[None], (z_total, rows_here, width_in)), "z", 0, 0, tiled=True
    ).reshape(z_total * blocks_here, TILE, width_in)

    def passed_tiles(table):
        table = table.reshape(x_total, z_total, core_total, rep_total, dom_total)
        table = lax.dynamic_slice(
            table, (0, z_here, 0, rep_here, 0), (x_total, 1, core_total, 1, dom_total)
        ).reshape(x_total * core_total, x_total, z_total, core_total)
        table = lax.dynamic_slice_in_dim(table, x_here, 1, 1)
        return lax.dynamic_slice_in_dim(table, core, 1, 3).reshape(-1)

    passed_cols = passed_tiles(tile_col)
    place = jnp.tile(jnp.arange(z_total), x_total * core_total)
    passed_first = ((x_here * z_total + place) * core_total + core) * group_blocks
    passed_first = passed_first + rep_here * blocks_here
    passed_offset = place * blocks_here + jnp.where(
        passed_cols >= 0, passed_cols - passed_first, 0
    )

    def held_tiles(table):
        row = lax.dynamic_slice(table, (dom_here, rep_here, 0), (1, 1, dom_total))
        return row.reshape(x_total, z_total, core_total).swapaxes(1, 2).reshape(-1)

    held_rows = held_tiles(tile_row)
    held_there = held_rows >= 0
    held_block = jnp.where(held_there, held_rows, 0)
    held_cols = jnp.where(held_there, held_tiles(tile_col), 0)
    held_limits = jnp.where(held_there, held_tiles(tile_count), 0)
    held_offset = jnp.where(held_there, held_block - group_first, 0)
    row_ids, col_ids = id_blocks[held_block], id_blocks[held_cols]
    masks = edge_masks(row_ids, col_ids, held_limits, False)
    masks_swapped = edge_masks(row_ids, col_ids, held_limits, True)

    arrived = lax.all_to_all(
        picked(passed_offset, column), ("x", "core"), 0, 0, tiled=True
    )
    partial_sums = tile_sums(held_offset, masks, arrived, group_blocks)
    pieces = lax.all_to_all(
        partial_sums.reshape(rep_total, rows_here, width_in), "rep", 0, 0, tiled=True
    )
    summed = pieces.astype(jnp.float32).sum(axis=0)

    own_first = group_first + rep_here * blocks_here
    group_rows = lax.dynamic_slice_in_dim(tile_row, dom_here, 1, 0).reshape(-1)
    group_limits = lax.dynamic_slice_in_dim(tile_count, dom_here, 1, 0).reshape(-1)
    owned_rows = group_rows[:, None] == own_first + jnp.arange(blocks_here)[None, :]
    degree = jnp.sum(jnp.where(owned_rows, group_limits[:, None], 0), axis=0).astype(jnp.float32)
    divisor = jnp.repeat(jnp.maximum(degree, 1.0), TILE)[:, None]
    mean_feats = (summed / divisor).astype(jnp.bfloat16)
    preact = jnp.dot(node_feats, self_weight, preferred_element_type=jnp.float32) + jnp.dot(
        mean_feats, neigh_weight, preferred_element_type=jnp.float32
    )
    hidden_out = jax.nn.silu(preact).astype(jnp.bfloat16)
    logistic = jax.nn.sigmoid(preact)
    pre_grad = (out_grad.astype(jnp.float32) * logistic * (1.0 + preact * (1.0 - logistic))).astype(
        jnp.bfloat16
    )
    over_rows = (((0,), (0,)), ((), ()))
    over_cols = (((1,), (1,)), ((), ()))
    mean_grad = lax.dot_general(
        pre_grad, neigh_weight, over_cols, preferred_element_type=jnp.float32
    )
    spread = (mean_grad / divisor).astype(jnp.bfloat16)
    group_spread = lax.all_to_all(
        jnp.broadcast_to(spread[None], (rep_total, rows_here, width_in)), "rep", 0, 0, tiled=True
    ).reshape(group_blocks, TILE, width_in)

    self_term = lax.dot_general(node_feats, pre_grad, over_rows, preferred_element_type=jnp.float32)
    neigh_term = lax.dot_general(
        mean_feats, pre_grad, over_rows, preferred_element_type=jnp.float32
    )
    first = core == 0
    share = jnp.where(first, self_term, neigh_term) + lax.ppermute(
        jnp.where(first, neigh_term, self_term), "core", [(0, 1), (1, 0)]
    )
    for axis in ("x", "z"):
        for bit in bits_of[axis]:
            share = halved(share, axis, bit)

    returning = tile_products(held_offset, masks_swapped, group_spread)
    returning, share = lax.optimization_barrier((returning, share))
    returned = lax.all_to_all(returning, ("x", "core"), 0, 0, tiled=True)
    for bit in bits_of["rep"]:
        share = share + pair_swap(share, "rep", bit)
    share = share * (1.0 / math.sqrt(rows_here * dom_total * rep_total))
    for bit in reversed(bits_of["z"]):
        share = doubled(share, "z", bit)
    column_sums = summed_into(passed_offset, returned, z_total * blocks_here)
    column_sums, share = lax.optimization_barrier((column_sums, share))
    parts = lax.all_to_all(
        column_sums.reshape(z_total, rows_here, width_in), "z", 0, 0, tiled=True
    )
    for bit in reversed(bits_of["x"]):
        share = doubled(share, "x", bit)
    other = lax.ppermute(share, "core", [(0, 1), (1, 0)])
    self_grad = jnp.where(first, share, other)
    neigh_grad = jnp.where(first, other, share)

    self_back = lax.dot_general(
        pre_grad, self_weight, over_cols, preferred_element_type=jnp.float32
    )
    transposed = parts.astype(jnp.float32).sum(axis=0)
    feat_grad = (self_back + transposed).astype(jnp.bfloat16)
    return (hidden_out, feat_grad, self_grad, neigh_grad)


def solution(mesh):
    torus = Mesh(mesh.devices.reshape(4, 8, 2, mesh.shape["rep"]), ALL)
    in_specs = (P(ALL, None), P(), P(), P(), P(), P(), P(), P(ALL, None))
    out_specs = (P(ALL, None), P(ALL, None), P(), P())
    return jax.shard_map(
        shards, mesh=torus, in_specs=in_specs, out_specs=out_specs, check_vma=False
    )
```

```python
import math

import jax
import jax.numpy as jnp
from jax import lax
from jax.experimental import pallas as pl
from jax.experimental.pallas import tpu as pltpu
from jax.sharding import Mesh
from jax.sharding import PartitionSpec as P

TILE = 128
DOM = ("x", "z", "core")
ALL = ("x", "z", "core", "rep")
STEP = 8


def edge_masks(row_ids, col_ids, limits, swapped):
    u = row_ids % 4093
    v = col_ids % 4091
    if swapped:
        u, v = u[:, None, :], v[:, :, None]
    else:
        u, v = u[:, :, None], v[:, None, :]
    hashed = (u * v + u + 3 * v) % 4099 % TILE
    return (hashed < limits[:, None, None]).astype(jnp.bfloat16)


def pair_swap(x, axis, bit):
    n = lax.axis_size(axis)
    return lax.ppermute(x, axis, [(i, i ^ bit) for i in range(n)])


def forward_kernel(offset_ref, mask_ref, feat_ref, out_ref, total_ref):
    step = pl.program_id(0)

    @pl.when(step == 0)
    def _():
        total_ref[...] = jnp.zeros_like(total_ref)

    products = [
        jnp.dot(mask_ref[t], feat_ref[t], preferred_element_type=jnp.float32) for t in range(STEP)
    ]
    for t in range(STEP):
        total_ref[offset_ref[step * STEP + t]] += products[t]

    @pl.when(step == pl.num_programs(0) - 1)
    def _():
        out_ref[...] = total_ref[...].astype(out_ref.dtype)


def tile_sums(offsets, masks, feats, blocks):
    slots, tile, width = feats.shape
    return pl.pallas_call(
        forward_kernel,
        grid_spec=pltpu.PrefetchScalarGridSpec(
            num_scalar_prefetch=1,
            grid=(slots // STEP,),
            in_specs=[
                pl.BlockSpec((STEP, tile, tile), lambda i, o: (i, 0, 0)),
                pl.BlockSpec((STEP, tile, width), lambda i, o: (i, 0, 0)),
            ],
            out_specs=pl.BlockSpec((blocks, tile, width), lambda i, o: (0, 0, 0)),
            scratch_shapes=[pltpu.VMEM((blocks, tile, width), jnp.float32)],
        ),
        out_shape=jax.ShapeDtypeStruct((blocks, tile, width), jnp.bfloat16),
        cost_estimate=pl.CostEstimate(
            flops=2 * slots * tile * tile * width,
            bytes_accessed=slots * tile * (tile + width) * 2,
            transcendentals=0,
        ),
        name="tile_sums",
    )(offsets, masks, feats)


def products_kernel(offset_ref, mask_ref, block_ref, out_ref):
    step = pl.program_id(0)
    for t in range(STEP):
        out_ref[t] = jnp.dot(
            mask_ref[t],
            block_ref[offset_ref[step * STEP + t]],
            preferred_element_type=jnp.float32,
        ).astype(out_ref.dtype)


def tile_products(offsets, masks, blocks):
    slots, tile, _ = masks.shape
    n, _, width = blocks.shape
    return pl.pallas_call(
        products_kernel,
        grid_spec=pltpu.PrefetchScalarGridSpec(
            num_scalar_prefetch=1,
            grid=(slots // STEP,),
            in_specs=[
                pl.BlockSpec((STEP, tile, tile), lambda i, o: (i, 0, 0)),
                pl.BlockSpec((n, tile, width), lambda i, o: (0, 0, 0)),
            ],
            out_specs=pl.BlockSpec((STEP, tile, width), lambda i, o: (i, 0, 0)),
        ),
        out_shape=jax.ShapeDtypeStruct((slots, tile, width), jnp.bfloat16),
        cost_estimate=pl.CostEstimate(
            flops=2 * slots * tile * tile * width,
            bytes_accessed=slots * tile * (tile + width) * 2,
            transcendentals=0,
        ),
        name="tile_products",
    )(offsets, masks, blocks)


def gathered_kernel(offset_ref, part_ref, out_ref, total_ref):
    step = pl.program_id(0)

    @pl.when(step == 0)
    def _():
        total_ref[...] = jnp.zeros_like(total_ref)

    for t in range(STEP):
        total_ref[offset_ref[step * STEP + t]] += part_ref[t].astype(jnp.float32)

    @pl.when(step == pl.num_programs(0) - 1)
    def _():
        out_ref[...] = total_ref[...].astype(out_ref.dtype)


def summed_into(offsets, parts, blocks):
    slots, tile, width = parts.shape
    return pl.pallas_call(
        gathered_kernel,
        grid_spec=pltpu.PrefetchScalarGridSpec(
            num_scalar_prefetch=1,
            grid=(slots // STEP,),
            in_specs=[pl.BlockSpec((STEP, tile, width), lambda i, o: (i, 0, 0))],
            out_specs=pl.BlockSpec((blocks, tile, width), lambda i, o: (0, 0, 0)),
            scratch_shapes=[pltpu.VMEM((blocks, tile, width), jnp.float32)],
        ),
        out_shape=jax.ShapeDtypeStruct((blocks, tile, width), jnp.bfloat16),
        cost_estimate=pl.CostEstimate(
            flops=slots * tile * width, bytes_accessed=slots * tile * width * 2, transcendentals=0
        ),
        name="summed_into",
    )(offsets, parts)


def pick_kernel(offset_ref, block_ref, out_ref, sems):
    slots = out_ref.shape[0]
    copies = [
        pltpu.make_async_copy(block_ref.at[offset_ref[t]], out_ref.at[t], sems.at[t])
        for t in range(slots)
    ]
    for copy in copies:
        copy.start()
    for copy in copies:
        copy.wait()


def picked(offsets, blocks):
    slots = offsets.shape[0]
    n, tile, width = blocks.shape
    return pl.pallas_call(
        pick_kernel,
        in_specs=[
            pl.BlockSpec(memory_space=pltpu.SMEM),
            pl.BlockSpec(memory_space=pl.ANY),
        ],
        out_specs=pl.BlockSpec(memory_space=pl.ANY),
        scratch_shapes=[pltpu.SemaphoreType.DMA((slots,))],
        out_shape=jax.ShapeDtypeStruct((slots, tile, width), blocks.dtype),
        cost_estimate=pl.CostEstimate(
            flops=0, bytes_accessed=(n + slots) * tile * width * 2, transcendentals=0
        ),
        name="picked",
    )(offsets, blocks)


def shifted(x, axis, by):
    n = lax.axis_size(axis)
    return lax.ppermute(x, axis, [(i, (i + by) % n) for i in range(n)])


DISTANCES = (-3, 0, 3, -4, -1, 2, -2, 1)


def place_of(device, here):
    far = (device - here + 4) % 8 - 4
    return sum(jnp.where(far == d, i, 0) for i, d in enumerate(DISTANCES))


def gather_of_eight(x, axis):
    near = jnp.stack([shifted(x, axis, 3), x, shifted(x, axis, -3)])
    return jnp.concatenate([near, shifted(near, axis, 1), shifted(near[:2], axis, -1)])


def sum_of_eight(x, axis):
    above = shifted(x[3:6], axis, -1).astype(jnp.float32)
    below = shifted(x[6:8], axis, 1).astype(jnp.float32)
    low = x[0].astype(jnp.float32) + above[0] + below[0]
    own = x[1].astype(jnp.float32) + above[1] + below[1]
    high = x[2].astype(jnp.float32) + above[2]
    low = shifted(low.astype(x.dtype), axis, -3).astype(jnp.float32)
    high = shifted(high.astype(x.dtype), axis, 3).astype(jnp.float32)
    return own + low + high


def halved(x, axis, bit):
    half = x.shape[0] // 2
    low = (lax.axis_index(axis) & bit) == 0
    other = pair_swap(jnp.where(low, x[half:], x[:half]), axis, bit)
    return jnp.where(low, x[:half], x[half:]) + other


def doubled(x, axis, bit):
    low = (lax.axis_index(axis) & bit) == 0
    other = pair_swap(x, axis, bit)
    return jnp.where(low, jnp.concatenate([x, other]), jnp.concatenate([other, x]))


def shards(
    node_feats, node_ids, tile_row, tile_col, tile_count, self_weight, neigh_weight, out_grad
):
    dom_total = lax.axis_size(DOM)
    rep_total = lax.axis_size("rep")
    x_total, z_total, core_total = (lax.axis_size(a) for a in DOM)
    dom_here = lax.axis_index(DOM)
    rep_here = lax.axis_index("rep")
    x_here, z_here, core = (lax.axis_index(a) for a in DOM)
    rows_here, width_in = node_feats.shape
    blocks_here = rows_here // TILE
    group_blocks = blocks_here * rep_total
    id_blocks = node_ids.reshape(-1, TILE)
    group_first = dom_here * group_blocks
    bits_of = {
        a: [1 << i for i in range(lax.axis_size(a).bit_length() - 1)] for a in ("x", "z", "rep")
    }

    half_in = width_in // 2

    column_1 = lax.all_to_all(
        jnp.broadcast_to(node_feats[None, :, :half_in], (z_total, rows_here, half_in)),
        "z",
        0,
        0,
        tiled=True,
    ).reshape(z_total * blocks_here, TILE, half_in)

    def passed_tiles(table):
        table = table.reshape(x_total, z_total, core_total, rep_total, dom_total)
        table = lax.dynamic_slice(
            table, (0, z_here, 0, rep_here, 0), (x_total, 1, core_total, 1, dom_total)
        ).reshape(x_total * core_total, x_total, z_total, core_total)
        table = lax.dynamic_slice_in_dim(table, x_here, 1, 1)
        return lax.dynamic_slice_in_dim(table, core, 1, 3).reshape(-1)

    passed_cols = passed_tiles(tile_col)
    place = jnp.tile(jnp.arange(z_total), x_total * core_total)
    passed_first = ((x_here * z_total + place) * core_total + core) * group_blocks
    passed_first = passed_first + rep_here * blocks_here
    passed_block = jnp.where(passed_cols >= 0, passed_cols - passed_first, 0)
    passed_offset = place * blocks_here + passed_block
    passed_near = place_of(place, z_here) * blocks_here + passed_block

    def held_tiles(table):
        row = lax.dynamic_slice(table, (dom_here, rep_here, 0), (1, 1, dom_total))
        return row.reshape(x_total, z_total, core_total).swapaxes(1, 2).reshape(-1)

    held_rows = held_tiles(tile_row)
    held_there = held_rows >= 0
    held_block = jnp.where(held_there, held_rows, 0)
    held_cols = jnp.where(held_there, held_tiles(tile_col), 0)
    held_limits = jnp.where(held_there, held_tiles(tile_count), 0)
    held_offset = jnp.where(held_there, held_block - group_first, 0)
    row_ids, col_ids = id_blocks[held_block], id_blocks[held_cols]
    masks = edge_masks(row_ids, col_ids, held_limits, False)
    masks_swapped = edge_masks(row_ids, col_ids, held_limits, True)

    held_owner = held_offset // blocks_here
    held_near = place_of(held_owner, rep_here) * blocks_here + held_offset % blocks_here

    column_1, masks, masks_swapped = lax.optimization_barrier((column_1, masks, masks_swapped))
    leaving_1 = picked(passed_offset, column_1)
    leaving_1, second = lax.optimization_barrier((leaving_1, node_feats[:, half_in:]))
    arrived_1 = lax.all_to_all(leaving_1, ("x", "core"), 0, 0, tiled=True)
    column_2 = gather_of_eight(second, "z").reshape(z_total * blocks_here, TILE, half_in)
    leaving_2 = picked(passed_near, column_2)
    arrived_1, leaving_2 = lax.optimization_barrier((arrived_1, leaving_2))
    arrived_2 = lax.all_to_all(leaving_2, ("x", "core"), 0, 0, tiled=True)
    sums_1 = tile_sums(held_near, masks, arrived_1, group_blocks)
    summed_1 = sum_of_eight(sums_1.reshape(rep_total, rows_here, half_in), "rep")
    arrived_2, summed_1 = lax.optimization_barrier((arrived_2, summed_1))
    sums_2 = tile_sums(held_offset, masks, arrived_2, group_blocks)
    pieces = lax.all_to_all(
        sums_2.reshape(rep_total, rows_here, half_in), "rep", 0, 0, tiled=True
    )
    summed = jnp.concatenate([summed_1, pieces.astype(jnp.float32).sum(axis=0)], axis=1)

    own_first = group_first + rep_here * blocks_here
    group_rows = lax.dynamic_slice_in_dim(tile_row, dom_here, 1, 0).reshape(-1)
    group_limits = lax.dynamic_slice_in_dim(tile_count, dom_here, 1, 0).reshape(-1)
    owned_rows = group_rows[:, None] == own_first + jnp.arange(blocks_here)[None, :]
    degree = jnp.sum(jnp.where(owned_rows, group_limits[:, None], 0), axis=0).astype(jnp.float32)
    divisor = jnp.repeat(jnp.maximum(degree, 1.0), TILE)[:, None]
    mean_feats = (summed / divisor).astype(jnp.bfloat16)
    preact = jnp.dot(node_feats, self_weight, preferred_element_type=jnp.float32) + jnp.dot(
        mean_feats, neigh_weight, preferred_element_type=jnp.float32
    )
    hidden_out = jax.nn.silu(preact).astype(jnp.bfloat16)
    logistic = jax.nn.sigmoid(preact)
    pre_grad = (out_grad.astype(jnp.float32) * logistic * (1.0 + preact * (1.0 - logistic))).astype(
        jnp.bfloat16
    )
    over_rows = (((0,), (0,)), ((), ()))
    over_cols = (((1,), (1,)), ((), ()))
    mean_grad = lax.dot_general(
        pre_grad, neigh_weight, over_cols, preferred_element_type=jnp.float32
    )
    spread = (mean_grad / divisor).astype(jnp.bfloat16)
    group_spread = lax.all_to_all(
        jnp.broadcast_to(spread[None], (rep_total, rows_here, width_in)), "rep", 0, 0, tiled=True
    ).reshape(group_blocks, TILE, width_in)

    self_term = lax.dot_general(node_feats, pre_grad, over_rows, preferred_element_type=jnp.float32)
    neigh_term = lax.dot_general(
        mean_feats, pre_grad, over_rows, preferred_element_type=jnp.float32
    )
    first = core == 0
    share = jnp.where(first, self_term, neigh_term) + lax.ppermute(
        jnp.where(first, neigh_term, self_term), "core", [(0, 1), (1, 0)]
    )
    for axis in ("x", "z"):
        for bit in bits_of[axis]:
            share = halved(share, axis, bit)

    returning = tile_products(held_offset, masks_swapped, group_spread)
    returning, share = lax.optimization_barrier((returning, share))
    returned = lax.all_to_all(returning, ("x", "core"), 0, 0, tiled=True)
    for bit in bits_of["rep"]:
        share = share + pair_swap(share, "rep", bit)
    share = share * (1.0 / math.sqrt(rows_here * dom_total * rep_total))
    for bit in reversed(bits_of["z"]):
        share = doubled(share, "z", bit)
    column_sums = summed_into(passed_offset, returned, z_total * blocks_here)
    column_sums, share = lax.optimization_barrier((column_sums, share))
    parts = lax.all_to_all(
        column_sums.reshape(z_total, rows_here, width_in), "z", 0, 0, tiled=True
    )
    for bit in reversed(bits_of["x"]):
        share = doubled(share, "x", bit)
    other = lax.ppermute(share, "core", [(0, 1), (1, 0)])
    self_grad = jnp.where(first, share, other)
    neigh_grad = jnp.where(first, other, share)

    self_back = lax.dot_general(
        pre_grad, self_weight, over_cols, preferred_element_type=jnp.float32
    )
    transposed = parts.astype(jnp.float32).sum(axis=0)
    feat_grad = (self_back + transposed).astype(jnp.bfloat16)
    return (hidden_out, feat_grad, self_grad, neigh_grad)


def solution(mesh):
    torus = Mesh(mesh.devices.reshape(4, 8, 2, mesh.shape["rep"]), ALL)
    in_specs = (P(ALL, None), P(), P(), P(), P(), P(), P(), P(ALL, None))
    out_specs = (P(ALL, None), P(ALL, None), P(), P())
    return jax.shard_map(
        shards, mesh=torus, in_specs=in_specs, out_specs=out_specs, check_vma=False
    )
```

```python
import math

import jax
import jax.numpy as jnp
from jax import lax
from jax.experimental import pallas as pl
from jax.experimental.pallas import tpu as pltpu
from jax.sharding import Mesh
from jax.sharding import PartitionSpec as P

TILE = 128
DOM = ("x", "z", "core")
ALL = ("x", "z", "core", "rep")
STEP = 32
LIMIT = pltpu.CompilerParams(vmem_limit_bytes=40 << 20)


def edge_masks(row_ids, col_ids, limits, swapped):
    u = row_ids % 4093
    v = col_ids % 4091
    if swapped:
        u, v = u[:, None, :], v[:, :, None]
    else:
        u, v = u[:, :, None], v[:, None, :]
    hashed = (u * v + u + 3 * v) % 4099 % TILE
    return (hashed < limits[:, None, None]).astype(jnp.bfloat16)


def pair_swap(x, axis, bit):
    n = lax.axis_size(axis)
    return lax.ppermute(x, axis, [(i, i ^ bit) for i in range(n)])


def forward_kernel(offset_ref, mask_ref, feat_ref, out_ref, total_ref):
    step = pl.program_id(0)

    @pl.when(step == 0)
    def _():
        total_ref[...] = jnp.zeros_like(total_ref)

    products = [
        jnp.dot(mask_ref[t], feat_ref[t], preferred_element_type=jnp.float32) for t in range(STEP)
    ]
    for t in range(STEP):
        total_ref[offset_ref[step * STEP + t]] += products[t]

    @pl.when(step == pl.num_programs(0) - 1)
    def _():
        out_ref[...] = total_ref[...].astype(out_ref.dtype)


def tile_sums(offsets, masks, feats, blocks):
    slots, tile, width = feats.shape
    return pl.pallas_call(
        forward_kernel,
        grid_spec=pltpu.PrefetchScalarGridSpec(
            num_scalar_prefetch=1,
            grid=(slots // STEP,),
            in_specs=[
                pl.BlockSpec((STEP, tile, tile), lambda i, o: (i, 0, 0)),
                pl.BlockSpec((STEP, tile, width), lambda i, o: (i, 0, 0)),
            ],
            out_specs=pl.BlockSpec((blocks, tile, width), lambda i, o: (0, 0, 0)),
            scratch_shapes=[pltpu.VMEM((blocks, tile, width), jnp.float32)],
        ),
        out_shape=jax.ShapeDtypeStruct((blocks, tile, width), jnp.bfloat16),
        cost_estimate=pl.CostEstimate(
            flops=2 * slots * tile * tile * width,
            bytes_accessed=slots * tile * (tile + width) * 2,
            transcendentals=0,
        ),
        compiler_params=LIMIT,
        name="tile_sums",
    )(offsets, masks, feats)


def products_kernel(offset_ref, mask_ref, block_ref, out_ref):
    step = pl.program_id(0)
    for t in range(STEP):
        out_ref[t] = jnp.dot(
            mask_ref[t],
            block_ref[offset_ref[step * STEP + t]],
            preferred_element_type=jnp.float32,
        ).astype(out_ref.dtype)


def tile_products(offsets, masks, blocks):
    slots, tile, _ = masks.shape
    n, _, width = blocks.shape
    return pl.pallas_call(
        products_kernel,
        grid_spec=pltpu.PrefetchScalarGridSpec(
            num_scalar_prefetch=1,
            grid=(slots // STEP,),
            in_specs=[
                pl.BlockSpec((STEP, tile, tile), lambda i, o: (i, 0, 0)),
                pl.BlockSpec((n, tile, width), lambda i, o: (0, 0, 0)),
            ],
            out_specs=pl.BlockSpec((STEP, tile, width), lambda i, o: (i, 0, 0)),
        ),
        out_shape=jax.ShapeDtypeStruct((slots, tile, width), jnp.bfloat16),
        cost_estimate=pl.CostEstimate(
            flops=2 * slots * tile * tile * width,
            bytes_accessed=slots * tile * (tile + width) * 2,
            transcendentals=0,
        ),
        compiler_params=LIMIT,
        name="tile_products",
    )(offsets, masks, blocks)


def gathered_kernel(offset_ref, part_ref, out_ref, total_ref):
    step = pl.program_id(0)

    @pl.when(step == 0)
    def _():
        total_ref[...] = jnp.zeros_like(total_ref)

    for t in range(STEP):
        total_ref[offset_ref[step * STEP + t]] += part_ref[t].astype(jnp.float32)

    @pl.when(step == pl.num_programs(0) - 1)
    def _():
        out_ref[...] = total_ref[...].astype(out_ref.dtype)


def summed_into(offsets, parts, blocks):
    slots, tile, width = parts.shape
    return pl.pallas_call(
        gathered_kernel,
        grid_spec=pltpu.PrefetchScalarGridSpec(
            num_scalar_prefetch=1,
            grid=(slots // STEP,),
            in_specs=[pl.BlockSpec((STEP, tile, width), lambda i, o: (i, 0, 0))],
            out_specs=pl.BlockSpec((blocks, tile, width), lambda i, o: (0, 0, 0)),
            scratch_shapes=[pltpu.VMEM((blocks, tile, width), jnp.float32)],
        ),
        out_shape=jax.ShapeDtypeStruct((blocks, tile, width), jnp.bfloat16),
        cost_estimate=pl.CostEstimate(
            flops=slots * tile * width, bytes_accessed=slots * tile * width * 2, transcendentals=0
        ),
        compiler_params=LIMIT,
        name="summed_into",
    )(offsets, parts)


def pick_kernel(offset_ref, *refs):
    *piece_refs, out_ref, held_ref, in_sems, out_sems = refs
    first = 0
    copies = []
    for piece in piece_refs:
        count = piece.shape[0]
        copies.append(
            pltpu.make_async_copy(
                piece, held_ref.at[pl.ds(first, count)], in_sems.at[len(copies)]
            )
        )
        first += count
    for copy in copies:
        copy.start()
    for copy in copies:
        copy.wait()
    copies = [
        pltpu.make_async_copy(held_ref.at[offset_ref[t]], out_ref.at[t], out_sems.at[t])
        for t in range(out_ref.shape[0])
    ]
    for copy in copies:
        copy.start()
    for copy in copies:
        copy.wait()


def picked(offsets, *pieces):
    slots = offsets.shape[0]
    n = sum(len(piece) for piece in pieces)
    _, tile, width = pieces[0].shape
    dtype = pieces[0].dtype
    return pl.pallas_call(
        pick_kernel,
        in_specs=[pl.BlockSpec(memory_space=pltpu.SMEM)]
        + [pl.BlockSpec(memory_space=pl.ANY)] * len(pieces),
        out_specs=pl.BlockSpec(memory_space=pl.ANY),
        scratch_shapes=[
            pltpu.VMEM((n, tile, width), dtype),
            pltpu.SemaphoreType.DMA((len(pieces),)),
            pltpu.SemaphoreType.DMA((slots,)),
        ],
        out_shape=jax.ShapeDtypeStruct((slots, tile, width), dtype),
        cost_estimate=pl.CostEstimate(
            flops=0, bytes_accessed=(n + slots) * tile * width * 2, transcendentals=0
        ),
        name="picked",
    )(offsets, *pieces)


def shifted(x, axis, by):
    n = lax.axis_size(axis)
    return lax.ppermute(x, axis, [(i, (i + by) % n) for i in range(n)])


DISTANCES = (-3, 0, 3, -4, -1, 2, -2, 1)


def place_of(device, here):
    far = (device - here + 4) % 8 - 4
    return sum(jnp.where(far == d, i, 0) for i, d in enumerate(DISTANCES))


def gather_of_eight(x, axis):
    near = jnp.stack([shifted(x, axis, 3), x, shifted(x, axis, -3)])
    return near, shifted(near, axis, 1), shifted(near[:2], axis, -1)


def sum_of_eight(x, axis):
    above = shifted(x[3:6], axis, -1).astype(jnp.float32)
    below = shifted(x[6:8], axis, 1).astype(jnp.float32)
    low = x[0].astype(jnp.float32) + above[0] + below[0]
    own = x[1].astype(jnp.float32) + above[1] + below[1]
    high = x[2].astype(jnp.float32) + above[2]
    return own, low.astype(x.dtype), high.astype(x.dtype)


def sum_of_eight_ended(own, low, high, axis):
    low = shifted(low, axis, -3).astype(jnp.float32)
    high = shifted(high, axis, 3).astype(jnp.float32)
    return own + low + high


def halved(x, axis, bit):
    half = x.shape[0] // 2
    low = (lax.axis_index(axis) & bit) == 0
    other = pair_swap(jnp.where(low, x[half:], x[:half]), axis, bit)
    return jnp.where(low, x[:half], x[half:]) + other


def doubled(x, axis, bit):
    low = (lax.axis_index(axis) & bit) == 0
    other = pair_swap(x, axis, bit)
    return jnp.where(low, jnp.concatenate([x, other]), jnp.concatenate([other, x]))


def shards(
    node_feats, node_ids, tile_row, tile_col, tile_count, self_weight, neigh_weight, out_grad
):
    dom_total = lax.axis_size(DOM)
    rep_total = lax.axis_size("rep")
    x_total, z_total, core_total = (lax.axis_size(a) for a in DOM)
    dom_here = lax.axis_index(DOM)
    rep_here = lax.axis_index("rep")
    x_here, z_here, core = (lax.axis_index(a) for a in DOM)
    rows_here, width_in = node_feats.shape
    blocks_here = rows_here // TILE
    group_blocks = blocks_here * rep_total
    id_blocks = node_ids.reshape(-1, TILE)
    group_first = dom_here * group_blocks
    bits_of = {
        a: [1 << i for i in range(lax.axis_size(a).bit_length() - 1)] for a in ("x", "z", "rep")
    }

    half_in = width_in // 2

    column_1 = lax.all_to_all(
        jnp.broadcast_to(node_feats[None, :, :half_in], (z_total, rows_here, half_in)),
        "z",
        0,
        0,
        tiled=True,
    ).reshape(z_total * blocks_here, TILE, half_in)

    def passed_tiles(table):
        table = table.reshape(x_total, z_total, core_total, rep_total, dom_total)
        table = lax.dynamic_slice(
            table, (0, z_here, 0, rep_here, 0), (x_total, 1, core_total, 1, dom_total)
        ).reshape(x_total * core_total, x_total, z_total, core_total)
        table = lax.dynamic_slice_in_dim(table, x_here, 1, 1)
        return lax.dynamic_slice_in_dim(table, core, 1, 3).reshape(-1)

    passed_cols = passed_tiles(tile_col)
    place = jnp.tile(jnp.arange(z_total), x_total * core_total)
    passed_first = ((x_here * z_total + place) * core_total + core) * group_blocks
    passed_first = passed_first + rep_here * blocks_here
    passed_block = jnp.where(passed_cols >= 0, passed_cols - passed_first, 0)
    passed_offset = place * blocks_here + passed_block
    passed_near = place_of(place, z_here) * blocks_here + passed_block

    def held_tiles(table):
        row = lax.dynamic_slice(table, (dom_here, rep_here, 0), (1, 1, dom_total))
        return row.reshape(x_total, z_total, core_total).swapaxes(1, 2).reshape(-1)

    held_rows = held_tiles(tile_row)
    held_there = held_rows >= 0
    held_block = jnp.where(held_there, held_rows, 0)
    held_cols = jnp.where(held_there, held_tiles(tile_col), 0)
    held_limits = jnp.where(held_there, held_tiles(tile_count), 0)
    held_offset = jnp.where(held_there, held_block - group_first, 0)
    row_ids, col_ids = id_blocks[held_block], id_blocks[held_cols]
    masks = edge_masks(row_ids, col_ids, held_limits, False)
    masks_swapped = edge_masks(row_ids, col_ids, held_limits, True)

    held_owner = held_offset // blocks_here
    held_near = place_of(held_owner, rep_here) * blocks_here + held_offset % blocks_here

    column_1, masks, masks_swapped = lax.optimization_barrier((column_1, masks, masks_swapped))
    leaving_1 = picked(passed_offset, column_1)
    leaving_1, second = lax.optimization_barrier((leaving_1, node_feats[:, half_in:]))
    arrived_1 = lax.all_to_all(leaving_1, ("x", "core"), 0, 0, tiled=True)
    column_2 = [x.reshape(-1, TILE, half_in) for x in gather_of_eight(second, "z")]
    leaving_2 = picked(passed_near, *column_2)
    arrived_1, leaving_2 = lax.optimization_barrier((arrived_1, leaving_2))
    arrived_2 = lax.all_to_all(leaving_2, ("x", "core"), 0, 0, tiled=True)
    sums_1 = tile_sums(held_near, masks, arrived_1, group_blocks)
    begun_1 = sum_of_eight(sums_1.reshape(rep_total, rows_here, half_in), "rep")
    arrived_2, begun_1 = lax.optimization_barrier((arrived_2, begun_1))
    summed_1 = sum_of_eight_ended(*begun_1, "rep")
    sums_2 = tile_sums(held_offset, masks, arrived_2, group_blocks)
    pieces = lax.all_to_all(
        sums_2.reshape(rep_total, rows_here, half_in), "rep", 0, 0, tiled=True
    )
    summed = jnp.concatenate([summed_1, pieces.astype(jnp.float32).sum(axis=0)], axis=1)

    own_first = group_first + rep_here * blocks_here
    group_rows = lax.dynamic_slice_in_dim(tile_row, dom_here, 1, 0).reshape(-1)
    group_limits = lax.dynamic_slice_in_dim(tile_count, dom_here, 1, 0).reshape(-1)
    owned_rows = group_rows[:, None] == own_first + jnp.arange(blocks_here)[None, :]
    degree = jnp.sum(jnp.where(owned_rows, group_limits[:, None], 0), axis=0).astype(jnp.float32)
    divisor = jnp.repeat(jnp.maximum(degree, 1.0), TILE)[:, None]
    mean_feats = (summed / divisor).astype(jnp.bfloat16)
    preact = jnp.dot(node_feats, self_weight, preferred_element_type=jnp.float32) + jnp.dot(
        mean_feats, neigh_weight, preferred_element_type=jnp.float32
    )
    hidden_out = jax.nn.silu(preact).astype(jnp.bfloat16)
    logistic = jax.nn.sigmoid(preact)
    pre_grad = (out_grad.astype(jnp.float32) * logistic * (1.0 + preact * (1.0 - logistic))).astype(
        jnp.bfloat16
    )
    over_rows = (((0,), (0,)), ((), ()))
    over_cols = (((1,), (1,)), ((), ()))
    mean_grad = lax.dot_general(
        pre_grad, neigh_weight, over_cols, preferred_element_type=jnp.float32
    )
    spread = (mean_grad / divisor).astype(jnp.bfloat16)
    group_spread = lax.all_to_all(
        jnp.broadcast_to(spread[None], (rep_total, rows_here, width_in)), "rep", 0, 0, tiled=True
    ).reshape(group_blocks, TILE, width_in)

    self_term = lax.dot_general(node_feats, pre_grad, over_rows, preferred_element_type=jnp.float32)
    neigh_term = lax.dot_general(
        mean_feats, pre_grad, over_rows, preferred_element_type=jnp.float32
    )
    first = core == 0
    share = jnp.where(first, self_term, neigh_term) + lax.ppermute(
        jnp.where(first, neigh_term, self_term), "core", [(0, 1), (1, 0)]
    )
    for axis in ("x", "z"):
        for bit in bits_of[axis]:
            share = halved(share, axis, bit)

    returning = tile_products(held_offset, masks_swapped, group_spread)
    returning, share = lax.optimization_barrier((returning, share))
    returned = lax.all_to_all(returning, ("x", "core"), 0, 0, tiled=True)
    for bit in bits_of["rep"]:
        share = share + pair_swap(share, "rep", bit)
    share = share * (1.0 / math.sqrt(rows_here * dom_total * rep_total))
    for bit in reversed(bits_of["z"]):
        share = doubled(share, "z", bit)
    column_sums = summed_into(passed_offset, returned, z_total * blocks_here)
    column_sums, share = lax.optimization_barrier((column_sums, share))
    parts = lax.all_to_all(
        column_sums.reshape(z_total, rows_here, width_in), "z", 0, 0, tiled=True
    )
    for bit in reversed(bits_of["x"]):
        share = doubled(share, "x", bit)
    other = lax.ppermute(share, "core", [(0, 1), (1, 0)])
    self_grad = jnp.where(first, share, other)
    neigh_grad = jnp.where(first, other, share)

    self_back = lax.dot_general(
        pre_grad, self_weight, over_cols, preferred_element_type=jnp.float32
    )
    transposed = parts.astype(jnp.float32).sum(axis=0)
    feat_grad = (self_back + transposed).astype(jnp.bfloat16)
    return (hidden_out, feat_grad, self_grad, neigh_grad)


def solution(mesh):
    torus = Mesh(mesh.devices.reshape(4, 8, 2, mesh.shape["rep"]), ALL)
    in_specs = (P(ALL, None), P(), P(), P(), P(), P(), P(), P(ALL, None))
    out_specs = (P(ALL, None), P(ALL, None), P(), P())
    return jax.shard_map(
        shards, mesh=torus, in_specs=in_specs, out_specs=out_specs, check_vma=False
    )
```

```python
import math

import jax
import jax.numpy as jnp
from jax import lax
from jax.experimental import pallas as pl
from jax.experimental.pallas import tpu as pltpu
from jax.sharding import Mesh
from jax.sharding import PartitionSpec as P

TILE = 128
DOM = ("x", "z", "core")
ALL = ("x", "z", "core", "rep")
STEP = 32
LIMIT = pltpu.CompilerParams(vmem_limit_bytes=40 << 20)


def edge_masks(row_ids, col_ids, limits, swapped):
    u = row_ids % 4093
    v = col_ids % 4091
    if swapped:
        u, v = u[:, None, :], v[:, :, None]
    else:
        u, v = u[:, :, None], v[:, None, :]
    hashed = (u * v + u + 3 * v) % 4099 % TILE
    return (hashed < limits[:, None, None]).astype(jnp.bfloat16)


def pair_swap(x, axis, bit):
    n = lax.axis_size(axis)
    return lax.ppermute(x, axis, [(i, i ^ bit) for i in range(n)])


def forward_kernel(offset_ref, mask_ref, feat_ref, out_ref, total_ref):
    step = pl.program_id(0)

    @pl.when(step == 0)
    def _():
        total_ref[...] = jnp.zeros_like(total_ref)

    products = [
        jnp.dot(mask_ref[t], feat_ref[t], preferred_element_type=jnp.float32) for t in range(STEP)
    ]
    for t in range(STEP):
        total_ref[offset_ref[step * STEP + t]] += products[t]

    @pl.when(step == pl.num_programs(0) - 1)
    def _():
        out_ref[...] = total_ref[...].astype(out_ref.dtype)


def tile_sums(offsets, masks, feats, blocks):
    slots, tile, width = feats.shape
    return pl.pallas_call(
        forward_kernel,
        grid_spec=pltpu.PrefetchScalarGridSpec(
            num_scalar_prefetch=1,
            grid=(slots // STEP,),
            in_specs=[
                pl.BlockSpec((STEP, tile, tile), lambda i, o: (i, 0, 0)),
                pl.BlockSpec((STEP, tile, width), lambda i, o: (i, 0, 0)),
            ],
            out_specs=pl.BlockSpec((blocks, tile, width), lambda i, o: (0, 0, 0)),
            scratch_shapes=[pltpu.VMEM((blocks, tile, width), jnp.float32)],
        ),
        out_shape=jax.ShapeDtypeStruct((blocks, tile, width), jnp.bfloat16),
        cost_estimate=pl.CostEstimate(
            flops=2 * slots * tile * tile * width,
            bytes_accessed=slots * tile * (tile + width) * 2,
            transcendentals=0,
        ),
        compiler_params=LIMIT,
        name="tile_sums",
    )(offsets, masks, feats)


def products_kernel(offset_ref, mask_ref, block_ref, out_ref):
    step = pl.program_id(0)
    for t in range(STEP):
        out_ref[t] = jnp.dot(
            mask_ref[t],
            block_ref[offset_ref[step * STEP + t]],
            preferred_element_type=jnp.float32,
        ).astype(out_ref.dtype)


def tile_products(offsets, masks, blocks):
    slots, tile, _ = masks.shape
    n, _, width = blocks.shape
    return pl.pallas_call(
        products_kernel,
        grid_spec=pltpu.PrefetchScalarGridSpec(
            num_scalar_prefetch=1,
            grid=(slots // STEP,),
            in_specs=[
                pl.BlockSpec((STEP, tile, tile), lambda i, o: (i, 0, 0)),
                pl.BlockSpec((n, tile, width), lambda i, o: (0, 0, 0)),
            ],
            out_specs=pl.BlockSpec((STEP, tile, width), lambda i, o: (i, 0, 0)),
        ),
        out_shape=jax.ShapeDtypeStruct((slots, tile, width), jnp.bfloat16),
        cost_estimate=pl.CostEstimate(
            flops=2 * slots * tile * tile * width,
            bytes_accessed=slots * tile * (tile + width) * 2,
            transcendentals=0,
        ),
        compiler_params=LIMIT,
        name="tile_products",
    )(offsets, masks, blocks)


def gathered_kernel(offset_ref, part_ref, out_ref, total_ref):
    step = pl.program_id(0)

    @pl.when(step == 0)
    def _():
        total_ref[...] = jnp.zeros_like(total_ref)

    for t in range(STEP):
        total_ref[offset_ref[step * STEP + t]] += part_ref[t].astype(jnp.float32)

    @pl.when(step == pl.num_programs(0) - 1)
    def _():
        out_ref[...] = total_ref[...].astype(out_ref.dtype)


def summed_into(offsets, parts, blocks):
    slots, tile, width = parts.shape
    return pl.pallas_call(
        gathered_kernel,
        grid_spec=pltpu.PrefetchScalarGridSpec(
            num_scalar_prefetch=1,
            grid=(slots // STEP,),
            in_specs=[pl.BlockSpec((STEP, tile, width), lambda i, o: (i, 0, 0))],
            out_specs=pl.BlockSpec((blocks, tile, width), lambda i, o: (0, 0, 0)),
            scratch_shapes=[pltpu.VMEM((blocks, tile, width), jnp.float32)],
        ),
        out_shape=jax.ShapeDtypeStruct((blocks, tile, width), jnp.bfloat16),
        cost_estimate=pl.CostEstimate(
            flops=slots * tile * width, bytes_accessed=slots * tile * width * 2, transcendentals=0
        ),
        compiler_params=LIMIT,
        name="summed_into",
    )(offsets, parts)


def pick_kernel(offset_ref, *refs):
    *piece_refs, out_ref, held_ref, in_sems, out_sems = refs
    first = 0
    copies = []
    for piece in piece_refs:
        count = piece.shape[0]
        copies.append(
            pltpu.make_async_copy(
                piece, held_ref.at[pl.ds(first, count)], in_sems.at[len(copies)]
            )
        )
        first += count
    for copy in copies:
        copy.start()
    for copy in copies:
        copy.wait()
    copies = [
        pltpu.make_async_copy(held_ref.at[offset_ref[t]], out_ref.at[t], out_sems.at[t])
        for t in range(out_ref.shape[0])
    ]
    for copy in copies:
        copy.start()
    for copy in copies:
        copy.wait()


def picked(offsets, *pieces):
    slots = offsets.shape[0]
    n = sum(len(piece) for piece in pieces)
    _, tile, width = pieces[0].shape
    dtype = pieces[0].dtype
    return pl.pallas_call(
        pick_kernel,
        in_specs=[pl.BlockSpec(memory_space=pltpu.SMEM)]
        + [pl.BlockSpec(memory_space=pl.ANY)] * len(pieces),
        out_specs=pl.BlockSpec(memory_space=pl.ANY),
        scratch_shapes=[
            pltpu.VMEM((n, tile, width), dtype),
            pltpu.SemaphoreType.DMA((len(pieces),)),
            pltpu.SemaphoreType.DMA((slots,)),
        ],
        out_shape=jax.ShapeDtypeStruct((slots, tile, width), dtype),
        cost_estimate=pl.CostEstimate(
            flops=0, bytes_accessed=(n + slots) * tile * width * 2, transcendentals=0
        ),
        name="picked",
    )(offsets, *pieces)


def shifted(x, axis, by):
    n = lax.axis_size(axis)
    return lax.ppermute(x, axis, [(i, (i + by) % n) for i in range(n)])


DISTANCES = (-3, 0, 3, -4, -1, 2, -2, 1)


def place_of(device, here):
    far = (device - here + 4) % 8 - 4
    return sum(jnp.where(far == d, i, 0) for i, d in enumerate(DISTANCES))


def gather_of_eight(x, axis):
    near = jnp.stack([shifted(x, axis, 3), x, shifted(x, axis, -3)])
    return near, shifted(near, axis, 1), shifted(near[:2], axis, -1)


def sum_of_eight(x, axis):
    above = shifted(x[3:6], axis, -1).astype(jnp.float32)
    below = shifted(x[6:8], axis, 1).astype(jnp.float32)
    low = x[0].astype(jnp.float32) + above[0] + below[0]
    own = x[1].astype(jnp.float32) + above[1] + below[1]
    high = x[2].astype(jnp.float32) + above[2]
    return own, low.astype(x.dtype), high.astype(x.dtype)


def sum_of_eight_ended(own, low, high, axis):
    low = shifted(low, axis, -3).astype(jnp.float32)
    high = shifted(high, axis, 3).astype(jnp.float32)
    return own + low + high


def halved(x, axis, bit):
    half = x.shape[0] // 2
    low = (lax.axis_index(axis) & bit) == 0
    other = pair_swap(jnp.where(low, x[half:], x[:half]), axis, bit)
    return jnp.where(low, x[:half], x[half:]) + other


def doubled(x, axis, bit):
    low = (lax.axis_index(axis) & bit) == 0
    other = pair_swap(x, axis, bit)
    return jnp.where(low, jnp.concatenate([x, other]), jnp.concatenate([other, x]))


def shards(
    node_feats, node_ids, tile_row, tile_col, tile_count, self_weight, neigh_weight, out_grad
):
    dom_total = lax.axis_size(DOM)
    rep_total = lax.axis_size("rep")
    x_total, z_total, core_total = (lax.axis_size(a) for a in DOM)
    dom_here = lax.axis_index(DOM)
    rep_here = lax.axis_index("rep")
    x_here, z_here, core = (lax.axis_index(a) for a in DOM)
    rows_here, width_in = node_feats.shape
    blocks_here = rows_here // TILE
    group_blocks = blocks_here * rep_total
    id_blocks = node_ids.reshape(-1, TILE)
    group_first = dom_here * group_blocks
    half_in = width_in // 2

    column_1 = lax.all_to_all(
        jnp.broadcast_to(node_feats[None, :, :half_in], (z_total, rows_here, half_in)),
        "z",
        0,
        0,
        tiled=True,
    ).reshape(z_total * blocks_here, TILE, half_in)

    def passed_tiles(table):
        table = table.reshape(x_total, z_total, core_total, rep_total, dom_total)
        table = lax.dynamic_slice(
            table, (0, z_here, 0, rep_here, 0), (x_total, 1, core_total, 1, dom_total)
        ).reshape(x_total * core_total, x_total, z_total, core_total)
        table = lax.dynamic_slice_in_dim(table, x_here, 1, 1)
        return lax.dynamic_slice_in_dim(table, core, 1, 3).reshape(-1)

    passed_cols = passed_tiles(tile_col)
    place = jnp.tile(jnp.arange(z_total), x_total * core_total)
    passed_first = ((x_here * z_total + place) * core_total + core) * group_blocks
    passed_first = passed_first + rep_here * blocks_here
    passed_block = jnp.where(passed_cols >= 0, passed_cols - passed_first, 0)
    passed_offset = place * blocks_here + passed_block
    passed_near = place_of(place, z_here) * blocks_here + passed_block

    def held_tiles(table):
        row = lax.dynamic_slice(table, (dom_here, rep_here, 0), (1, 1, dom_total))
        return row.reshape(x_total, z_total, core_total).swapaxes(1, 2).reshape(-1)

    held_rows = held_tiles(tile_row)
    held_there = held_rows >= 0
    held_block = jnp.where(held_there, held_rows, 0)
    held_cols = jnp.where(held_there, held_tiles(tile_col), 0)
    held_limits = jnp.where(held_there, held_tiles(tile_count), 0)
    held_offset = jnp.where(held_there, held_block - group_first, 0)
    row_ids, col_ids = id_blocks[held_block], id_blocks[held_cols]
    masks = edge_masks(row_ids, col_ids, held_limits, False)
    masks_swapped = edge_masks(row_ids, col_ids, held_limits, True)

    held_owner = held_offset // blocks_here
    held_near = place_of(held_owner, rep_here) * blocks_here + held_offset % blocks_here

    column_1, masks, masks_swapped = lax.optimization_barrier((column_1, masks, masks_swapped))
    leaving_1 = picked(passed_offset, column_1)
    leaving_1, second = lax.optimization_barrier((leaving_1, node_feats[:, half_in:]))
    arrived_1 = lax.all_to_all(leaving_1, ("x", "core"), 0, 0, tiled=True)
    column_2 = [x.reshape(-1, TILE, half_in) for x in gather_of_eight(second, "z")]
    leaving_2 = picked(passed_near, *column_2)
    arrived_1, leaving_2 = lax.optimization_barrier((arrived_1, leaving_2))
    arrived_2 = lax.all_to_all(leaving_2, ("x", "core"), 0, 0, tiled=True)
    sums_1 = tile_sums(held_near, masks, arrived_1, group_blocks)
    begun_1 = sum_of_eight(sums_1.reshape(rep_total, rows_here, half_in), "rep")
    arrived_2, begun_1 = lax.optimization_barrier((arrived_2, begun_1))
    summed_1 = sum_of_eight_ended(*begun_1, "rep")
    sums_2 = tile_sums(held_offset, masks, arrived_2, group_blocks)
    sums_2, summed_1 = lax.optimization_barrier((sums_2, summed_1))
    pieces = lax.all_to_all(
        sums_2.reshape(rep_total, rows_here, half_in), "rep", 0, 0, tiled=True
    )
    summed = jnp.concatenate([summed_1, pieces.astype(jnp.float32).sum(axis=0)], axis=1)

    own_first = group_first + rep_here * blocks_here
    group_rows = lax.dynamic_slice_in_dim(tile_row, dom_here, 1, 0).reshape(-1)
    group_limits = lax.dynamic_slice_in_dim(tile_count, dom_here, 1, 0).reshape(-1)
    owned_rows = group_rows[:, None] == own_first + jnp.arange(blocks_here)[None, :]
    degree = jnp.sum(jnp.where(owned_rows, group_limits[:, None], 0), axis=0).astype(jnp.float32)
    divisor = jnp.repeat(jnp.maximum(degree, 1.0), TILE)[:, None]
    mean_feats = (summed / divisor).astype(jnp.bfloat16)
    preact = jnp.dot(node_feats, self_weight, preferred_element_type=jnp.float32) + jnp.dot(
        mean_feats, neigh_weight, preferred_element_type=jnp.float32
    )
    hidden_out = jax.nn.silu(preact).astype(jnp.bfloat16)
    logistic = jax.nn.sigmoid(preact)
    pre_grad = (out_grad.astype(jnp.float32) * logistic * (1.0 + preact * (1.0 - logistic))).astype(
        jnp.bfloat16
    )
    over_rows = (((0,), (0,)), ((), ()))
    over_cols = (((1,), (1,)), ((), ()))
    mean_grad = lax.dot_general(
        pre_grad, neigh_weight, over_cols, preferred_element_type=jnp.float32
    )
    spread = (mean_grad / divisor).astype(jnp.bfloat16)
    spread = jnp.broadcast_to(spread[None], (rep_total, rows_here, width_in))
    spread, mean_feats, summing = lax.optimization_barrier((spread, mean_feats, pre_grad))
    group_spread = lax.all_to_all(spread, "rep", 0, 0, tiled=True)
    group_spread = group_spread.reshape(group_blocks, TILE, width_in)

    self_term = lax.dot_general(node_feats, summing, over_rows, preferred_element_type=jnp.float32)
    neigh_term = lax.dot_general(
        mean_feats, summing, over_rows, preferred_element_type=jnp.float32
    )
    first = core == 0
    share = jnp.where(first, self_term, neigh_term) + lax.ppermute(
        jnp.where(first, neigh_term, self_term), "core", [(0, 1), (1, 0)]
    )
    for axis, bit in (("x", 1), ("x", 2), ("z", 1), ("z", 2)):
        share = halved(share, axis, bit)

    returning = tile_products(held_offset, masks_swapped, group_spread)
    returning, share = lax.optimization_barrier((returning, share))
    returned = lax.all_to_all(returning, ("x", "core"), 0, 0, tiled=True)
    for axis, bit in (("z", 4), ("rep", 1), ("rep", 2), ("rep", 4)):
        share = share + pair_swap(share, axis, bit)
    share = share * (1.0 / math.sqrt(rows_here * dom_total * rep_total))
    for bit in (2, 1):
        share = doubled(share, "z", bit)
    column_sums = summed_into(passed_offset, returned, z_total * blocks_here)
    column_sums, share = lax.optimization_barrier((column_sums, share))
    parts = lax.all_to_all(
        column_sums.reshape(z_total, rows_here, width_in), "z", 0, 0, tiled=True
    )
    for bit in (2, 1):
        share = doubled(share, "x", bit)
    other = lax.ppermute(share, "core", [(0, 1), (1, 0)])
    self_grad = jnp.where(first, share, other)
    neigh_grad = jnp.where(first, other, share)

    self_back = lax.dot_general(
        pre_grad, self_weight, over_cols, preferred_element_type=jnp.float32
    )
    transposed = parts.astype(jnp.float32).sum(axis=0)
    feat_grad = (self_back + transposed).astype(jnp.bfloat16)
    return (hidden_out, feat_grad, self_grad, neigh_grad)


def solution(mesh):
    torus = Mesh(mesh.devices.reshape(4, 8, 2, mesh.shape["rep"]), ALL)
    in_specs = (P(ALL, None), P(), P(), P(), P(), P(), P(), P(ALL, None))
    out_specs = (P(ALL, None), P(ALL, None), P(), P())
    return jax.shard_map(
        shards, mesh=torus, in_specs=in_specs, out_specs=out_specs, check_vma=False
    )
```

```python
import math

import jax
import jax.numpy as jnp
from jax import lax
from jax.experimental import pallas as pl
from jax.experimental.pallas import tpu as pltpu
from jax.sharding import Mesh
from jax.sharding import PartitionSpec as P

TILE = 128
DOM = ("x", "z", "core")
ALL = ("x", "z", "core", "rep")
STEP = 32


def edge_masks(row_ids, col_ids, limits, swapped):
    u = row_ids % 4093
    v = col_ids % 4091
    if swapped:
        u, v = u[:, None, :], v[:, :, None]
    else:
        u, v = u[:, :, None], v[:, None, :]
    hashed = (u * v + u + 3 * v) % 4099 % TILE
    return (hashed < limits[:, None, None]).astype(jnp.bfloat16)


def pair_swap(x, axis, bit):
    n = lax.axis_size(axis)
    return lax.ppermute(x, axis, [(i, i ^ bit) for i in range(n)])


def forward_kernel(offset_ref, mask_ref, feat_ref, out_ref, total_ref):
    step = pl.program_id(0)

    @pl.when(step == 0)
    def _():
        total_ref[...] = jnp.zeros_like(total_ref)

    products = [
        jnp.dot(mask_ref[t], feat_ref[t], preferred_element_type=jnp.float32) for t in range(STEP)
    ]
    for t in range(STEP):
        total_ref[offset_ref[step * STEP + t]] += products[t]

    @pl.when(step == pl.num_programs(0) - 1)
    def _():
        out_ref[...] = total_ref[...].astype(out_ref.dtype)


def tile_sums(offsets, masks, feats, blocks):
    slots, tile, width = feats.shape
    return pl.pallas_call(
        forward_kernel,
        grid_spec=pltpu.PrefetchScalarGridSpec(
            num_scalar_prefetch=1,
            grid=(slots // STEP,),
            in_specs=[
                pl.BlockSpec((STEP, tile, tile), lambda i, o: (i, 0, 0)),
                pl.BlockSpec((STEP, tile, width), lambda i, o: (i, 0, 0)),
            ],
            out_specs=pl.BlockSpec((blocks, tile, width), lambda i, o: (0, 0, 0)),
            scratch_shapes=[pltpu.VMEM((blocks, tile, width), jnp.float32)],
        ),
        out_shape=jax.ShapeDtypeStruct((blocks, tile, width), jnp.bfloat16),
        cost_estimate=pl.CostEstimate(
            flops=2 * slots * tile * tile * width,
            bytes_accessed=slots * tile * (tile + width) * 2,
            transcendentals=0,
        ),
        compiler_params=pltpu.CompilerParams(vmem_limit_bytes=40 << 20),
        name="tile_sums",
    )(offsets, masks, feats)


def products_kernel(offset_ref, mask_ref, block_ref, out_ref):
    step = pl.program_id(0)
    for t in range(STEP):
        out_ref[t] = jnp.dot(
            mask_ref[t],
            block_ref[offset_ref[step * STEP + t]],
            preferred_element_type=jnp.float32,
        ).astype(out_ref.dtype)


def tile_products(offsets, masks, blocks, half):
    slots, tile, _ = masks.shape
    n, _, width = blocks.shape
    width = width // 2
    return pl.pallas_call(
        products_kernel,
        grid_spec=pltpu.PrefetchScalarGridSpec(
            num_scalar_prefetch=1,
            grid=(slots // STEP,),
            in_specs=[
                pl.BlockSpec((STEP, tile, tile), lambda i, o: (i, 0, 0)),
                pl.BlockSpec((n, tile, width), lambda i, o: (0, 0, half)),
            ],
            out_specs=pl.BlockSpec((STEP, tile, width), lambda i, o: (i, 0, 0)),
        ),
        out_shape=jax.ShapeDtypeStruct((slots, tile, width), jnp.bfloat16),
        cost_estimate=pl.CostEstimate(
            flops=2 * slots * tile * tile * width,
            bytes_accessed=slots * tile * (tile + width) * 2,
            transcendentals=0,
        ),
        compiler_params=pltpu.CompilerParams(vmem_limit_bytes=60 << 20),
        name="tile_products",
    )(offsets, masks, blocks)


def gathered_kernel(offset_ref, part_ref, out_ref, total_ref):
    step = pl.program_id(0)

    @pl.when(step == 0)
    def _():
        total_ref[...] = jnp.zeros_like(total_ref)

    for t in range(STEP):
        total_ref[offset_ref[step * STEP + t]] += part_ref[t].astype(jnp.float32)

    @pl.when(step == pl.num_programs(0) - 1)
    def _():
        out_ref[...] = total_ref[...].astype(out_ref.dtype)


def summed_into(offsets, parts, blocks):
    slots, tile, width = parts.shape
    return pl.pallas_call(
        gathered_kernel,
        grid_spec=pltpu.PrefetchScalarGridSpec(
            num_scalar_prefetch=1,
            grid=(slots // STEP,),
            in_specs=[pl.BlockSpec((STEP, tile, width), lambda i, o: (i, 0, 0))],
            out_specs=pl.BlockSpec((blocks, tile, width), lambda i, o: (0, 0, 0)),
            scratch_shapes=[pltpu.VMEM((blocks, tile, width), jnp.float32)],
        ),
        out_shape=jax.ShapeDtypeStruct((blocks, tile, width), jnp.bfloat16),
        cost_estimate=pl.CostEstimate(
            flops=slots * tile * width, bytes_accessed=slots * tile * width * 2, transcendentals=0
        ),
        compiler_params=pltpu.CompilerParams(vmem_limit_bytes=40 << 20),
        name="summed_into",
    )(offsets, parts)


def pick_kernel(offset_ref, *refs):
    *piece_refs, out_ref, held_ref, in_sems, out_sems = refs
    first = 0
    copies = []
    for piece in piece_refs:
        count = piece.shape[0]
        copies.append(
            pltpu.make_async_copy(
                piece, held_ref.at[pl.ds(first, count)], in_sems.at[len(copies)]
            )
        )
        first += count
    for copy in copies:
        copy.start()
    for copy in copies:
        copy.wait()
    copies = [
        pltpu.make_async_copy(held_ref.at[offset_ref[t]], out_ref.at[t], out_sems.at[t])
        for t in range(out_ref.shape[0])
    ]
    for copy in copies:
        copy.start()
    for copy in copies:
        copy.wait()


def picked(offsets, *pieces):
    slots = offsets.shape[0]
    n = sum(len(piece) for piece in pieces)
    _, tile, width = pieces[0].shape
    dtype = pieces[0].dtype
    return pl.pallas_call(
        pick_kernel,
        in_specs=[pl.BlockSpec(memory_space=pltpu.SMEM)]
        + [pl.BlockSpec(memory_space=pl.ANY)] * len(pieces),
        out_specs=pl.BlockSpec(memory_space=pl.ANY),
        scratch_shapes=[
            pltpu.VMEM((n, tile, width), dtype),
            pltpu.SemaphoreType.DMA((len(pieces),)),
            pltpu.SemaphoreType.DMA((slots,)),
        ],
        out_shape=jax.ShapeDtypeStruct((slots, tile, width), dtype),
        cost_estimate=pl.CostEstimate(
            flops=0, bytes_accessed=(n + slots) * tile * width * 2, transcendentals=0
        ),
        name="picked",
    )(offsets, *pieces)


def shifted(x, axis, by):
    n = lax.axis_size(axis)
    return lax.ppermute(x, axis, [(i, (i + by) % n) for i in range(n)])


DISTANCES = (-3, 0, 3, -4, -1, 2, -2, 1)


def place_of(device, here):
    far = (device - here + 4) % 8 - 4
    return sum(jnp.where(far == d, i, 0) for i, d in enumerate(DISTANCES))


def gather_of_eight(x, axis):
    near = jnp.stack([shifted(x, axis, 3), x, shifted(x, axis, -3)])
    return near, shifted(near, axis, 1), shifted(near[:2], axis, -1)


def sum_of_eight(x, axis):
    above = shifted(x[3:6], axis, -1).astype(jnp.float32)
    below = shifted(x[6:8], axis, 1).astype(jnp.float32)
    low = x[0].astype(jnp.float32) + above[0] + below[0]
    own = x[1].astype(jnp.float32) + above[1] + below[1]
    high = x[2].astype(jnp.float32) + above[2]
    return own, shifted(low.astype(x.dtype), axis, -3), shifted(high.astype(x.dtype), axis, 3)


def halved(x, axis, bit):
    half = x.shape[0] // 2
    low = (lax.axis_index(axis) & bit) == 0
    other = pair_swap(jnp.where(low, x[half:], x[:half]), axis, bit)
    return jnp.where(low, x[:half], x[half:]) + other


def doubled(x, axis, bit):
    low = (lax.axis_index(axis) & bit) == 0
    other = pair_swap(x, axis, bit)
    return jnp.where(low, jnp.concatenate([x, other]), jnp.concatenate([other, x]))


def shards(
    node_feats, node_ids, tile_row, tile_col, tile_count, self_weight, neigh_weight, out_grad
):
    dom_total = lax.axis_size(DOM)
    rep_total = lax.axis_size("rep")
    x_total, z_total, core_total = (lax.axis_size(a) for a in DOM)
    dom_here = lax.axis_index(DOM)
    rep_here = lax.axis_index("rep")
    x_here, z_here, core = (lax.axis_index(a) for a in DOM)
    rows_here, width_in = node_feats.shape
    blocks_here = rows_here // TILE
    group_blocks = blocks_here * rep_total
    id_blocks = node_ids.reshape(-1, TILE)
    group_first = dom_here * group_blocks
    half_in = width_in // 2

    column_1 = lax.all_to_all(
        jnp.broadcast_to(node_feats[None, :, :half_in], (z_total, rows_here, half_in)),
        "z",
        0,
        0,
        tiled=True,
    ).reshape(z_total * blocks_here, TILE, half_in)

    def passed_tiles(table):
        table = table.reshape(x_total, z_total, core_total, rep_total, dom_total)
        table = lax.dynamic_slice(
            table, (0, z_here, 0, rep_here, 0), (x_total, 1, core_total, 1, dom_total)
        ).reshape(x_total * core_total, x_total, z_total, core_total)
        table = lax.dynamic_slice_in_dim(table, x_here, 1, 1)
        return lax.dynamic_slice_in_dim(table, core, 1, 3).reshape(-1)

    passed_cols = passed_tiles(tile_col)
    place = jnp.tile(jnp.arange(z_total), x_total * core_total)
    passed_first = ((x_here * z_total + place) * core_total + core) * group_blocks
    passed_first = passed_first + rep_here * blocks_here
    passed_block = jnp.where(passed_cols >= 0, passed_cols - passed_first, 0)
    passed_offset = place * blocks_here + passed_block
    passed_near = place_of(place, z_here) * blocks_here + passed_block

    def held_tiles(table):
        row = lax.dynamic_slice(table, (dom_here, rep_here, 0), (1, 1, dom_total))
        return row.reshape(x_total, z_total, core_total).swapaxes(1, 2).reshape(-1)

    held_rows = held_tiles(tile_row)
    held_there = held_rows >= 0
    held_block = jnp.where(held_there, held_rows, 0)
    held_cols = jnp.where(held_there, held_tiles(tile_col), 0)
    held_limits = jnp.where(held_there, held_tiles(tile_count), 0)
    held_offset = jnp.where(held_there, held_block - group_first, 0)
    row_ids, col_ids = id_blocks[held_block], id_blocks[held_cols]
    masks = edge_masks(row_ids, col_ids, held_limits, False)
    masks_swapped = edge_masks(row_ids, col_ids, held_limits, True)

    held_owner = held_offset // blocks_here
    held_near = place_of(held_owner, rep_here) * blocks_here + held_offset % blocks_here

    column_1, masks, masks_swapped = lax.optimization_barrier((column_1, masks, masks_swapped))
    leaving_1 = picked(passed_offset, column_1)
    leaving_1, second = lax.optimization_barrier((leaving_1, node_feats[:, half_in:]))
    arrived_1 = lax.all_to_all(leaving_1, ("x", "core"), 0, 0, tiled=True)
    column_2 = [x.reshape(-1, TILE, half_in) for x in gather_of_eight(second, "z")]
    leaving_2 = picked(passed_near, *column_2)
    arrived_1, leaving_2 = lax.optimization_barrier((arrived_1, leaving_2))
    arrived_2 = lax.all_to_all(leaving_2, ("x", "core"), 0, 0, tiled=True)
    sums_1 = tile_sums(held_near, masks, arrived_1, group_blocks)
    own_1, low_1, high_1 = sum_of_eight(sums_1.reshape(rep_total, rows_here, half_in), "rep")
    arrived_2, low_1, high_1 = lax.optimization_barrier((arrived_2, low_1, high_1))
    summed_1 = own_1 + low_1.astype(jnp.float32) + high_1.astype(jnp.float32)
    sums_2 = tile_sums(held_offset, masks, arrived_2, group_blocks)
    pieces = lax.all_to_all(
        sums_2.reshape(rep_total, rows_here, half_in), "rep", 0, 0, tiled=True
    )
    summed = jnp.concatenate([summed_1, pieces.astype(jnp.float32).sum(axis=0)], axis=1)

    own_first = group_first + rep_here * blocks_here
    group_rows = lax.dynamic_slice_in_dim(tile_row, dom_here, 1, 0).reshape(-1)
    group_limits = lax.dynamic_slice_in_dim(tile_count, dom_here, 1, 0).reshape(-1)
    owned_rows = group_rows[:, None] == own_first + jnp.arange(blocks_here)[None, :]
    degree = jnp.sum(jnp.where(owned_rows, group_limits[:, None], 0), axis=0).astype(jnp.float32)
    divisor = jnp.repeat(jnp.maximum(degree, 1.0), TILE)[:, None]
    mean_feats = (summed / divisor).astype(jnp.bfloat16)
    preact = jnp.dot(node_feats, self_weight, preferred_element_type=jnp.float32) + jnp.dot(
        mean_feats, neigh_weight, preferred_element_type=jnp.float32
    )
    hidden_out = jax.nn.silu(preact).astype(jnp.bfloat16)
    logistic = jax.nn.sigmoid(preact)
    pre_grad = (out_grad.astype(jnp.float32) * logistic * (1.0 + preact * (1.0 - logistic))).astype(
        jnp.bfloat16
    )
    over_rows = (((0,), (0,)), ((), ()))
    over_cols = (((1,), (1,)), ((), ()))
    mean_grad = lax.dot_general(
        pre_grad, neigh_weight, over_cols, preferred_element_type=jnp.float32
    )
    spread = (mean_grad / divisor).astype(jnp.bfloat16)
    spread = jnp.broadcast_to(spread[None], (rep_total, rows_here, width_in))
    spread, mean_feats, summing = lax.optimization_barrier((spread, mean_feats, pre_grad))
    group_spread = lax.all_to_all(spread, "rep", 0, 0, tiled=True)
    group_spread = group_spread.reshape(group_blocks, TILE, width_in)

    self_term = lax.dot_general(node_feats, summing, over_rows, preferred_element_type=jnp.float32)
    neigh_term = lax.dot_general(
        mean_feats, summing, over_rows, preferred_element_type=jnp.float32
    )
    first = core == 0
    share = jnp.where(first, self_term, neigh_term) + lax.ppermute(
        jnp.where(first, neigh_term, self_term), "core", [(0, 1), (1, 0)]
    )
    for axis, bit in (("x", 1), ("x", 2), ("z", 1)):
        share = halved(share, axis, bit)
    share = share + pair_swap(share, "z", 2)

    returning_1 = tile_products(held_offset, masks_swapped, group_spread, 0)
    returning_1, group_spread, share = lax.optimization_barrier((returning_1, group_spread, share))
    returned_1 = lax.all_to_all(returning_1, ("x", "core"), 0, 0, tiled=True)
    returning_2 = tile_products(held_offset, masks_swapped, group_spread, 1)
    for axis, bit in (("z", 4), ("rep", 1), ("rep", 2), ("rep", 4)):
        share = share + pair_swap(share, axis, bit)
    share = share * (1.0 / math.sqrt(rows_here * dom_total * rep_total))
    share = doubled(share, "z", 1)

    returned_1, returning_2, share = lax.optimization_barrier((returned_1, returning_2, share))
    returned_2 = lax.all_to_all(returning_2, ("x", "core"), 0, 0, tiled=True)
    column_1 = summed_into(passed_near, returned_1, z_total * blocks_here)
    own_1, low_1, high_1 = sum_of_eight(column_1.reshape(z_total, rows_here, half_in), "z")
    returned_2, low_1, high_1 = lax.optimization_barrier((returned_2, low_1, high_1))
    column_2 = summed_into(passed_offset, returned_2, z_total * blocks_here)

    column_2, share = lax.optimization_barrier((column_2, share))
    parts = lax.all_to_all(column_2.reshape(z_total, rows_here, half_in), "z", 0, 0, tiled=True)
    for bit in (2, 1):
        share = doubled(share, "x", bit)
    other = lax.ppermute(share, "core", [(0, 1), (1, 0)])
    self_grad = jnp.where(first, share, other)
    neigh_grad = jnp.where(first, other, share)

    self_back = lax.dot_general(
        pre_grad, self_weight, over_cols, preferred_element_type=jnp.float32
    )
    transposed = jnp.concatenate(
        [
            own_1 + low_1.astype(jnp.float32) + high_1.astype(jnp.float32),
            parts.astype(jnp.float32).sum(axis=0),
        ],
        axis=1,
    )
    feat_grad = (self_back + transposed).astype(jnp.bfloat16)
    return (hidden_out, feat_grad, self_grad, neigh_grad)


def solution(mesh):
    torus = Mesh(mesh.devices.reshape(4, 8, 2, mesh.shape["rep"]), ALL)
    in_specs = (P(ALL, None), P(), P(), P(), P(), P(), P(), P(ALL, None))
    out_specs = (P(ALL, None), P(ALL, None), P(), P())
    return jax.shard_map(
        shards, mesh=torus, in_specs=in_specs, out_specs=out_specs, check_vma=False
    )
```

```python
import math

import jax
import jax.numpy as jnp
from jax import lax
from jax.experimental import pallas as pl
from jax.experimental.pallas import tpu as pltpu
from jax.sharding import Mesh
from jax.sharding import PartitionSpec as P

TILE = 128
DOM = ("x", "z", "core")
ALL = ("x", "z", "core", "rep")
STEP = 32


def edge_masks(row_ids, col_ids, limits, swapped):
    u = row_ids % 4093
    v = col_ids % 4091
    if swapped:
        u, v = u[:, None, :], v[:, :, None]
    else:
        u, v = u[:, :, None], v[:, None, :]
    hashed = (u * v + u + 3 * v) % 4099 % TILE
    return (hashed < limits[:, None, None]).astype(jnp.bfloat16)


def pair_swap(x, axis, bit):
    n = lax.axis_size(axis)
    return lax.ppermute(x, axis, [(i, i ^ bit) for i in range(n)])


def forward_kernel(offset_ref, mask_ref, feat_ref, out_ref, total_ref):
    step = pl.program_id(0)

    @pl.when(step == 0)
    def _():
        total_ref[...] = jnp.zeros_like(total_ref)

    products = [
        jnp.dot(mask_ref[t], feat_ref[t], preferred_element_type=jnp.float32) for t in range(STEP)
    ]
    for t in range(STEP):
        total_ref[offset_ref[step * STEP + t]] += products[t]

    @pl.when(step == pl.num_programs(0) - 1)
    def _():
        out_ref[...] = total_ref[...].astype(out_ref.dtype)


def tile_sums(offsets, masks, feats, blocks):
    slots, tile, width = feats.shape
    return pl.pallas_call(
        forward_kernel,
        grid_spec=pltpu.PrefetchScalarGridSpec(
            num_scalar_prefetch=1,
            grid=(slots // STEP,),
            in_specs=[
                pl.BlockSpec((STEP, tile, tile), lambda i, o: (i, 0, 0)),
                pl.BlockSpec((STEP, tile, width), lambda i, o: (i, 0, 0)),
            ],
            out_specs=pl.BlockSpec((blocks, tile, width), lambda i, o: (0, 0, 0)),
            scratch_shapes=[pltpu.VMEM((blocks, tile, width), jnp.float32)],
        ),
        out_shape=jax.ShapeDtypeStruct((blocks, tile, width), jnp.bfloat16),
        cost_estimate=pl.CostEstimate(
            flops=2 * slots * tile * tile * width,
            bytes_accessed=slots * tile * (tile + width) * 2,
            transcendentals=0,
        ),
        compiler_params=pltpu.CompilerParams(vmem_limit_bytes=40 << 20),
        name="tile_sums",
    )(offsets, masks, feats)


def products_kernel(offset_ref, mask_ref, block_ref, out_ref):
    step = pl.program_id(0)
    for t in range(STEP):
        out_ref[t] = jnp.dot(
            mask_ref[t],
            block_ref[offset_ref[step * STEP + t]],
            preferred_element_type=jnp.float32,
        ).astype(out_ref.dtype)


def tile_products(offsets, masks, blocks):
    slots, tile, _ = masks.shape
    n, _, width = blocks.shape
    return pl.pallas_call(
        products_kernel,
        grid_spec=pltpu.PrefetchScalarGridSpec(
            num_scalar_prefetch=1,
            grid=(slots // STEP,),
            in_specs=[
                pl.BlockSpec((STEP, tile, tile), lambda i, o: (i, 0, 0)),
                pl.BlockSpec((n, tile, width), lambda i, o: (0, 0, 0)),
            ],
            out_specs=pl.BlockSpec((STEP, tile, width), lambda i, o: (i, 0, 0)),
        ),
        out_shape=jax.ShapeDtypeStruct((slots, tile, width), jnp.bfloat16),
        cost_estimate=pl.CostEstimate(
            flops=2 * slots * tile * tile * width,
            bytes_accessed=slots * tile * (tile + width) * 2,
            transcendentals=0,
        ),
        compiler_params=pltpu.CompilerParams(vmem_limit_bytes=60 << 20),
        name="tile_products",
    )(offsets, masks, blocks)


def gathered_kernel(offset_ref, part_ref, out_ref, total_ref):
    step = pl.program_id(0)

    @pl.when(step == 0)
    def _():
        total_ref[...] = jnp.zeros_like(total_ref)

    for t in range(STEP):
        total_ref[offset_ref[step * STEP + t]] += part_ref[t].astype(jnp.float32)

    @pl.when(step == pl.num_programs(0) - 1)
    def _():
        out_ref[...] = total_ref[...].astype(out_ref.dtype)


def summed_into(offsets, parts, blocks):
    slots, tile, width = parts.shape
    return pl.pallas_call(
        gathered_kernel,
        grid_spec=pltpu.PrefetchScalarGridSpec(
            num_scalar_prefetch=1,
            grid=(slots // STEP,),
            in_specs=[pl.BlockSpec((STEP, tile, width), lambda i, o: (i, 0, 0))],
            out_specs=pl.BlockSpec((blocks, tile, width), lambda i, o: (0, 0, 0)),
            scratch_shapes=[pltpu.VMEM((blocks, tile, width), jnp.float32)],
        ),
        out_shape=jax.ShapeDtypeStruct((blocks, tile, width), jnp.bfloat16),
        cost_estimate=pl.CostEstimate(
            flops=slots * tile * width, bytes_accessed=slots * tile * width * 2, transcendentals=0
        ),
        compiler_params=pltpu.CompilerParams(vmem_limit_bytes=40 << 20),
        name="summed_into",
    )(offsets, parts)


def pick_kernel(offset_ref, *refs):
    *piece_refs, out_ref, held_ref, in_sems, out_sems = refs
    first = 0
    copies = []
    for piece in piece_refs:
        count = piece.shape[0]
        copies.append(
            pltpu.make_async_copy(
                piece, held_ref.at[pl.ds(first, count)], in_sems.at[len(copies)]
            )
        )
        first += count
    for copy in copies:
        copy.start()
    for copy in copies:
        copy.wait()
    copies = [
        pltpu.make_async_copy(held_ref.at[offset_ref[t]], out_ref.at[t], out_sems.at[t])
        for t in range(out_ref.shape[0])
    ]
    for copy in copies:
        copy.start()
    for copy in copies:
        copy.wait()


def picked(offsets, *pieces):
    slots = offsets.shape[0]
    n = sum(len(piece) for piece in pieces)
    _, tile, width = pieces[0].shape
    dtype = pieces[0].dtype
    return pl.pallas_call(
        pick_kernel,
        in_specs=[pl.BlockSpec(memory_space=pltpu.SMEM)]
        + [pl.BlockSpec(memory_space=pl.ANY)] * len(pieces),
        out_specs=pl.BlockSpec(memory_space=pl.ANY),
        scratch_shapes=[
            pltpu.VMEM((n, tile, width), dtype),
            pltpu.SemaphoreType.DMA((len(pieces),)),
            pltpu.SemaphoreType.DMA((slots,)),
        ],
        out_shape=jax.ShapeDtypeStruct((slots, tile, width), dtype),
        cost_estimate=pl.CostEstimate(
            flops=0, bytes_accessed=(n + slots) * tile * width * 2, transcendentals=0
        ),
        name="picked",
    )(offsets, *pieces)


def shifted(x, axis, by):
    n = lax.axis_size(axis)
    return lax.ppermute(x, axis, [(i, (i + by) % n) for i in range(n)])


DISTANCES = (-3, 0, 3, -4, -1, 2, -2, 1)


def place_of(device, here):
    far = (device - here + 4) % 8 - 4
    return sum(jnp.where(far == d, i, 0) for i, d in enumerate(DISTANCES))


def gather_of_eight(x, axis):
    near = jnp.stack([shifted(x, axis, 3), x, shifted(x, axis, -3)])
    return near, shifted(near, axis, 1), shifted(near[:2], axis, -1)


def sum_of_eight(x, axis):
    above = shifted(x[3:6], axis, -1).astype(jnp.float32)
    below = shifted(x[6:8], axis, 1).astype(jnp.float32)
    low = x[0].astype(jnp.float32) + above[0] + below[0]
    own = x[1].astype(jnp.float32) + above[1] + below[1]
    high = x[2].astype(jnp.float32) + above[2]
    return own, shifted(low.astype(x.dtype), axis, -3), shifted(high.astype(x.dtype), axis, 3)


def halved(x, axis, bit):
    half = x.shape[0] // 2
    low = (lax.axis_index(axis) & bit) == 0
    other = pair_swap(jnp.where(low, x[half:], x[:half]), axis, bit)
    return jnp.where(low, x[:half], x[half:]) + other


def doubled(x, axis, bit):
    low = (lax.axis_index(axis) & bit) == 0
    other = pair_swap(x, axis, bit)
    return jnp.where(low, jnp.concatenate([x, other]), jnp.concatenate([other, x]))


def shards(
    node_feats, node_ids, tile_row, tile_col, tile_count, self_weight, neigh_weight, out_grad
):
    dom_total = lax.axis_size(DOM)
    rep_total = lax.axis_size("rep")
    x_total, z_total, core_total = (lax.axis_size(a) for a in DOM)
    dom_here = lax.axis_index(DOM)
    rep_here = lax.axis_index("rep")
    x_here, z_here, core = (lax.axis_index(a) for a in DOM)
    rows_here, width_in = node_feats.shape
    blocks_here = rows_here // TILE
    group_blocks = blocks_here * rep_total
    id_blocks = node_ids.reshape(-1, TILE)
    group_first = dom_here * group_blocks
    half_in = width_in // 2

    column_1 = lax.all_to_all(
        jnp.broadcast_to(node_feats[None, :, :half_in], (z_total, rows_here, half_in)),
        "z",
        0,
        0,
        tiled=True,
    ).reshape(z_total * blocks_here, TILE, half_in)

    def passed_tiles(table):
        table = table.reshape(x_total, z_total, core_total, rep_total, dom_total)
        table = lax.dynamic_slice(
            table, (0, z_here, 0, rep_here, 0), (x_total, 1, core_total, 1, dom_total)
        ).reshape(x_total * core_total, x_total, z_total, core_total)
        table = lax.dynamic_slice_in_dim(table, x_here, 1, 1)
        return lax.dynamic_slice_in_dim(table, core, 1, 3).reshape(-1)

    passed_cols = passed_tiles(tile_col)
    place = jnp.tile(jnp.arange(z_total), x_total * core_total)
    passed_first = ((x_here * z_total + place) * core_total + core) * group_blocks
    passed_first = passed_first + rep_here * blocks_here
    passed_block = jnp.where(passed_cols >= 0, passed_cols - passed_first, 0)
    passed_offset = place * blocks_here + passed_block
    passed_near = place_of(place, z_here) * blocks_here + passed_block

    def held_tiles(table):
        row = lax.dynamic_slice(table, (dom_here, rep_here, 0), (1, 1, dom_total))
        return row.reshape(x_total, z_total, core_total).swapaxes(1, 2).reshape(-1)

    held_rows = held_tiles(tile_row)
    held_there = held_rows >= 0
    held_block = jnp.where(held_there, held_rows, 0)
    held_cols = jnp.where(held_there, held_tiles(tile_col), 0)
    held_limits = jnp.where(held_there, held_tiles(tile_count), 0)
    held_offset = jnp.where(held_there, held_block - group_first, 0)
    row_ids, col_ids = id_blocks[held_block], id_blocks[held_cols]
    masks = edge_masks(row_ids, col_ids, held_limits, False)
    masks_swapped = edge_masks(row_ids, col_ids, held_limits, True)

    held_owner = held_offset // blocks_here
    held_near = place_of(held_owner, rep_here) * blocks_here + held_offset % blocks_here

    column_1, masks, masks_swapped = lax.optimization_barrier((column_1, masks, masks_swapped))
    leaving_1 = picked(passed_offset, column_1)
    leaving_1, second = lax.optimization_barrier((leaving_1, node_feats[:, half_in:]))
    arrived_1 = lax.all_to_all(leaving_1, ("x", "core"), 0, 0, tiled=True)
    column_2 = [x.reshape(-1, TILE, half_in) for x in gather_of_eight(second, "z")]
    leaving_2 = picked(passed_near, *column_2)
    arrived_1, leaving_2 = lax.optimization_barrier((arrived_1, leaving_2))
    arrived_2 = lax.all_to_all(leaving_2, ("x", "core"), 0, 0, tiled=True)
    sums_1 = tile_sums(held_near, masks, arrived_1, group_blocks)
    own_1, low_1, high_1 = sum_of_eight(sums_1.reshape(rep_total, rows_here, half_in), "rep")
    arrived_2, low_1, high_1 = lax.optimization_barrier((arrived_2, low_1, high_1))
    summed_1 = own_1 + low_1.astype(jnp.float32) + high_1.astype(jnp.float32)
    sums_2 = tile_sums(held_offset, masks, arrived_2, group_blocks)
    pieces = lax.all_to_all(
        sums_2.reshape(rep_total, rows_here, half_in), "rep", 0, 0, tiled=True
    )
    summed = jnp.concatenate([summed_1, pieces.astype(jnp.float32).sum(axis=0)], axis=1)

    own_first = group_first + rep_here * blocks_here
    group_rows = lax.dynamic_slice_in_dim(tile_row, dom_here, 1, 0).reshape(-1)
    group_limits = lax.dynamic_slice_in_dim(tile_count, dom_here, 1, 0).reshape(-1)
    owned_rows = group_rows[:, None] == own_first + jnp.arange(blocks_here)[None, :]
    degree = jnp.sum(jnp.where(owned_rows, group_limits[:, None], 0), axis=0).astype(jnp.float32)
    divisor = jnp.repeat(jnp.maximum(degree, 1.0), TILE)[:, None]
    mean_feats = (summed / divisor).astype(jnp.bfloat16)
    preact = jnp.dot(node_feats, self_weight, preferred_element_type=jnp.float32) + jnp.dot(
        mean_feats, neigh_weight, preferred_element_type=jnp.float32
    )
    hidden_out = jax.nn.silu(preact).astype(jnp.bfloat16)
    logistic = jax.nn.sigmoid(preact)
    pre_grad = (out_grad.astype(jnp.float32) * logistic * (1.0 + preact * (1.0 - logistic))).astype(
        jnp.bfloat16
    )
    over_rows = (((0,), (0,)), ((), ()))
    over_cols = (((1,), (1,)), ((), ()))
    mean_grad = lax.dot_general(
        pre_grad, neigh_weight, over_cols, preferred_element_type=jnp.float32
    )
    spread = (mean_grad / divisor).astype(jnp.bfloat16)
    spread = jnp.broadcast_to(spread[None], (rep_total, rows_here, width_in))
    spread, mean_feats, summing = lax.optimization_barrier((spread, mean_feats, pre_grad))
    group_spread = lax.all_to_all(spread, "rep", 0, 0, tiled=True)
    group_spread = group_spread.reshape(group_blocks, TILE, width_in)

    self_term = lax.dot_general(node_feats, summing, over_rows, preferred_element_type=jnp.float32)
    neigh_term = lax.dot_general(
        mean_feats, summing, over_rows, preferred_element_type=jnp.float32
    )
    first = core == 0
    share = jnp.where(first, self_term, neigh_term) + lax.ppermute(
        jnp.where(first, neigh_term, self_term), "core", [(0, 1), (1, 0)]
    )
    for axis, bit in (("x", 1), ("x", 2), ("z", 1)):
        share = halved(share, axis, bit)
    share = share + pair_swap(share, "z", 2)

    returning = tile_products(held_offset, masks_swapped, group_spread)
    returning, group_spread, share = lax.optimization_barrier((returning, group_spread, share))
    returned = lax.all_to_all(returning, ("x", "core"), 0, 0, tiled=True)
    for axis, bit in (("z", 4), ("rep", 1), ("rep", 2), ("rep", 4)):
        share = share + pair_swap(share, axis, bit)
    share = share * (1.0 / math.sqrt(rows_here * dom_total * rep_total))
    share = doubled(share, "z", 1)
    column_sums = summed_into(passed_offset, returned, z_total * blocks_here)
    column_sums, share = lax.optimization_barrier((column_sums, share))
    parts = lax.all_to_all(
        column_sums.reshape(z_total, rows_here, width_in), "z", 0, 0, tiled=True
    )
    for bit in (2, 1):
        share = doubled(share, "x", bit)
    other = lax.ppermute(share, "core", [(0, 1), (1, 0)])
    self_grad = jnp.where(first, share, other)
    neigh_grad = jnp.where(first, other, share)

    self_back = lax.dot_general(
        pre_grad, self_weight, over_cols, preferred_element_type=jnp.float32
    )
    transposed = parts.astype(jnp.float32).sum(axis=0)
    feat_grad = (self_back + transposed).astype(jnp.bfloat16)
    return (hidden_out, feat_grad, self_grad, neigh_grad)


def solution(mesh):
    torus = Mesh(mesh.devices.reshape(4, 8, 2, mesh.shape["rep"]), ALL)
    in_specs = (P(ALL, None), P(), P(), P(), P(), P(), P(), P(ALL, None))
    out_specs = (P(ALL, None), P(ALL, None), P(), P())
    return jax.shard_map(
        shards, mesh=torus, in_specs=in_specs, out_specs=out_specs, check_vma=False
    )
```

```python
import math

import jax
import jax.numpy as jnp
from jax import lax
from jax.experimental import pallas as pl
from jax.experimental.pallas import tpu as pltpu
from jax.sharding import Mesh
from jax.sharding import PartitionSpec as P

TILE = 128
DOM = ("x", "z", "core")
ALL = ("x", "z", "core", "rep")
STEP = 32


def edge_masks(row_ids, col_ids, limits, swapped):
    u = row_ids % 4093
    v = col_ids % 4091
    if swapped:
        u, v = u[:, None, :], v[:, :, None]
    else:
        u, v = u[:, :, None], v[:, None, :]
    hashed = (u * v + u + 3 * v) % 4099 % TILE
    return (hashed < limits[:, None, None]).astype(jnp.bfloat16)


def pair_swap(x, axis, bit):
    n = lax.axis_size(axis)
    return lax.ppermute(x, axis, [(i, i ^ bit) for i in range(n)])


def forward_kernel(offset_ref, mask_ref, feat_ref, out_ref, total_ref):
    step = pl.program_id(0)

    @pl.when(step == 0)
    def _():
        total_ref[...] = jnp.zeros_like(total_ref)

    products = [
        jnp.dot(mask_ref[t], feat_ref[t], preferred_element_type=jnp.float32) for t in range(STEP)
    ]
    for t in range(STEP):
        total_ref[offset_ref[step * STEP + t]] += products[t]

    @pl.when(step == pl.num_programs(0) - 1)
    def _():
        out_ref[...] = total_ref[...].astype(out_ref.dtype)


def tile_sums(offsets, masks, feats, blocks):
    slots, tile, width = feats.shape
    return pl.pallas_call(
        forward_kernel,
        grid_spec=pltpu.PrefetchScalarGridSpec(
            num_scalar_prefetch=1,
            grid=(slots // STEP,),
            in_specs=[
                pl.BlockSpec((STEP, tile, tile), lambda i, o: (i, 0, 0)),
                pl.BlockSpec((STEP, tile, width), lambda i, o: (i, 0, 0)),
            ],
            out_specs=pl.BlockSpec((blocks, tile, width), lambda i, o: (0, 0, 0)),
            scratch_shapes=[pltpu.VMEM((blocks, tile, width), jnp.float32)],
        ),
        out_shape=jax.ShapeDtypeStruct((blocks, tile, width), jnp.bfloat16),
        cost_estimate=pl.CostEstimate(
            flops=2 * slots * tile * tile * width,
            bytes_accessed=slots * tile * (tile + width) * 2,
            transcendentals=0,
        ),
        compiler_params=pltpu.CompilerParams(vmem_limit_bytes=40 << 20),
        name="tile_sums",
    )(offsets, masks, feats)


def products_kernel(offset_ref, mask_ref, *refs):
    *piece_refs, out_ref, held_ref = refs
    step = pl.program_id(0)

    @pl.when(step == 0)
    def _():
        first = 0
        for piece in piece_refs:
            held_ref[first : first + piece.shape[0]] = piece[...]
            first += piece.shape[0]

    for t in range(STEP):
        out_ref[t] = jnp.dot(
            mask_ref[t],
            held_ref[offset_ref[step * STEP + t]],
            preferred_element_type=jnp.float32,
        ).astype(out_ref.dtype)


def tile_products(offsets, masks, *pieces):
    slots, tile, _ = masks.shape
    n = sum(len(piece) for piece in pieces)
    width = pieces[0].shape[2]
    return pl.pallas_call(
        products_kernel,
        grid_spec=pltpu.PrefetchScalarGridSpec(
            num_scalar_prefetch=1,
            grid=(slots // STEP,),
            in_specs=[pl.BlockSpec((STEP, tile, tile), lambda i, o: (i, 0, 0))]
            + [pl.BlockSpec(piece.shape, lambda i, o: (0, 0, 0)) for piece in pieces],
            out_specs=pl.BlockSpec((STEP, tile, width), lambda i, o: (i, 0, 0)),
            scratch_shapes=[pltpu.VMEM((n, tile, width), pieces[0].dtype)],
        ),
        out_shape=jax.ShapeDtypeStruct((slots, tile, width), jnp.bfloat16),
        cost_estimate=pl.CostEstimate(
            flops=2 * slots * tile * tile * width,
            bytes_accessed=slots * tile * (tile + width) * 2,
            transcendentals=0,
        ),
        compiler_params=pltpu.CompilerParams(vmem_limit_bytes=60 << 20),
        name="tile_products",
    )(offsets, masks, *pieces)


def gathered_kernel(offset_ref, part_ref, *refs):
    *beside_ref, out_ref, total_ref = refs
    step = pl.program_id(0)

    @pl.when(step == 0)
    def _():
        total_ref[...] = jnp.zeros_like(total_ref)

    for t in range(STEP):
        total_ref[offset_ref[step * STEP + t]] += part_ref[t].astype(jnp.float32)

    @pl.when(step == pl.num_programs(0) - 1)
    def _():
        width = total_ref.shape[2]
        if beside_ref:
            out_ref[:, :, :width] = beside_ref[0][...]
        out_ref[:, :, -width:] = total_ref[...].astype(out_ref.dtype)


def summed_into(offsets, parts, blocks, *beside):
    slots, tile, width = parts.shape
    out = (blocks, tile, width * (1 + len(beside)))
    return pl.pallas_call(
        gathered_kernel,
        grid_spec=pltpu.PrefetchScalarGridSpec(
            num_scalar_prefetch=1,
            grid=(slots // STEP,),
            in_specs=[pl.BlockSpec((STEP, tile, width), lambda i, o: (i, 0, 0))]
            + [pl.BlockSpec(x.shape, lambda i, o: (0, 0, 0)) for x in beside],
            out_specs=pl.BlockSpec(out, lambda i, o: (0, 0, 0)),
            scratch_shapes=[pltpu.VMEM((blocks, tile, width), jnp.float32)],
        ),
        out_shape=jax.ShapeDtypeStruct(out, jnp.bfloat16),
        cost_estimate=pl.CostEstimate(
            flops=slots * tile * width, bytes_accessed=slots * tile * width * 2, transcendentals=0
        ),
        compiler_params=pltpu.CompilerParams(vmem_limit_bytes=40 << 20),
        name="summed_into",
    )(offsets, parts, *beside)


def pick_kernel(offset_ref, *refs):
    *piece_refs, out_ref, held_ref, in_sems, out_sems = refs
    first = 0
    copies = []
    for piece in piece_refs:
        count = piece.shape[0]
        copies.append(
            pltpu.make_async_copy(
                piece, held_ref.at[pl.ds(first, count)], in_sems.at[len(copies)]
            )
        )
        first += count
    for copy in copies:
        copy.start()
    for copy in copies:
        copy.wait()
    copies = [
        pltpu.make_async_copy(held_ref.at[offset_ref[t]], out_ref.at[t], out_sems.at[t])
        for t in range(out_ref.shape[0])
    ]
    for copy in copies:
        copy.start()
    for copy in copies:
        copy.wait()


def picked(offsets, *pieces):
    slots = offsets.shape[0]
    n = sum(len(piece) for piece in pieces)
    _, tile, width = pieces[0].shape
    dtype = pieces[0].dtype
    return pl.pallas_call(
        pick_kernel,
        in_specs=[pl.BlockSpec(memory_space=pltpu.SMEM)]
        + [pl.BlockSpec(memory_space=pl.ANY)] * len(pieces),
        out_specs=pl.BlockSpec(memory_space=pl.ANY),
        scratch_shapes=[
            pltpu.VMEM((n, tile, width), dtype),
            pltpu.SemaphoreType.DMA((len(pieces),)),
            pltpu.SemaphoreType.DMA((slots,)),
        ],
        out_shape=jax.ShapeDtypeStruct((slots, tile, width), dtype),
        cost_estimate=pl.CostEstimate(
            flops=0, bytes_accessed=(n + slots) * tile * width * 2, transcendentals=0
        ),
        name="picked",
    )(offsets, *pieces)


def shifted(x, axis, by):
    n = lax.axis_size(axis)
    return lax.ppermute(x, axis, [(i, (i + by) % n) for i in range(n)])


DISTANCES = (-3, 0, 3, -4, -1, 2, -2, 1)


def place_of(device, here):
    far = (device - here + 4) % 8 - 4
    return sum(jnp.where(far == d, i, 0) for i, d in enumerate(DISTANCES))


def gather_of_eight(x, axis):
    near = jnp.stack([shifted(x, axis, 3), x, shifted(x, axis, -3)])
    return near, shifted(near, axis, 1), shifted(near[:2], axis, -1)


def sum_of_eight(x, axis):
    above = shifted(x[3:6], axis, -1).astype(jnp.float32)
    below = shifted(x[6:8], axis, 1).astype(jnp.float32)
    low = x[0].astype(jnp.float32) + above[0] + below[0]
    own = x[1].astype(jnp.float32) + above[1] + below[1]
    high = x[2].astype(jnp.float32) + above[2]
    return own, shifted(low.astype(x.dtype), axis, -3), shifted(high.astype(x.dtype), axis, 3)


def halved(x, axis, bit):
    half = x.shape[0] // 2
    low = (lax.axis_index(axis) & bit) == 0
    other = pair_swap(jnp.where(low, x[half:], x[:half]), axis, bit)
    return jnp.where(low, x[:half], x[half:]) + other


def doubled(x, axis, bit):
    low = (lax.axis_index(axis) & bit) == 0
    other = pair_swap(x, axis, bit)
    return jnp.where(low, jnp.concatenate([x, other]), jnp.concatenate([other, x]))


def shards(
    node_feats, node_ids, tile_row, tile_col, tile_count, self_weight, neigh_weight, out_grad
):
    dom_total = lax.axis_size(DOM)
    rep_total = lax.axis_size("rep")
    x_total, z_total, core_total = (lax.axis_size(a) for a in DOM)
    dom_here = lax.axis_index(DOM)
    rep_here = lax.axis_index("rep")
    x_here, z_here, core = (lax.axis_index(a) for a in DOM)
    rows_here, width_in = node_feats.shape
    blocks_here = rows_here // TILE
    group_blocks = blocks_here * rep_total
    id_blocks = node_ids.reshape(-1, TILE)
    group_first = dom_here * group_blocks
    half_in = width_in // 2

    column_1 = lax.all_to_all(
        jnp.broadcast_to(node_feats[None, :, :half_in], (z_total, rows_here, half_in)),
        "z",
        0,
        0,
        tiled=True,
    ).reshape(z_total * blocks_here, TILE, half_in)

    def passed_tiles(table):
        table = table.reshape(x_total, z_total, core_total, rep_total, dom_total)
        table = lax.dynamic_slice(
            table, (0, z_here, 0, rep_here, 0), (x_total, 1, core_total, 1, dom_total)
        ).reshape(x_total * core_total, x_total, z_total, core_total)
        table = lax.dynamic_slice_in_dim(table, x_here, 1, 1)
        return lax.dynamic_slice_in_dim(table, core, 1, 3).reshape(-1)

    passed_cols = passed_tiles(tile_col)
    place = jnp.tile(jnp.arange(z_total), x_total * core_total)
    passed_first = ((x_here * z_total + place) * core_total + core) * group_blocks
    passed_first = passed_first + rep_here * blocks_here
    passed_block = jnp.where(passed_cols >= 0, passed_cols - passed_first, 0)
    passed_offset = place * blocks_here + passed_block
    passed_near = place_of(place, z_here) * blocks_here + passed_block

    def held_tiles(table):
        row = lax.dynamic_slice(table, (dom_here, rep_here, 0), (1, 1, dom_total))
        return row.reshape(x_total, z_total, core_total).swapaxes(1, 2).reshape(-1)

    held_rows = held_tiles(tile_row)
    held_there = held_rows >= 0
    held_block = jnp.where(held_there, held_rows, 0)
    held_cols = jnp.where(held_there, held_tiles(tile_col), 0)
    held_limits = jnp.where(held_there, held_tiles(tile_count), 0)
    held_offset = jnp.where(held_there, held_block - group_first, 0)
    row_ids, col_ids = id_blocks[held_block], id_blocks[held_cols]
    masks = edge_masks(row_ids, col_ids, held_limits, False)
    masks_swapped = edge_masks(row_ids, col_ids, held_limits, True)

    held_owner = held_offset // blocks_here
    held_near = place_of(held_owner, rep_here) * blocks_here + held_offset % blocks_here

    column_1, masks, masks_swapped = lax.optimization_barrier((column_1, masks, masks_swapped))
    leaving_1 = picked(passed_offset, column_1)
    leaving_1, second = lax.optimization_barrier((leaving_1, node_feats[:, half_in:]))
    arrived_1 = lax.all_to_all(leaving_1, ("x", "core"), 0, 0, tiled=True)
    column_2 = [x.reshape(-1, TILE, half_in) for x in gather_of_eight(second, "z")]
    leaving_2 = picked(passed_near, *column_2)
    arrived_1, leaving_2 = lax.optimization_barrier((arrived_1, leaving_2))
    arrived_2 = lax.all_to_all(leaving_2, ("x", "core"), 0, 0, tiled=True)
    sums_1 = tile_sums(held_near, masks, arrived_1, group_blocks)
    own_1, low_1, high_1 = sum_of_eight(sums_1.reshape(rep_total, rows_here, half_in), "rep")
    arrived_2, low_1 = lax.optimization_barrier((arrived_2, low_1))
    sums_2 = tile_sums(held_offset, masks, arrived_2, group_blocks)
    sums_2, high_1 = lax.optimization_barrier((sums_2, high_1))
    pieces = lax.all_to_all(
        sums_2.reshape(rep_total, rows_here, half_in), "rep", 0, 0, tiled=True
    )
    summed_1 = own_1 + low_1.astype(jnp.float32) + high_1.astype(jnp.float32)
    summed = jnp.concatenate([summed_1, pieces.astype(jnp.float32).sum(axis=0)], axis=1)

    own_first = group_first + rep_here * blocks_here
    group_rows = lax.dynamic_slice_in_dim(tile_row, dom_here, 1, 0).reshape(-1)
    group_limits = lax.dynamic_slice_in_dim(tile_count, dom_here, 1, 0).reshape(-1)
    owned_rows = group_rows[:, None] == own_first + jnp.arange(blocks_here)[None, :]
    degree = jnp.sum(jnp.where(owned_rows, group_limits[:, None], 0), axis=0).astype(jnp.float32)
    divisor = jnp.repeat(jnp.maximum(degree, 1.0), TILE)[:, None]
    mean_feats = (summed / divisor).astype(jnp.bfloat16)
    preact = jnp.dot(node_feats, self_weight, preferred_element_type=jnp.float32) + jnp.dot(
        mean_feats, neigh_weight, preferred_element_type=jnp.float32
    )
    hidden_out = jax.nn.silu(preact).astype(jnp.bfloat16)
    logistic = jax.nn.sigmoid(preact)
    pre_grad = (out_grad.astype(jnp.float32) * logistic * (1.0 + preact * (1.0 - logistic))).astype(
        jnp.bfloat16
    )
    over_rows = (((0,), (0,)), ((), ()))
    over_cols = (((1,), (1,)), ((), ()))
    mean_grad = lax.dot_general(
        pre_grad, neigh_weight, over_cols, preferred_element_type=jnp.float32
    )
    spread = (mean_grad / divisor).astype(jnp.bfloat16)
    spread_1 = jnp.broadcast_to(spread[None, :, :half_in], (rep_total, rows_here, half_in))
    spread_1, spread_2, mean_feats, summing = lax.optimization_barrier(
        (spread_1, spread[:, half_in:], mean_feats, pre_grad)
    )
    group_1 = lax.all_to_all(spread_1, "rep", 0, 0, tiled=True)
    group_1 = group_1.reshape(group_blocks, TILE, half_in)

    self_term = lax.dot_general(node_feats, summing, over_rows, preferred_element_type=jnp.float32)
    neigh_term = lax.dot_general(
        mean_feats, summing, over_rows, preferred_element_type=jnp.float32
    )
    first = core == 0
    share = jnp.where(first, self_term, neigh_term) + lax.ppermute(
        jnp.where(first, neigh_term, self_term), "core", [(0, 1), (1, 0)]
    )
    for bit in (1, 2):
        share = halved(share, "x", bit)

    returning_1 = tile_products(held_offset, masks_swapped, group_1)
    returning_1, spread_2, share = lax.optimization_barrier((returning_1, spread_2, share))
    returned_1 = lax.all_to_all(returning_1, ("x", "core"), 0, 0, tiled=True)
    group_2 = [x.reshape(-1, TILE, half_in) for x in gather_of_eight(spread_2, "rep")]
    share = halved(share, "z", 1)
    returning_2 = tile_products(held_near, masks_swapped, *group_2)

    returned_1, returning_2, share = lax.optimization_barrier((returned_1, returning_2, share))
    returned_2 = lax.all_to_all(returning_2, ("x", "core"), 0, 0, tiled=True)
    column_1 = summed_into(passed_offset, returned_1, z_total * blocks_here)
    for axis, bit in (("z", 2), ("z", 4), ("rep", 1)):
        share = share + pair_swap(share, axis, bit)
    share = doubled(share, "z", 1)
    column_sums = summed_into(passed_offset, returned_2, z_total * blocks_here, column_1)

    column_sums, share = lax.optimization_barrier((column_sums, share))
    parts = lax.all_to_all(
        column_sums.reshape(z_total, rows_here, width_in), "z", 0, 0, tiled=True
    )
    for bit in (2, 4):
        share = share + pair_swap(share, "rep", bit)
    share = share * (1.0 / math.sqrt(rows_here * dom_total * rep_total))
    for bit in (2, 1):
        share = doubled(share, "x", bit)
    other = lax.ppermute(share, "core", [(0, 1), (1, 0)])
    self_grad = jnp.where(first, share, other)
    neigh_grad = jnp.where(first, other, share)

    self_back = lax.dot_general(
        pre_grad, self_weight, over_cols, preferred_element_type=jnp.float32
    )
    transposed = parts.astype(jnp.float32).sum(axis=0)
    feat_grad = (self_back + transposed).astype(jnp.bfloat16)
    return (hidden_out, feat_grad, self_grad, neigh_grad)


def solution(mesh):
    torus = Mesh(mesh.devices.reshape(4, 8, 2, mesh.shape["rep"]), ALL)
    in_specs = (P(ALL, None), P(), P(), P(), P(), P(), P(), P(ALL, None))
    out_specs = (P(ALL, None), P(ALL, None), P(), P())
    return jax.shard_map(
        shards, mesh=torus, in_specs=in_specs, out_specs=out_specs, check_vma=False
    )
```

```python
import math

import jax
import jax.numpy as jnp
from jax import lax
from jax.experimental import pallas as pl
from jax.experimental.pallas import tpu as pltpu
from jax.sharding import Mesh
from jax.sharding import PartitionSpec as P

TILE = 128
DOM = ("x", "z", "core")
ALL = ("x", "z", "core", "rep")
STEP = 32


def edge_masks(row_ids, col_ids, limits, swapped):
    u = row_ids % 4093
    v = col_ids % 4091
    if swapped:
        u, v = u[:, None, :], v[:, :, None]
    else:
        u, v = u[:, :, None], v[:, None, :]
    hashed = (u * v + u + 3 * v) % 4099 % TILE
    return (hashed < limits[:, None, None]).astype(jnp.bfloat16)


def pair_swap(x, axis, bit):
    n = lax.axis_size(axis)
    return lax.ppermute(x, axis, [(i, i ^ bit) for i in range(n)])


def forward_kernel(offset_ref, mask_ref, feat_ref, out_ref, total_ref):
    step = pl.program_id(0)

    @pl.when(step == 0)
    def _():
        total_ref[...] = jnp.zeros_like(total_ref)

    products = [
        jnp.dot(mask_ref[t], feat_ref[t], preferred_element_type=jnp.float32) for t in range(STEP)
    ]
    for t in range(STEP):
        total_ref[offset_ref[step * STEP + t]] += products[t]

    @pl.when(step == pl.num_programs(0) - 1)
    def _():
        out_ref[...] = total_ref[...].astype(out_ref.dtype)


def tile_sums(offsets, masks, feats, blocks):
    slots, tile, width = feats.shape
    return pl.pallas_call(
        forward_kernel,
        grid_spec=pltpu.PrefetchScalarGridSpec(
            num_scalar_prefetch=1,
            grid=(slots // STEP,),
            in_specs=[
                pl.BlockSpec((STEP, tile, tile), lambda i, o: (i, 0, 0)),
                pl.BlockSpec((STEP, tile, width), lambda i, o: (i, 0, 0)),
            ],
            out_specs=pl.BlockSpec((blocks, tile, width), lambda i, o: (0, 0, 0)),
            scratch_shapes=[pltpu.VMEM((blocks, tile, width), jnp.float32)],
        ),
        out_shape=jax.ShapeDtypeStruct((blocks, tile, width), jnp.bfloat16),
        cost_estimate=pl.CostEstimate(
            flops=2 * slots * tile * tile * width,
            bytes_accessed=slots * tile * (tile + width) * 2,
            transcendentals=0,
        ),
        compiler_params=pltpu.CompilerParams(vmem_limit_bytes=40 << 20),
        name="tile_sums",
    )(offsets, masks, feats)


def products_kernel(offset_ref, mask_ref, block_ref, out_ref):
    first = pl.program_id(0) * len(mask_ref)
    for t in range(len(mask_ref)):
        out_ref[t] = jnp.dot(
            mask_ref[t],
            block_ref[offset_ref[first + t]],
            preferred_element_type=jnp.float32,
        ).astype(out_ref.dtype)


def tile_products(offsets, masks, blocks, step):
    slots, tile, _ = masks.shape
    n, _, width = blocks.shape
    return pl.pallas_call(
        products_kernel,
        grid_spec=pltpu.PrefetchScalarGridSpec(
            num_scalar_prefetch=1,
            grid=(slots // step,),
            in_specs=[
                pl.BlockSpec((step, tile, tile), lambda i, o: (i, 0, 0)),
                pl.BlockSpec((n, tile, width), lambda i, o: (0, 0, 0)),
            ],
            out_specs=pl.BlockSpec((step, tile, width), lambda i, o: (i, 0, 0)),
        ),
        out_shape=jax.ShapeDtypeStruct((slots, tile, width), jnp.bfloat16),
        cost_estimate=pl.CostEstimate(
            flops=2 * slots * tile * tile * width,
            bytes_accessed=slots * tile * (tile + width) * 2,
            transcendentals=0,
        ),
        compiler_params=pltpu.CompilerParams(vmem_limit_bytes=60 << 20),
        name="tile_products",
    )(offsets, masks, blocks)


def gathered_kernel(offset_ref, part_ref, out_ref, total_ref):
    step = pl.program_id(0)

    @pl.when(step == 0)
    def _():
        total_ref[...] = jnp.zeros_like(total_ref)

    for t in range(len(part_ref)):
        total_ref[offset_ref[step * len(part_ref) + t]] += part_ref[t].astype(jnp.float32)

    @pl.when(step == pl.num_programs(0) - 1)
    def _():
        out_ref[...] = total_ref[...].astype(out_ref.dtype)


def summed_into(offsets, parts, blocks, step, dtype):
    slots, tile, width = parts.shape
    return pl.pallas_call(
        gathered_kernel,
        grid_spec=pltpu.PrefetchScalarGridSpec(
            num_scalar_prefetch=1,
            grid=(slots // step,),
            in_specs=[pl.BlockSpec((step, tile, width), lambda i, o: (i, 0, 0))],
            out_specs=pl.BlockSpec((blocks, tile, width), lambda i, o: (0, 0, 0)),
            scratch_shapes=[pltpu.VMEM((blocks, tile, width), jnp.float32)],
        ),
        out_shape=jax.ShapeDtypeStruct((blocks, tile, width), dtype),
        cost_estimate=pl.CostEstimate(
            flops=slots * tile * width, bytes_accessed=slots * tile * width * 2, transcendentals=0
        ),
        compiler_params=pltpu.CompilerParams(vmem_limit_bytes=40 << 20),
        name="summed_into",
    )(offsets, parts)


def pick_kernel(offset_ref, *refs):
    *piece_refs, out_ref, held_ref, in_sems, out_sems = refs
    first = 0
    copies = []
    for piece in piece_refs:
        count = piece.shape[0]
        copies.append(
            pltpu.make_async_copy(
                piece, held_ref.at[pl.ds(first, count)], in_sems.at[len(copies)]
            )
        )
        first += count
    for copy in copies:
        copy.start()
    for copy in copies:
        copy.wait()
    copies = [
        pltpu.make_async_copy(held_ref.at[offset_ref[t]], out_ref.at[t], out_sems.at[t])
        for t in range(out_ref.shape[0])
    ]
    for copy in copies:
        copy.start()
    for copy in copies:
        copy.wait()


def picked(offsets, *pieces):
    slots = offsets.shape[0]
    n = sum(len(piece) for piece in pieces)
    _, tile, width = pieces[0].shape
    dtype = pieces[0].dtype
    return pl.pallas_call(
        pick_kernel,
        in_specs=[pl.BlockSpec(memory_space=pltpu.SMEM)]
        + [pl.BlockSpec(memory_space=pl.ANY)] * len(pieces),
        out_specs=pl.BlockSpec(memory_space=pl.ANY),
        scratch_shapes=[
            pltpu.VMEM((n, tile, width), dtype),
            pltpu.SemaphoreType.DMA((len(pieces),)),
            pltpu.SemaphoreType.DMA((slots,)),
        ],
        out_shape=jax.ShapeDtypeStruct((slots, tile, width), dtype),
        cost_estimate=pl.CostEstimate(
            flops=0, bytes_accessed=(n + slots) * tile * width * 2, transcendentals=0
        ),
        name="picked",
    )(offsets, *pieces)


def shifted(x, axis, by):
    n = lax.axis_size(axis)
    return lax.ppermute(x, axis, [(i, (i + by) % n) for i in range(n)])


DISTANCES = (-3, 0, 3, -4, -1, 2, -2, 1)


def place_of(device, here):
    far = (device - here + 4) % 8 - 4
    return sum(jnp.where(far == d, i, 0) for i, d in enumerate(DISTANCES))


def gather_of_eight(x, axis):
    near = jnp.stack([shifted(x, axis, 3), x, shifted(x, axis, -3)])
    return near, shifted(near, axis, 1), shifted(near[:2], axis, -1)


def sum_of_eight(x, axis):
    above = shifted(x[3:6], axis, -1).astype(jnp.float32)
    below = shifted(x[6:8], axis, 1).astype(jnp.float32)
    low = x[0].astype(jnp.float32) + above[0] + below[0]
    own = x[1].astype(jnp.float32) + above[1] + below[1]
    high = x[2].astype(jnp.float32) + above[2]
    return own, shifted(low.astype(x.dtype), axis, -3), shifted(high.astype(x.dtype), axis, 3)


def halved(x, axis, bit):
    half = x.shape[0] // 2
    low = (lax.axis_index(axis) & bit) == 0
    other = pair_swap(jnp.where(low, x[half:], x[:half]), axis, bit)
    return jnp.where(low, x[:half], x[half:]) + other


def doubled(x, axis, bit):
    low = (lax.axis_index(axis) & bit) == 0
    other = pair_swap(x, axis, bit)
    return jnp.where(low, jnp.concatenate([x, other]), jnp.concatenate([other, x]))


def shards(
    node_feats, node_ids, tile_row, tile_col, tile_count, self_weight, neigh_weight, out_grad
):
    dom_total = lax.axis_size(DOM)
    rep_total = lax.axis_size("rep")
    x_total, z_total, core_total = (lax.axis_size(a) for a in DOM)
    dom_here = lax.axis_index(DOM)
    rep_here = lax.axis_index("rep")
    x_here, z_here, core = (lax.axis_index(a) for a in DOM)
    rows_here, width_in = node_feats.shape
    blocks_here = rows_here // TILE
    group_blocks = blocks_here * rep_total
    id_blocks = node_ids.reshape(-1, TILE)
    group_first = dom_here * group_blocks
    half_in = width_in // 2

    column_1 = lax.all_to_all(
        jnp.broadcast_to(node_feats[None, :, :half_in], (z_total, rows_here, half_in)),
        "z",
        0,
        0,
        tiled=True,
    ).reshape(z_total * blocks_here, TILE, half_in)

    groups = x_total * core_total

    def by_distance(table):
        table = lax.dynamic_slice_in_dim(jnp.concatenate([table, table], axis=1), z_here, z_total, 1)
        table = jnp.stack([table[:, d % z_total] for d in DISTANCES], axis=2)
        return table.reshape(groups, z_total)

    table = tile_col.reshape(x_total, z_total, core_total, rep_total, dom_total)
    table = lax.dynamic_slice(
        table, (0, z_here, 0, rep_here, 0), (x_total, 1, core_total, 1, dom_total)
    ).reshape(groups, x_total, z_total, core_total)
    table = lax.dynamic_slice_in_dim(table, x_here, 1, 1)
    table = lax.dynamic_slice_in_dim(table, core, 1, 3).reshape(groups, z_total)
    table = lax.dynamic_slice_in_dim(jnp.concatenate([table, table], axis=1), z_here, z_total, 1)
    passed_cols = jnp.stack([table[:, d % z_total] for d in DISTANCES], axis=1)
    place = (z_here + jnp.array(DISTANCES)[None, :]) % z_total
    passed_first = ((x_here * z_total + place) * core_total + core) * group_blocks
    passed_first = passed_first + rep_here * blocks_here
    passed_block = jnp.where(passed_cols >= 0, passed_cols - passed_first, 0)
    passed_offset = (place * blocks_here + passed_block).reshape(-1)
    near = jnp.arange(z_total)[None, :] * blocks_here
    passed_near = (near + passed_block).reshape(-1)

    def held_tiles(table):
        row = lax.dynamic_slice(table, (dom_here, rep_here, 0), (1, 1, dom_total))
        return by_distance(row.reshape(x_total, z_total, core_total))

    held_rows = held_tiles(tile_row)
    held_there = held_rows >= 0
    held_block = jnp.where(held_there, held_rows, 0)
    held_cols = jnp.where(held_there, held_tiles(tile_col), 0)
    held_limits = jnp.where(held_there, held_tiles(tile_count), 0)
    held_place = jnp.where(held_there, held_block - group_first, 0)
    row_ids, col_ids = id_blocks[held_block.reshape(-1)], id_blocks[held_cols.reshape(-1)]
    masks = edge_masks(row_ids, col_ids, held_limits.reshape(-1), False)
    held_offset = held_place.reshape(-1)

    def masks_of(part):
        ids = [x.reshape(groups, z_total, TILE)[:, part].reshape(-1, TILE) for x in (row_ids, col_ids)]
        return edge_masks(*ids, held_limits[:, part].reshape(-1), True)

    one, three = slice(3, None), slice(0, 3)
    masks_one, masks_three = masks_of(one), masks_of(three)
    place_one, place_three = (held_place[:, part].reshape(-1) for part in (one, three))
    back_one = (near[:, three.stop :] - three.stop * blocks_here + passed_block[:, one]).reshape(-1)
    back_three = (near[:, three] + passed_block[:, three]).reshape(-1)
    held_owner = held_offset // blocks_here
    held_near = place_of(held_owner, rep_here) * blocks_here + held_offset % blocks_here

    column_1, masks, masks_one, masks_three = lax.optimization_barrier(
        (column_1, masks, masks_one, masks_three)
    )
    leaving_1 = picked(passed_offset, column_1)
    leaving_1, second = lax.optimization_barrier((leaving_1, node_feats[:, half_in:]))
    arrived_1 = lax.all_to_all(leaving_1, ("x", "core"), 0, 0, tiled=True)
    column_2 = [x.reshape(-1, TILE, half_in) for x in gather_of_eight(second, "z")]
    leaving_2 = picked(passed_near, *column_2)
    arrived_1, leaving_2 = lax.optimization_barrier((arrived_1, leaving_2))
    arrived_2 = lax.all_to_all(leaving_2, ("x", "core"), 0, 0, tiled=True)
    sums_1 = tile_sums(held_near, masks, arrived_1, group_blocks)
    own_1, low_1, high_1 = sum_of_eight(sums_1.reshape(rep_total, rows_here, half_in), "rep")
    arrived_2, low_1 = lax.optimization_barrier((arrived_2, low_1))
    sums_2 = tile_sums(held_offset, masks, arrived_2, group_blocks)
    sums_2, high_1 = lax.optimization_barrier((sums_2, high_1))
    pieces = lax.all_to_all(
        sums_2.reshape(rep_total, rows_here, half_in), "rep", 0, 0, tiled=True
    )
    summed_1 = own_1 + low_1.astype(jnp.float32) + high_1.astype(jnp.float32)
    summed = jnp.concatenate([summed_1, pieces.astype(jnp.float32).sum(axis=0)], axis=1)

    own_first = group_first + rep_here * blocks_here
    group_rows = lax.dynamic_slice_in_dim(tile_row, dom_here, 1, 0).reshape(-1)
    group_limits = lax.dynamic_slice_in_dim(tile_count, dom_here, 1, 0).reshape(-1)
    owned_rows = group_rows[:, None] == own_first + jnp.arange(blocks_here)[None, :]
    degree = jnp.sum(jnp.where(owned_rows, group_limits[:, None], 0), axis=0).astype(jnp.float32)
    divisor = jnp.repeat(jnp.maximum(degree, 1.0), TILE)[:, None]
    mean_feats = (summed / divisor).astype(jnp.bfloat16)
    preact = jnp.dot(node_feats, self_weight, preferred_element_type=jnp.float32) + jnp.dot(
        mean_feats, neigh_weight, preferred_element_type=jnp.float32
    )
    hidden_out = jax.nn.silu(preact).astype(jnp.bfloat16)
    logistic = jax.nn.sigmoid(preact)
    pre_grad = (out_grad.astype(jnp.float32) * logistic * (1.0 + preact * (1.0 - logistic))).astype(
        jnp.bfloat16
    )
    over_rows = (((0,), (0,)), ((), ()))
    over_cols = (((1,), (1,)), ((), ()))
    mean_grad = lax.dot_general(
        pre_grad, neigh_weight, over_cols, preferred_element_type=jnp.float32
    )
    spread = (mean_grad / divisor).astype(jnp.bfloat16)
    spread = jnp.broadcast_to(spread[None], (rep_total, rows_here, width_in))
    spread, mean_feats, summing = lax.optimization_barrier((spread, mean_feats, pre_grad))
    group_spread = lax.all_to_all(spread, "rep", 0, 0, tiled=True)
    group_spread = group_spread.reshape(group_blocks, TILE, width_in)

    self_term = lax.dot_general(node_feats, summing, over_rows, preferred_element_type=jnp.float32)
    neigh_term = lax.dot_general(
        mean_feats, summing, over_rows, preferred_element_type=jnp.float32
    )
    first = core == 0
    share = jnp.where(first, self_term, neigh_term) + lax.ppermute(
        jnp.where(first, neigh_term, self_term), "core", [(0, 1), (1, 0)]
    )
    for axis, bit in (("x", 1), ("x", 2), ("z", 1)):
        share = halved(share, axis, bit)
    share = share + pair_swap(share, "z", 2)

    returning_1 = tile_products(place_one, masks_one, group_spread, 20)
    returning_1, group_spread, share = lax.optimization_barrier((returning_1, group_spread, share))
    returned_1 = lax.all_to_all(returning_1, ("x", "core"), 0, 0, tiled=True)
    returning_2 = tile_products(place_three, masks_three, group_spread, 24)
    for axis, bit in (("z", 4), ("rep", 1), ("rep", 2), ("rep", 4)):
        share = share + pair_swap(share, axis, bit)
    share = share * (1.0 / math.sqrt(rows_here * dom_total * rep_total))
    share = doubled(share, "z", 1)

    returned_1, returning_2, share = lax.optimization_barrier((returned_1, returning_2, share))
    returned_2 = lax.all_to_all(returning_2, ("x", "core"), 0, 0, tiled=True)
    column = summed_into(back_one, returned_1, 5 * blocks_here, 20, jnp.bfloat16)
    column = column.reshape(5, rows_here, width_in)
    above, below = shifted(column[:3], "z", -1), shifted(column[3:], "z", 1)
    returned_2, above, below, share = lax.optimization_barrier((returned_2, above, below, share))
    column = summed_into(back_three, returned_2, 3 * blocks_here, 24, jnp.float32)
    column = column.reshape(3, rows_here, width_in)

    low = column[0] + above[0].astype(jnp.float32) + below[0].astype(jnp.float32)
    high = column[2] + above[2].astype(jnp.float32)
    low, high, share = lax.optimization_barrier(
        (low.astype(jnp.bfloat16), high.astype(jnp.bfloat16), share)
    )
    low, high = shifted(low, "z", -3), shifted(high, "z", 3)
    for bit in (2, 1):
        share = doubled(share, "x", bit)
    share, low, high = lax.optimization_barrier((share, low, high))
    other = lax.ppermute(share, "core", [(0, 1), (1, 0)])
    self_grad = jnp.where(first, share, other)
    neigh_grad = jnp.where(first, other, share)

    self_back = lax.dot_general(
        pre_grad, self_weight, over_cols, preferred_element_type=jnp.float32
    )
    transposed = column[1] + above[1].astype(jnp.float32) + below[1].astype(jnp.float32)
    transposed = transposed + low.astype(jnp.float32) + high.astype(jnp.float32)
    feat_grad = (self_back + transposed).astype(jnp.bfloat16)
    return (hidden_out, feat_grad, self_grad, neigh_grad)


def solution(mesh):
    torus = Mesh(mesh.devices.reshape(4, 8, 2, mesh.shape["rep"]), ALL)
    in_specs = (P(ALL, None), P(), P(), P(), P(), P(), P(), P(ALL, None))
    out_specs = (P(ALL, None), P(ALL, None), P(), P())
    return jax.shard_map(
        shards, mesh=torus, in_specs=in_specs, out_specs=out_specs, check_vma=False
    )
```

```python
import math

import jax
import jax.numpy as jnp
from jax import lax
from jax.experimental import pallas as pl
from jax.experimental.pallas import tpu as pltpu
from jax.sharding import Mesh
from jax.sharding import PartitionSpec as P

TILE = 128
DOM = ("x", "z", "core")
ALL = ("x", "z", "core", "rep")
STEP = 32


def edge_masks(row_ids, col_ids, limits, swapped):
    u = row_ids % 4093
    v = col_ids % 4091
    if swapped:
        u, v = u[:, None, :], v[:, :, None]
    else:
        u, v = u[:, :, None], v[:, None, :]
    hashed = (u * v + u + 3 * v) % 4099 % TILE
    return (hashed < limits[:, None, None]).astype(jnp.bfloat16)


def pair_swap(x, axis, bit):
    n = lax.axis_size(axis)
    return lax.ppermute(x, axis, [(i, i ^ bit) for i in range(n)])


def forward_kernel(offset_ref, mask_ref, feat_ref, out_ref, total_ref):
    step = pl.program_id(0)

    @pl.when(step == 0)
    def _():
        total_ref[...] = jnp.zeros_like(total_ref)

    products = [
        jnp.dot(mask_ref[t], feat_ref[t], preferred_element_type=jnp.float32) for t in range(STEP)
    ]
    for t in range(STEP):
        total_ref[offset_ref[step * STEP + t]] += products[t]

    @pl.when(step == pl.num_programs(0) - 1)
    def _():
        out_ref[...] = total_ref[...].astype(out_ref.dtype)


def tile_sums(offsets, masks, feats, blocks):
    slots, tile, width = feats.shape
    return pl.pallas_call(
        forward_kernel,
        grid_spec=pltpu.PrefetchScalarGridSpec(
            num_scalar_prefetch=1,
            grid=(slots // STEP,),
            in_specs=[
                pl.BlockSpec((STEP, tile, tile), lambda i, o: (i, 0, 0)),
                pl.BlockSpec((STEP, tile, width), lambda i, o: (i, 0, 0)),
            ],
            out_specs=pl.BlockSpec((blocks, tile, width), lambda i, o: (0, 0, 0)),
            scratch_shapes=[pltpu.VMEM((blocks, tile, width), jnp.float32)],
        ),
        out_shape=jax.ShapeDtypeStruct((blocks, tile, width), jnp.bfloat16),
        cost_estimate=pl.CostEstimate(
            flops=2 * slots * tile * tile * width,
            bytes_accessed=slots * tile * (tile + width) * 2,
            transcendentals=0,
        ),
        compiler_params=pltpu.CompilerParams(vmem_limit_bytes=40 << 20),
        name="tile_sums",
    )(offsets, masks, feats)


def products_kernel(offset_ref, mask_ref, block_ref, out_ref):
    step = pl.program_id(0)
    for t in range(STEP):
        out_ref[t] = jnp.dot(
            mask_ref[t],
            block_ref[offset_ref[step * STEP + t]],
            preferred_element_type=jnp.float32,
        ).astype(out_ref.dtype)


def tile_products(offsets, masks, blocks):
    slots, tile, _ = masks.shape
    n, _, width = blocks.shape
    return pl.pallas_call(
        products_kernel,
        grid_spec=pltpu.PrefetchScalarGridSpec(
            num_scalar_prefetch=1,
            grid=(slots // STEP,),
            in_specs=[
                pl.BlockSpec((STEP, tile, tile), lambda i, o: (i, 0, 0)),
                pl.BlockSpec((n, tile, width), lambda i, o: (0, 0, 0)),
            ],
            out_specs=pl.BlockSpec((STEP, tile, width), lambda i, o: (i, 0, 0)),
        ),
        out_shape=jax.ShapeDtypeStruct((slots, tile, width), jnp.bfloat16),
        cost_estimate=pl.CostEstimate(
            flops=2 * slots * tile * tile * width,
            bytes_accessed=slots * tile * (tile + width) * 2,
            transcendentals=0,
        ),
        compiler_params=pltpu.CompilerParams(vmem_limit_bytes=60 << 20),
        name="tile_products",
    )(offsets, masks, blocks)


def gathered_kernel(offset_ref, part_ref, out_ref, total_ref):
    step = pl.program_id(0)

    @pl.when(step == 0)
    def _():
        total_ref[...] = jnp.zeros_like(total_ref)

    for t in range(STEP):
        total_ref[offset_ref[step * STEP + t]] += part_ref[t].astype(jnp.float32)

    @pl.when(step == pl.num_programs(0) - 1)
    def _():
        out_ref[...] = total_ref[...].astype(out_ref.dtype)


def summed_into(offsets, parts, blocks):
    slots, tile, width = parts.shape
    return pl.pallas_call(
        gathered_kernel,
        grid_spec=pltpu.PrefetchScalarGridSpec(
            num_scalar_prefetch=1,
            grid=(slots // STEP,),
            in_specs=[pl.BlockSpec((STEP, tile, width), lambda i, o: (i, 0, 0))],
            out_specs=pl.BlockSpec((blocks, tile, width), lambda i, o: (0, 0, 0)),
            scratch_shapes=[pltpu.VMEM((blocks, tile, width), jnp.float32)],
        ),
        out_shape=jax.ShapeDtypeStruct((blocks, tile, width), jnp.bfloat16),
        cost_estimate=pl.CostEstimate(
            flops=slots * tile * width, bytes_accessed=slots * tile * width * 2, transcendentals=0
        ),
        compiler_params=pltpu.CompilerParams(vmem_limit_bytes=40 << 20),
        name="summed_into",
    )(offsets, parts)


def pick_kernel(offset_ref, *refs):
    *piece_refs, out_ref, held_ref = refs
    step = pl.program_id(0)

    @pl.when(step == 0)
    def _():
        first = 0
        for piece in piece_refs:
            held_ref[first : first + len(piece)] = piece[...]
            first += len(piece)

    for t in range(STEP):
        out_ref[t] = held_ref[offset_ref[step * STEP + t]]


def picked(offsets, *pieces):
    slots = offsets.shape[0]
    n = sum(len(piece) for piece in pieces)
    _, tile, width = pieces[0].shape
    dtype = pieces[0].dtype
    return pl.pallas_call(
        pick_kernel,
        grid_spec=pltpu.PrefetchScalarGridSpec(
            num_scalar_prefetch=1,
            grid=(slots // STEP,),
            in_specs=[pl.BlockSpec(piece.shape, lambda i, o: (0, 0, 0)) for piece in pieces],
            out_specs=pl.BlockSpec((STEP, tile, width), lambda i, o: (i, 0, 0)),
            scratch_shapes=[pltpu.VMEM((n, tile, width), dtype)],
        ),
        out_shape=jax.ShapeDtypeStruct((slots, tile, width), dtype),
        cost_estimate=pl.CostEstimate(
            flops=0, bytes_accessed=(n + slots) * tile * width * 2, transcendentals=0
        ),
        compiler_params=pltpu.CompilerParams(vmem_limit_bytes=60 << 20),
        name="picked",
    )(offsets, *pieces)


def shifted(x, axis, by):
    n = lax.axis_size(axis)
    return lax.ppermute(x, axis, [(i, (i + by) % n) for i in range(n)])


DISTANCES = (-3, 0, 3, -4, -1, 2, -2, 1)


def place_of(device, here):
    far = (device - here + 4) % 8 - 4
    return sum(jnp.where(far == d, i, 0) for i, d in enumerate(DISTANCES))


def gather_of_eight(x, axis):
    near = jnp.stack([shifted(x, axis, 3), x, shifted(x, axis, -3)])
    return near, shifted(near, axis, 1), shifted(near[:2], axis, -1)


def sum_of_eight(x, axis):
    above = shifted(x[3:6], axis, -1).astype(jnp.float32)
    below = shifted(x[6:8], axis, 1).astype(jnp.float32)
    low = x[0].astype(jnp.float32) + above[0] + below[0]
    own = x[1].astype(jnp.float32) + above[1] + below[1]
    high = x[2].astype(jnp.float32) + above[2]
    return own, shifted(low.astype(x.dtype), axis, -3), shifted(high.astype(x.dtype), axis, 3)


def halved(x, axis, bit):
    half = x.shape[0] // 2
    low = (lax.axis_index(axis) & bit) == 0
    other = pair_swap(jnp.where(low, x[half:], x[:half]), axis, bit)
    return jnp.where(low, x[:half], x[half:]) + other


def doubled(x, axis, bit):
    low = (lax.axis_index(axis) & bit) == 0
    other = pair_swap(x, axis, bit)
    return jnp.where(low, jnp.concatenate([x, other]), jnp.concatenate([other, x]))


def shards(
    node_feats, node_ids, tile_row, tile_col, tile_count, self_weight, neigh_weight, out_grad
):
    dom_total = lax.axis_size(DOM)
    rep_total = lax.axis_size("rep")
    x_total, z_total, core_total = (lax.axis_size(a) for a in DOM)
    dom_here = lax.axis_index(DOM)
    rep_here = lax.axis_index("rep")
    x_here, z_here, core = (lax.axis_index(a) for a in DOM)
    rows_here, width_in = node_feats.shape
    blocks_here = rows_here // TILE
    group_blocks = blocks_here * rep_total
    id_blocks = node_ids.reshape(-1, TILE)
    group_first = dom_here * group_blocks
    half_in = width_in // 2

    column_1 = lax.all_to_all(
        jnp.broadcast_to(node_feats[None, :, :half_in], (z_total, rows_here, half_in)),
        "z",
        0,
        0,
        tiled=True,
    ).reshape(z_total * blocks_here, TILE, half_in)

    def passed_tiles(table):
        table = table.reshape(x_total, z_total, core_total, rep_total, dom_total)
        table = lax.dynamic_slice(
            table, (0, z_here, 0, rep_here, 0), (x_total, 1, core_total, 1, dom_total)
        ).reshape(x_total * core_total, x_total, z_total, core_total)
        table = lax.dynamic_slice_in_dim(table, x_here, 1, 1)
        return lax.dynamic_slice_in_dim(table, core, 1, 3).reshape(-1)

    passed_cols = passed_tiles(tile_col)
    place = jnp.tile(jnp.arange(z_total), x_total * core_total)
    passed_first = ((x_here * z_total + place) * core_total + core) * group_blocks
    passed_first = passed_first + rep_here * blocks_here
    passed_block = jnp.where(passed_cols >= 0, passed_cols - passed_first, 0)
    passed_offset = place * blocks_here + passed_block
    passed_near = place_of(place, z_here) * blocks_here + passed_block

    def held_tiles(table):
        row = lax.dynamic_slice(table, (dom_here, rep_here, 0), (1, 1, dom_total))
        return row.reshape(x_total, z_total, core_total).swapaxes(1, 2).reshape(-1)

    held_rows = held_tiles(tile_row)
    held_there = held_rows >= 0
    held_block = jnp.where(held_there, held_rows, 0)
    held_cols = jnp.where(held_there, held_tiles(tile_col), 0)
    held_limits = jnp.where(held_there, held_tiles(tile_count), 0)
    held_offset = jnp.where(held_there, held_block - group_first, 0)
    row_ids, col_ids = id_blocks[held_block], id_blocks[held_cols]
    masks = edge_masks(row_ids, col_ids, held_limits, False)
    masks_swapped = edge_masks(row_ids, col_ids, held_limits, True)

    held_owner = held_offset // blocks_here
    held_near = place_of(held_owner, rep_here) * blocks_here + held_offset % blocks_here

    column_1, masks, masks_swapped = lax.optimization_barrier((column_1, masks, masks_swapped))
    leaving_1 = picked(passed_offset, column_1)
    leaving_1, second = lax.optimization_barrier((leaving_1, node_feats[:, half_in:]))
    arrived_1 = lax.all_to_all(leaving_1, ("x", "core"), 0, 0, tiled=True)
    column_2 = [x.reshape(-1, TILE, half_in) for x in gather_of_eight(second, "z")]
    leaving_2 = picked(passed_near, *column_2)
    arrived_1, leaving_2 = lax.optimization_barrier((arrived_1, leaving_2))
    arrived_2 = lax.all_to_all(leaving_2, ("x", "core"), 0, 0, tiled=True)
    sums_1 = tile_sums(held_near, masks, arrived_1, group_blocks)
    own_1, low_1, high_1 = sum_of_eight(sums_1.reshape(rep_total, rows_here, half_in), "rep")
    arrived_2, low_1 = lax.optimization_barrier((arrived_2, low_1))
    sums_2 = tile_sums(held_offset, masks, arrived_2, group_blocks)
    sums_2, high_1 = lax.optimization_barrier((sums_2, high_1))
    pieces = lax.all_to_all(
        sums_2.reshape(rep_total, rows_here, half_in), "rep", 0, 0, tiled=True
    )
    summed_1 = own_1 + low_1.astype(jnp.float32) + high_1.astype(jnp.float32)
    summed = jnp.concatenate([summed_1, pieces.astype(jnp.float32).sum(axis=0)], axis=1)

    own_first = group_first + rep_here * blocks_here
    group_rows = lax.dynamic_slice_in_dim(tile_row, dom_here, 1, 0).reshape(-1)
    group_limits = lax.dynamic_slice_in_dim(tile_count, dom_here, 1, 0).reshape(-1)
    owned_rows = group_rows[:, None] == own_first + jnp.arange(blocks_here)[None, :]
    degree = jnp.sum(jnp.where(owned_rows, group_limits[:, None], 0), axis=0).astype(jnp.float32)
    divisor = jnp.repeat(jnp.maximum(degree, 1.0), TILE)[:, None]
    mean_feats = (summed / divisor).astype(jnp.bfloat16)
    preact = jnp.dot(node_feats, self_weight, preferred_element_type=jnp.float32) + jnp.dot(
        mean_feats, neigh_weight, preferred_element_type=jnp.float32
    )
    hidden_out = jax.nn.silu(preact).astype(jnp.bfloat16)
    logistic = jax.nn.sigmoid(preact)
    pre_grad = (out_grad.astype(jnp.float32) * logistic * (1.0 + preact * (1.0 - logistic))).astype(
        jnp.bfloat16
    )
    over_rows = (((0,), (0,)), ((), ()))
    over_cols = (((1,), (1,)), ((), ()))
    mean_grad = lax.dot_general(
        pre_grad, neigh_weight, over_cols, preferred_element_type=jnp.float32
    )
    spread = (mean_grad / divisor).astype(jnp.bfloat16)
    spread = jnp.broadcast_to(spread[None], (rep_total, rows_here, width_in))
    spread, mean_feats, summing = lax.optimization_barrier((spread, mean_feats, pre_grad))
    group_spread = lax.all_to_all(spread, "rep", 0, 0, tiled=True)
    group_spread = group_spread.reshape(group_blocks, TILE, width_in)

    self_term = lax.dot_general(node_feats, summing, over_rows, preferred_element_type=jnp.float32)
    neigh_term = lax.dot_general(
        mean_feats, summing, over_rows, preferred_element_type=jnp.float32
    )
    first = core == 0
    share = jnp.where(first, self_term, neigh_term) + lax.ppermute(
        jnp.where(first, neigh_term, self_term), "core", [(0, 1), (1, 0)]
    )
    for axis, bit in (("x", 1), ("x", 2), ("z", 1)):
        share = halved(share, axis, bit)
    share = share + pair_swap(share, "z", 2)

    returning = tile_products(held_offset, masks_swapped, group_spread)
    returning, group_spread, share = lax.optimization_barrier((returning, group_spread, share))
    returned = lax.all_to_all(returning, ("x", "core"), 0, 0, tiled=True)
    for axis, bit in (("z", 4), ("rep", 1), ("rep", 2), ("rep", 4)):
        share = share + pair_swap(share, axis, bit)
    share = share * (1.0 / math.sqrt(rows_here * dom_total * rep_total))
    share = doubled(share, "z", 1)
    column_sums = summed_into(passed_offset, returned, z_total * blocks_here)
    column_sums, share = lax.optimization_barrier((column_sums, share))
    parts = lax.all_to_all(
        column_sums.reshape(z_total, rows_here, width_in), "z", 0, 0, tiled=True
    )
    for bit in (2, 1):
        share = doubled(share, "x", bit)
    other = lax.ppermute(share, "core", [(0, 1), (1, 0)])
    self_grad = jnp.where(first, share, other)
    neigh_grad = jnp.where(first, other, share)

    self_back = lax.dot_general(
        pre_grad, self_weight, over_cols, preferred_element_type=jnp.float32
    )
    transposed = parts.astype(jnp.float32).sum(axis=0)
    feat_grad = (self_back + transposed).astype(jnp.bfloat16)
    return (hidden_out, feat_grad, self_grad, neigh_grad)


def solution(mesh):
    torus = Mesh(mesh.devices.reshape(4, 8, 2, mesh.shape["rep"]), ALL)
    in_specs = (P(ALL, None), P(), P(), P(), P(), P(), P(), P(ALL, None))
    out_specs = (P(ALL, None), P(ALL, None), P(), P())
    return jax.shard_map(
        shards, mesh=torus, in_specs=in_specs, out_specs=out_specs, check_vma=False
    )
```

```python
import math

import jax
import jax.numpy as jnp
from jax import lax
from jax.experimental import pallas as pl
from jax.experimental.pallas import tpu as pltpu
from jax.sharding import Mesh
from jax.sharding import PartitionSpec as P

TILE = 128
DOM = ("x", "z", "core")
ALL = ("x", "z", "core", "rep")
STEP = 32


def edge_masks(row_ids, col_ids, limits, swapped):
    u = row_ids % 4093
    v = col_ids % 4091
    if swapped:
        u, v = u[:, None, :], v[:, :, None]
    else:
        u, v = u[:, :, None], v[:, None, :]
    hashed = (u * v + u + 3 * v) % 4099 % TILE
    return (hashed < limits[:, None, None]).astype(jnp.bfloat16)


def pair_swap(x, axis, bit):
    n = lax.axis_size(axis)
    return lax.ppermute(x, axis, [(i, i ^ bit) for i in range(n)])


def forward_kernel(offset_ref, mask_ref, feat_ref, out_ref, total_ref):
    step = pl.program_id(0)

    @pl.when(step == 0)
    def _():
        total_ref[...] = jnp.zeros_like(total_ref)

    products = [
        jnp.dot(mask_ref[t], feat_ref[t], preferred_element_type=jnp.float32) for t in range(STEP)
    ]
    for t in range(STEP):
        total_ref[offset_ref[step * STEP + t]] += products[t]

    @pl.when(step == pl.num_programs(0) - 1)
    def _():
        out_ref[...] = total_ref[...].astype(out_ref.dtype)


def tile_sums(offsets, masks, feats, blocks, limit):
    slots, tile, width = feats.shape
    return pl.pallas_call(
        forward_kernel,
        grid_spec=pltpu.PrefetchScalarGridSpec(
            num_scalar_prefetch=1,
            grid=(slots // STEP,),
            in_specs=[
                pl.BlockSpec((STEP, tile, tile), lambda i, o: (i, 0, 0)),
                pl.BlockSpec((STEP, tile, width), lambda i, o: (i, 0, 0)),
            ],
            out_specs=pl.BlockSpec((blocks, tile, width), lambda i, o: (0, 0, 0)),
            scratch_shapes=[pltpu.VMEM((blocks, tile, width), jnp.float32)],
        ),
        out_shape=jax.ShapeDtypeStruct((blocks, tile, width), jnp.bfloat16),
        cost_estimate=pl.CostEstimate(
            flops=2 * slots * tile * tile * width,
            bytes_accessed=slots * tile * (tile + width) * 2,
            transcendentals=0,
        ),
        compiler_params=pltpu.CompilerParams(vmem_limit_bytes=limit << 20),
        name="tile_sums",
    )(offsets, masks, feats)


def products_kernel(offset_ref, mask_ref, block_ref, out_ref):
    step = pl.program_id(0)
    for t in range(STEP):
        out_ref[t] = jnp.dot(
            mask_ref[t],
            block_ref[offset_ref[step * STEP + t]],
            preferred_element_type=jnp.float32,
        ).astype(out_ref.dtype)


def tile_products(offsets, masks, blocks):
    slots, tile, _ = masks.shape
    n, _, width = blocks.shape
    return pl.pallas_call(
        products_kernel,
        grid_spec=pltpu.PrefetchScalarGridSpec(
            num_scalar_prefetch=1,
            grid=(slots // STEP,),
            in_specs=[
                pl.BlockSpec((STEP, tile, tile), lambda i, o: (i, 0, 0)),
                pl.BlockSpec((n, tile, width), lambda i, o: (0, 0, 0)),
            ],
            out_specs=pl.BlockSpec((STEP, tile, width), lambda i, o: (i, 0, 0)),
        ),
        out_shape=jax.ShapeDtypeStruct((slots, tile, width), jnp.bfloat16),
        cost_estimate=pl.CostEstimate(
            flops=2 * slots * tile * tile * width,
            bytes_accessed=slots * tile * (tile + width) * 2,
            transcendentals=0,
        ),
        compiler_params=pltpu.CompilerParams(vmem_limit_bytes=60 << 20),
        name="tile_products",
    )(offsets, masks, blocks)


def gathered_kernel(offset_ref, part_ref, out_ref, total_ref):
    step = pl.program_id(0)

    @pl.when(step == 0)
    def _():
        total_ref[...] = jnp.zeros_like(total_ref)

    for t in range(STEP):
        total_ref[offset_ref[step * STEP + t]] += part_ref[t].astype(jnp.float32)

    @pl.when(step == pl.num_programs(0) - 1)
    def _():
        out_ref[...] = total_ref[...].astype(out_ref.dtype)


def summed_into(offsets, parts, blocks):
    slots, tile, width = parts.shape
    return pl.pallas_call(
        gathered_kernel,
        grid_spec=pltpu.PrefetchScalarGridSpec(
            num_scalar_prefetch=1,
            grid=(slots // STEP,),
            in_specs=[pl.BlockSpec((STEP, tile, width), lambda i, o: (i, 0, 0))],
            out_specs=pl.BlockSpec((blocks, tile, width), lambda i, o: (0, 0, 0)),
            scratch_shapes=[pltpu.VMEM((blocks, tile, width), jnp.float32)],
        ),
        out_shape=jax.ShapeDtypeStruct((blocks, tile, width), jnp.bfloat16),
        cost_estimate=pl.CostEstimate(
            flops=slots * tile * width, bytes_accessed=slots * tile * width * 2, transcendentals=0
        ),
        compiler_params=pltpu.CompilerParams(vmem_limit_bytes=40 << 20),
        name="summed_into",
    )(offsets, parts)


def pick_kernel(offset_ref, *refs):
    *piece_refs, out_ref, held_ref = refs
    step = pl.program_id(0)

    @pl.when(step == 0)
    def _():
        first = 0
        for piece in piece_refs:
            held_ref[first : first + len(piece)] = piece[...]
            first += len(piece)

    for t in range(STEP):
        out_ref[t] = held_ref[offset_ref[step * STEP + t]]


def picked(offsets, *pieces):
    slots = offsets.shape[0]
    n = sum(len(piece) for piece in pieces)
    _, tile, width = pieces[0].shape
    dtype = pieces[0].dtype
    return pl.pallas_call(
        pick_kernel,
        grid_spec=pltpu.PrefetchScalarGridSpec(
            num_scalar_prefetch=1,
            grid=(slots // STEP,),
            in_specs=[pl.BlockSpec(piece.shape, lambda i, o: (0, 0, 0)) for piece in pieces],
            out_specs=pl.BlockSpec((STEP, tile, width), lambda i, o: (i, 0, 0)),
            scratch_shapes=[pltpu.VMEM((n, tile, width), dtype)],
        ),
        out_shape=jax.ShapeDtypeStruct((slots, tile, width), dtype),
        cost_estimate=pl.CostEstimate(
            flops=0, bytes_accessed=(n + slots) * tile * width * 2, transcendentals=0
        ),
        compiler_params=pltpu.CompilerParams(vmem_limit_bytes=60 << 20),
        name="picked",
    )(offsets, *pieces)


def shifted(x, axis, by):
    n = lax.axis_size(axis)
    return lax.ppermute(x, axis, [(i, (i + by) % n) for i in range(n)])


DISTANCES = (-3, 0, 3, -4, -1, 2, -2, 1)


def place_of(device, here):
    far = (device - here + 4) % 8 - 4
    return sum(jnp.where(far == d, i, 0) for i, d in enumerate(DISTANCES))


def gather_of_eight(x, axis):
    near = jnp.stack([shifted(x, axis, 3), x, shifted(x, axis, -3)])
    return near, shifted(near, axis, 1), shifted(near[:2], axis, -1)


def sum_of_eight(x, axis):
    above, below = shifted(x[3:6], axis, -1), shifted(x[6:8], axis, 1)

    def added(*parts):
        return sum(part.astype(jnp.float32) for part in parts)

    low = added(x[0], above[0], below[0])
    own = added(x[1], above[1], below[1])
    high = added(x[2], above[2])
    return own, shifted(low.astype(x.dtype), axis, -3), shifted(high.astype(x.dtype), axis, 3)


def halved(x, axis, bit):
    half = x.shape[0] // 2
    low = (lax.axis_index(axis) & bit) == 0
    other = pair_swap(jnp.where(low, x[half:], x[:half]), axis, bit)
    return jnp.where(low, x[:half], x[half:]) + other


def doubled(x, axis, bit):
    low = (lax.axis_index(axis) & bit) == 0
    other = pair_swap(x, axis, bit)
    return jnp.where(low, jnp.concatenate([x, other]), jnp.concatenate([other, x]))


def shards(
    node_feats, node_ids, tile_row, tile_col, tile_count, self_weight, neigh_weight, out_grad
):
    dom_total = lax.axis_size(DOM)
    rep_total = lax.axis_size("rep")
    x_total, z_total, core_total = (lax.axis_size(a) for a in DOM)
    dom_here = lax.axis_index(DOM)
    rep_here = lax.axis_index("rep")
    x_here, z_here, core = (lax.axis_index(a) for a in DOM)
    rows_here, width_in = node_feats.shape
    blocks_here = rows_here // TILE
    group_blocks = blocks_here * rep_total
    id_blocks = node_ids.reshape(-1, TILE)
    group_first = dom_here * group_blocks
    half_in = width_in // 2

    column_1 = lax.all_to_all(
        jnp.broadcast_to(node_feats[None, :, :half_in], (z_total, rows_here, half_in)),
        "z",
        0,
        0,
        tiled=True,
    ).reshape(z_total * blocks_here, TILE, half_in)

    def passed_tiles(table):
        table = table.reshape(x_total, z_total, core_total, rep_total, dom_total)
        table = lax.dynamic_slice(
            table, (0, z_here, 0, rep_here, 0), (x_total, 1, core_total, 1, dom_total)
        ).reshape(x_total * core_total, x_total, z_total, core_total)
        table = lax.dynamic_slice_in_dim(table, x_here, 1, 1)
        return lax.dynamic_slice_in_dim(table, core, 1, 3).reshape(-1)

    passed_cols = passed_tiles(tile_col)
    place = jnp.tile(jnp.arange(z_total), x_total * core_total)
    passed_first = ((x_here * z_total + place) * core_total + core) * group_blocks
    passed_first = passed_first + rep_here * blocks_here
    passed_block = jnp.where(passed_cols >= 0, passed_cols - passed_first, 0)
    passed_offset = place * blocks_here + passed_block
    passed_near = place_of(place, z_here) * blocks_here + passed_block

    def held_tiles(table):
        row = lax.dynamic_slice(table, (dom_here, rep_here, 0), (1, 1, dom_total))
        return row.reshape(x_total, z_total, core_total).swapaxes(1, 2).reshape(-1)

    held_rows = held_tiles(tile_row)
    held_there = held_rows >= 0
    held_block = jnp.where(held_there, held_rows, 0)
    held_cols = jnp.where(held_there, held_tiles(tile_col), 0)
    held_limits = jnp.where(held_there, held_tiles(tile_count), 0)
    held_offset = jnp.where(held_there, held_block - group_first, 0)
    row_ids, col_ids = id_blocks[held_block], id_blocks[held_cols]
    masks = edge_masks(row_ids, col_ids, held_limits, False)
    masks_swapped = edge_masks(row_ids, col_ids, held_limits, True)

    held_owner = held_offset // blocks_here
    held_near = place_of(held_owner, rep_here) * blocks_here + held_offset % blocks_here

    column_1, masks, masks_swapped = lax.optimization_barrier((column_1, masks, masks_swapped))
    leaving_1 = picked(passed_offset, column_1)
    leaving_1, second = lax.optimization_barrier((leaving_1, node_feats[:, half_in:]))
    arrived_1 = lax.all_to_all(leaving_1, ("x", "core"), 0, 0, tiled=True)
    column_2 = [x.reshape(-1, TILE, half_in) for x in gather_of_eight(second, "z")]
    leaving_2 = picked(passed_near, *column_2)
    arrived_1, leaving_2 = lax.optimization_barrier((arrived_1, leaving_2))
    arrived_2 = lax.all_to_all(leaving_2, ("x", "core"), 0, 0, tiled=True)
    sums_1 = tile_sums(held_near, masks, arrived_1, group_blocks, 40)
    own_1, low_1, high_1 = sum_of_eight(sums_1.reshape(rep_total, rows_here, half_in), "rep")
    arrived_2, low_1 = lax.optimization_barrier((arrived_2, low_1))
    sums_2 = tile_sums(held_offset, masks, arrived_2, group_blocks, 60)
    sums_2, high_1 = lax.optimization_barrier((sums_2, high_1))
    pieces = lax.all_to_all(
        sums_2.reshape(rep_total, rows_here, half_in), "rep", 0, 0, tiled=True
    )
    summed_1 = own_1 + low_1.astype(jnp.float32) + high_1.astype(jnp.float32)
    summed = jnp.concatenate([summed_1, pieces.astype(jnp.float32).sum(axis=0)], axis=1)

    own_first = group_first + rep_here * blocks_here
    group_rows = lax.dynamic_slice_in_dim(tile_row, dom_here, 1, 0).reshape(-1)
    group_limits = lax.dynamic_slice_in_dim(tile_count, dom_here, 1, 0).reshape(-1)
    owned_rows = group_rows[:, None] == own_first + jnp.arange(blocks_here)[None, :]
    degree = jnp.sum(jnp.where(owned_rows, group_limits[:, None], 0), axis=0).astype(jnp.float32)
    divisor = jnp.repeat(jnp.maximum(degree, 1.0), TILE)[:, None]
    mean_feats = (summed / divisor).astype(jnp.bfloat16)
    preact = jnp.dot(node_feats, self_weight, preferred_element_type=jnp.float32) + jnp.dot(
        mean_feats, neigh_weight, preferred_element_type=jnp.float32
    )
    hidden_out = jax.nn.silu(preact).astype(jnp.bfloat16)
    logistic = jax.nn.sigmoid(preact)
    pre_grad = (out_grad.astype(jnp.float32) * logistic * (1.0 + preact * (1.0 - logistic))).astype(
        jnp.bfloat16
    )
    over_rows = (((0,), (0,)), ((), ()))
    over_cols = (((1,), (1,)), ((), ()))
    mean_grad = lax.dot_general(
        pre_grad, neigh_weight, over_cols, preferred_element_type=jnp.float32
    )
    spread = (mean_grad / divisor).astype(jnp.bfloat16)
    spread = jnp.broadcast_to(spread[None], (rep_total, rows_here, width_in))
    spread, mean_feats, summing = lax.optimization_barrier((spread, mean_feats, pre_grad))
    group_spread = lax.all_to_all(spread, "rep", 0, 0, tiled=True)
    group_spread = group_spread.reshape(group_blocks, TILE, width_in)

    self_term = lax.dot_general(node_feats, summing, over_rows, preferred_element_type=jnp.float32)
    neigh_term = lax.dot_general(
        mean_feats, summing, over_rows, preferred_element_type=jnp.float32
    )
    first = core == 0
    share = jnp.where(first, self_term, neigh_term) + lax.ppermute(
        jnp.where(first, neigh_term, self_term), "core", [(0, 1), (1, 0)]
    )
    for axis, bit in (("x", 1), ("x", 2), ("z", 1)):
        share = halved(share, axis, bit)
    share = share + pair_swap(share, "z", 2)

    returning = tile_products(held_offset, masks_swapped, group_spread)
    returning, group_spread, share = lax.optimization_barrier((returning, group_spread, share))
    returned = lax.all_to_all(returning, ("x", "core"), 0, 0, tiled=True)
    for axis, bit in (("z", 4), ("rep", 1), ("rep", 2), ("rep", 4)):
        share = share + pair_swap(share, axis, bit)
    share = share * (1.0 / math.sqrt(rows_here * dom_total * rep_total))
    share = doubled(share, "z", 1)
    column_sums = summed_into(passed_offset, returned, z_total * blocks_here)
    column_sums, share = lax.optimization_barrier((column_sums, share))
    parts = lax.all_to_all(
        column_sums.reshape(z_total, rows_here, width_in), "z", 0, 0, tiled=True
    )
    for bit in (2, 1):
        share = doubled(share, "x", bit)
    other = lax.ppermute(share, "core", [(0, 1), (1, 0)])
    self_grad = jnp.where(first, share, other)
    neigh_grad = jnp.where(first, other, share)

    self_back = lax.dot_general(
        pre_grad, self_weight, over_cols, preferred_element_type=jnp.float32
    )
    transposed = parts.astype(jnp.float32).sum(axis=0)
    feat_grad = (self_back + transposed).astype(jnp.bfloat16)
    return (hidden_out, feat_grad, self_grad, neigh_grad)


def solution(mesh):
    torus = Mesh(mesh.devices.reshape(4, 8, 2, mesh.shape["rep"]), ALL)
    in_specs = (P(ALL, None), P(), P(), P(), P(), P(), P(), P(ALL, None))
    out_specs = (P(ALL, None), P(ALL, None), P(), P())
    return jax.shard_map(
        shards, mesh=torus, in_specs=in_specs, out_specs=out_specs, check_vma=False
    )
```

```python
import math

import jax
import jax.numpy as jnp
from jax import lax
from jax.experimental import pallas as pl
from jax.experimental.pallas import tpu as pltpu
from jax.sharding import Mesh
from jax.sharding import PartitionSpec as P

TILE = 128
DOM = ("x", "z", "core")
ALL = ("x", "z", "core", "rep")
STEP = 32


def edge_masks(row_ids, col_ids, limits, swapped):
    u = row_ids % 4093
    v = col_ids % 4091
    if swapped:
        u, v = u[:, None, :], v[:, :, None]
    else:
        u, v = u[:, :, None], v[:, None, :]
    hashed = (u * v + u + 3 * v) % 4099 % TILE
    return (hashed < limits[:, None, None]).astype(jnp.bfloat16)


def pair_swap(x, axis, bit):
    n = lax.axis_size(axis)
    return lax.ppermute(x, axis, [(i, i ^ bit) for i in range(n)])


def forward_kernel(offset_ref, mask_ref, feat_ref, out_ref, total_ref):
    step = pl.program_id(0)

    @pl.when(step == 0)
    def _():
        total_ref[...] = jnp.zeros_like(total_ref)

    products = [
        jnp.dot(mask_ref[t], feat_ref[t], preferred_element_type=jnp.float32) for t in range(STEP)
    ]
    for t in range(STEP):
        total_ref[offset_ref[step * STEP + t]] += products[t]

    @pl.when(step == pl.num_programs(0) - 1)
    def _():
        out_ref[...] = total_ref[...].astype(out_ref.dtype)


def tile_sums(offsets, masks, feats, blocks, limit):
    slots, tile, width = feats.shape
    return pl.pallas_call(
        forward_kernel,
        grid_spec=pltpu.PrefetchScalarGridSpec(
            num_scalar_prefetch=1,
            grid=(slots // STEP,),
            in_specs=[
                pl.BlockSpec((STEP, tile, tile), lambda i, o: (i, 0, 0)),
                pl.BlockSpec((STEP, tile, width), lambda i, o: (i, 0, 0)),
            ],
            out_specs=pl.BlockSpec((blocks, tile, width), lambda i, o: (0, 0, 0)),
            scratch_shapes=[pltpu.VMEM((blocks, tile, width), jnp.float32)],
        ),
        out_shape=jax.ShapeDtypeStruct((blocks, tile, width), jnp.bfloat16),
        cost_estimate=pl.CostEstimate(
            flops=2 * slots * tile * tile * width,
            bytes_accessed=slots * tile * (tile + width) * 2,
            transcendentals=0,
        ),
        compiler_params=pltpu.CompilerParams(vmem_limit_bytes=limit << 20),
        name="tile_sums",
    )(offsets, masks, feats)


def products_kernel(offset_ref, mask_ref, block_ref, out_ref):
    step = pl.program_id(0)
    for t in range(STEP):
        out_ref[t] = jnp.dot(
            mask_ref[t],
            block_ref[offset_ref[step * STEP + t]],
            preferred_element_type=jnp.float32,
        ).astype(out_ref.dtype)


def tile_products(offsets, masks, blocks):
    slots, tile, _ = masks.shape
    n, _, width = blocks.shape
    return pl.pallas_call(
        products_kernel,
        grid_spec=pltpu.PrefetchScalarGridSpec(
            num_scalar_prefetch=1,
            grid=(slots // STEP,),
            in_specs=[
                pl.BlockSpec((STEP, tile, tile), lambda i, o: (i, 0, 0)),
                pl.BlockSpec((n, tile, width), lambda i, o: (0, 0, 0)),
            ],
            out_specs=pl.BlockSpec((STEP, tile, width), lambda i, o: (i, 0, 0)),
        ),
        out_shape=jax.ShapeDtypeStruct((slots, tile, width), jnp.bfloat16),
        cost_estimate=pl.CostEstimate(
            flops=2 * slots * tile * tile * width,
            bytes_accessed=slots * tile * (tile + width) * 2,
            transcendentals=0,
        ),
        compiler_params=pltpu.CompilerParams(vmem_limit_bytes=60 << 20),
        name="tile_products",
    )(offsets, masks, blocks)


def gathered_kernel(offset_ref, part_ref, out_ref, total_ref):
    step = pl.program_id(0)

    @pl.when(step == 0)
    def _():
        total_ref[...] = jnp.zeros_like(total_ref)

    for t in range(STEP):
        total_ref[offset_ref[step * STEP + t]] += part_ref[t].astype(jnp.float32)

    @pl.when(step == pl.num_programs(0) - 1)
    def _():
        out_ref[...] = total_ref[...].astype(out_ref.dtype)


def summed_into(offsets, parts, blocks):
    slots, tile, width = parts.shape
    return pl.pallas_call(
        gathered_kernel,
        grid_spec=pltpu.PrefetchScalarGridSpec(
            num_scalar_prefetch=1,
            grid=(slots // STEP,),
            in_specs=[pl.BlockSpec((STEP, tile, width), lambda i, o: (i, 0, 0))],
            out_specs=pl.BlockSpec((blocks, tile, width), lambda i, o: (0, 0, 0)),
            scratch_shapes=[pltpu.VMEM((blocks, tile, width), jnp.float32)],
        ),
        out_shape=jax.ShapeDtypeStruct((blocks, tile, width), jnp.bfloat16),
        cost_estimate=pl.CostEstimate(
            flops=slots * tile * width, bytes_accessed=slots * tile * width * 2, transcendentals=0
        ),
        compiler_params=pltpu.CompilerParams(vmem_limit_bytes=40 << 20),
        name="summed_into",
    )(offsets, parts)


def pick_kernel(offset_ref, *refs):
    *piece_refs, out_ref, held_ref = refs
    step = pl.program_id(0)

    @pl.when(step == 0)
    def _():
        first = 0
        for piece in piece_refs:
            held_ref[first : first + len(piece)] = piece[...]
            first += len(piece)

    for t in range(STEP):
        out_ref[t] = held_ref[offset_ref[step * STEP + t]]


def picked(offsets, *pieces):
    slots = offsets.shape[0]
    n = sum(len(piece) for piece in pieces)
    _, tile, width = pieces[0].shape
    dtype = pieces[0].dtype
    return pl.pallas_call(
        pick_kernel,
        grid_spec=pltpu.PrefetchScalarGridSpec(
            num_scalar_prefetch=1,
            grid=(slots // STEP,),
            in_specs=[pl.BlockSpec(piece.shape, lambda i, o: (0, 0, 0)) for piece in pieces],
            out_specs=pl.BlockSpec((STEP, tile, width), lambda i, o: (i, 0, 0)),
            scratch_shapes=[pltpu.VMEM((n, tile, width), dtype)],
        ),
        out_shape=jax.ShapeDtypeStruct((slots, tile, width), dtype),
        cost_estimate=pl.CostEstimate(
            flops=0, bytes_accessed=(n + slots) * tile * width * 2, transcendentals=0
        ),
        compiler_params=pltpu.CompilerParams(vmem_limit_bytes=60 << 20),
        name="picked",
    )(offsets, *pieces)


def shifted(x, axis, by):
    n = lax.axis_size(axis)
    return lax.ppermute(x, axis, [(i, (i + by) % n) for i in range(n)])


DISTANCES = (-3, 0, 3, -4, -1, 2, -2, 1)


def place_of(device, here):
    far = (device - here + 4) % 8 - 4
    return sum(jnp.where(far == d, i, 0) for i, d in enumerate(DISTANCES))


def gather_of_eight(x, axis):
    near = jnp.stack([shifted(x, axis, 3), x, shifted(x, axis, -3)])
    return near, shifted(near, axis, 1), shifted(near[:2], axis, -1)


def sum_of_eight(x, axis):
    above, below = shifted(x[3:6], axis, -1), shifted(x[6:8], axis, 1)

    def added(*parts):
        return sum(part.astype(jnp.float32) for part in parts)

    low = added(x[0], above[0], below[0])
    own = added(x[1], above[1], below[1])
    high = added(x[2], above[2])
    return own, shifted(low.astype(x.dtype), axis, -3), shifted(high.astype(x.dtype), axis, 3)


def halved(x, axis, bit):
    half = x.shape[0] // 2
    low = (lax.axis_index(axis) & bit) == 0
    other = pair_swap(jnp.where(low, x[half:], x[:half]), axis, bit)
    return jnp.where(low, x[:half], x[half:]) + other


def doubled(x, axis, bit):
    low = (lax.axis_index(axis) & bit) == 0
    other = pair_swap(x, axis, bit)
    return jnp.where(low, jnp.concatenate([x, other]), jnp.concatenate([other, x]))


def shards(
    node_feats, node_ids, tile_row, tile_col, tile_count, self_weight, neigh_weight, out_grad
):
    dom_total = lax.axis_size(DOM)
    rep_total = lax.axis_size("rep")
    x_total, z_total, core_total = (lax.axis_size(a) for a in DOM)
    dom_here = lax.axis_index(DOM)
    rep_here = lax.axis_index("rep")
    x_here, z_here, core = (lax.axis_index(a) for a in DOM)
    rows_here, width_in = node_feats.shape
    blocks_here = rows_here // TILE
    group_blocks = blocks_here * rep_total
    id_blocks = node_ids.reshape(-1, TILE)
    group_first = dom_here * group_blocks
    half_in = width_in // 2

    column_1 = lax.all_to_all(
        jnp.broadcast_to(node_feats[None, :, :half_in], (z_total, rows_here, half_in)),
        "z",
        0,
        0,
        tiled=True,
    ).reshape(z_total * blocks_here, TILE, half_in)

    def passed_tiles(table):
        table = table.reshape(x_total, z_total, core_total, rep_total, dom_total)
        table = lax.dynamic_slice(
            table, (0, z_here, 0, rep_here, 0), (x_total, 1, core_total, 1, dom_total)
        ).reshape(x_total * core_total, x_total, z_total, core_total)
        table = lax.dynamic_slice_in_dim(table, x_here, 1, 1)
        return lax.dynamic_slice_in_dim(table, core, 1, 3).reshape(-1)

    passed_cols = passed_tiles(tile_col)
    place = jnp.tile(jnp.arange(z_total), x_total * core_total)
    passed_first = ((x_here * z_total + place) * core_total + core) * group_blocks
    passed_first = passed_first + rep_here * blocks_here
    passed_block = jnp.where(passed_cols >= 0, passed_cols - passed_first, 0)
    passed_offset = place * blocks_here + passed_block
    passed_near = place_of(place, z_here) * blocks_here + passed_block

    def held_tiles(table):
        row = lax.dynamic_slice(table, (dom_here, rep_here, 0), (1, 1, dom_total))
        return row.reshape(x_total, z_total, core_total).swapaxes(1, 2).reshape(-1)

    held_rows = held_tiles(tile_row)
    held_there = held_rows >= 0
    held_block = jnp.where(held_there, held_rows, 0)
    held_cols = jnp.where(held_there, held_tiles(tile_col), 0)
    held_limits = jnp.where(held_there, held_tiles(tile_count), 0)
    held_offset = jnp.where(held_there, held_block - group_first, 0)
    row_ids, col_ids = id_blocks[held_block], id_blocks[held_cols]
    masks = edge_masks(row_ids, col_ids, held_limits, False)
    masks_swapped = edge_masks(row_ids, col_ids, held_limits, True)

    held_owner = held_offset // blocks_here
    held_near = place_of(held_owner, rep_here) * blocks_here + held_offset % blocks_here

    column_1, masks, masks_swapped = lax.optimization_barrier((column_1, masks, masks_swapped))
    leaving_1 = picked(passed_offset, column_1)
    leaving_1, second = lax.optimization_barrier((leaving_1, node_feats))
    second = second[:, half_in:]
    arrived_1 = lax.all_to_all(leaving_1, ("x", "core"), 0, 0, tiled=True)
    column_2 = [x.reshape(-1, TILE, half_in) for x in gather_of_eight(second, "z")]
    leaving_2 = picked(passed_near, *column_2)
    arrived_1, leaving_2 = lax.optimization_barrier((arrived_1, leaving_2))
    arrived_2 = lax.all_to_all(leaving_2, ("x", "core"), 0, 0, tiled=True)
    sums_1 = tile_sums(held_near, masks, arrived_1, group_blocks, 40)
    own_1, low_1, high_1 = sum_of_eight(sums_1.reshape(rep_total, rows_here, half_in), "rep")
    arrived_2, low_1 = lax.optimization_barrier((arrived_2, low_1))
    sums_2 = tile_sums(held_offset, masks, arrived_2, group_blocks, 60)
    sums_2, high_1 = lax.optimization_barrier((sums_2, high_1))
    pieces = lax.all_to_all(
        sums_2.reshape(rep_total, rows_here, half_in), "rep", 0, 0, tiled=True
    )
    summed_1 = own_1 + low_1.astype(jnp.float32) + high_1.astype(jnp.float32)
    summed = jnp.concatenate([summed_1, pieces.astype(jnp.float32).sum(axis=0)], axis=1)

    own_first = group_first + rep_here * blocks_here
    group_rows = lax.dynamic_slice_in_dim(tile_row, dom_here, 1, 0).reshape(-1)
    group_limits = lax.dynamic_slice_in_dim(tile_count, dom_here, 1, 0).reshape(-1)
    owned_rows = group_rows[:, None] == own_first + jnp.arange(blocks_here)[None, :]
    degree = jnp.sum(jnp.where(owned_rows, group_limits[:, None], 0), axis=0).astype(jnp.float32)
    divisor = jnp.repeat(jnp.maximum(degree, 1.0), TILE)[:, None]
    mean_feats = (summed / divisor).astype(jnp.bfloat16)
    preact = jnp.dot(node_feats, self_weight, preferred_element_type=jnp.float32) + jnp.dot(
        mean_feats, neigh_weight, preferred_element_type=jnp.float32
    )
    hidden_out = jax.nn.silu(preact).astype(jnp.bfloat16)
    logistic = jax.nn.sigmoid(preact)
    pre_grad = (out_grad.astype(jnp.float32) * logistic * (1.0 + preact * (1.0 - logistic))).astype(
        jnp.bfloat16
    )
    over_rows = (((0,), (0,)), ((), ()))
    over_cols = (((1,), (1,)), ((), ()))
    mean_grad = lax.dot_general(
        pre_grad, neigh_weight, over_cols, preferred_element_type=jnp.float32
    )
    spread = (mean_grad / divisor).astype(jnp.bfloat16)
    spread = jnp.broadcast_to(spread[None], (rep_total, rows_here, width_in))
    spread, mean_feats, summing = lax.optimization_barrier((spread, mean_feats, pre_grad))
    group_spread = lax.all_to_all(spread, "rep", 0, 0, tiled=True)
    group_spread = group_spread.reshape(group_blocks, TILE, width_in)

    self_term = lax.dot_general(node_feats, summing, over_rows, preferred_element_type=jnp.float32)
    neigh_term = lax.dot_general(
        mean_feats, summing, over_rows, preferred_element_type=jnp.float32
    )
    first = core == 0
    share = jnp.where(first, self_term, neigh_term) + lax.ppermute(
        jnp.where(first, neigh_term, self_term), "core", [(0, 1), (1, 0)]
    )
    for axis, bit in (("x", 1), ("x", 2), ("z", 1)):
        share = halved(share, axis, bit)
    share = share + pair_swap(share, "z", 2)

    returning = tile_products(held_offset, masks_swapped, group_spread)
    returning, group_spread, share = lax.optimization_barrier((returning, group_spread, share))
    returned = lax.all_to_all(returning, ("x", "core"), 0, 0, tiled=True)
    for axis, bit in (("z", 4), ("rep", 1), ("rep", 2), ("rep", 4)):
        share = share + pair_swap(share, axis, bit)
    share = share * (1.0 / math.sqrt(rows_here * dom_total * rep_total))
    share = doubled(share, "z", 1)
    column_sums = summed_into(passed_offset, returned, z_total * blocks_here)
    column_sums, share = lax.optimization_barrier((column_sums, share))
    parts = lax.all_to_all(
        column_sums.reshape(z_total, rows_here, width_in), "z", 0, 0, tiled=True
    )
    for bit in (2, 1):
        share = doubled(share, "x", bit)
    other = lax.ppermute(share, "core", [(0, 1), (1, 0)])
    self_grad = jnp.where(first, share, other)
    neigh_grad = jnp.where(first, other, share)

    self_back = lax.dot_general(
        pre_grad, self_weight, over_cols, preferred_element_type=jnp.float32
    )
    transposed = parts.astype(jnp.float32).sum(axis=0)
    feat_grad = (self_back + transposed).astype(jnp.bfloat16)
    return (hidden_out, feat_grad, self_grad, neigh_grad)


def solution(mesh):
    torus = Mesh(mesh.devices.reshape(4, 8, 2, mesh.shape["rep"]), ALL)
    in_specs = (P(ALL, None), P(), P(), P(), P(), P(), P(), P(ALL, None))
    out_specs = (P(ALL, None), P(ALL, None), P(), P())
    return jax.shard_map(
        shards, mesh=torus, in_specs=in_specs, out_specs=out_specs, check_vma=False
    )
```
